512 devices in a mesh: mem: 16 (over y, x), lon: 16 (over z_lo, core), lat: 2 (over z_hi).
Axes of the slice: x: 4, y: 4, z: 16 (z_hi: 2, z_lo: 8; z = z_hi * 8 + z_lo), core: 2. Of those that a mesh axis runs over, the one named last changes fastest.
Arguments:
- prior_sample_set: float32 [128, 8, 8, 2048], P('mem', None, 'lat', 'lon'), may hold values from -18 to 18
- eastward_cfl_number: float32 [8, 8, 2048], P(None, 'lat', 'lon'), may hold values from -0.35 to 0.35
- northward_cfl_number: float32 [8, 8, 2048], P(None, 'lat', 'lon'), may hold values from -0.35 to 0.35
- spreading_number: float32 [8, 8, 2048], P(None, 'lat', 'lon')
- obs_value: float32 [2, 16, 256], P('lat', 'lon'), may hold values from -6 to 6
- obs_site: int32 [2, 16, 256], P('lat', 'lon'), may hold values from 0 to 4095
- neighbours: int32 [8, 2048, 128], P('lat', 'lon'), may hold values from 0 to 2303, as said below
- loc_weight: float32 [8, 2048, 128], P('lat', 'lon'), may hold values from 0.15 to 1
Outputs:
- analysis: float32 [128, 8, 8, 2048], P('mem', None, 'lat', 'lon')
The draws below stay inside these ranges and needn't reach their ends.
Inputs may be any that keep to these rules, and one draw needn't show every extreme that they name: obs_site[a, b, o] = l * 4 * 128 + i * 128 + j names level l, row i and column j inside block (a, b). `neighbours`: each entry is ((p + 1) * 3 + (t + 1)) * 256 + o with p and t in -1, 0, 1 and o below 256; the block a + p always lies within the grid's latitude blocks.
All inputs are finite; a program needn't handle non-finite values.
Results may differ from the reference program's by a relative error of at most 0.0003.
Values sent between devices are 32-bit elements; how exact they have to be, the bound alone decides.
No kernel may reach another device: no remote copies, remote signals or barrier semaphores. Data moves between devices by JAX's collectives and lax.ppermute only.
A program may use at most 64 MiB of HBM per device.

```python
import math
import jax
import jax.numpy as jnp
from jax import lax

SAMPLE_TOTAL = 128
ALTITUDE_TIERS = 8
NORTH_SOUTH_SPAN = 4
EAST_WEST_SPAN = 128
NOB = 256
NNB = 128
STEPS = 4
NS_ITERS = 4
NLAT = 8
NLON = 2048
N_LON = 16
N_LAT = 2


def strip_layout():
    column = jnp.arange(NLON, dtype=jnp.int32)
    place = column % EAST_WEST_SPAN
    block = column // EAST_WEST_SPAN
    blocks_total = NLON // EAST_WEST_SPAN
    boundary = jnp.where(place < STEPS, block, (block + 1) % blocks_total)
    in_strip = (place < STEPS) | (place >= EAST_WEST_SPAN - STEPS)
    return (boundary.astype(jnp.int32), in_strip)


def draw_eastward_cfl_number(key, part):
    key = jax.random.fold_in(key, 21)
    keys = jax.random.split(key, 2)
    blocks_total = NLON // EAST_WEST_SPAN
    boundary, in_strip = strip_layout()
    signs = jax.random.randint(keys[0], (ALTITUDE_TIERS, NLAT, blocks_total), 0, 2, dtype=jnp.int32) * 2 - 1
    signs = signs.at[0, 0, 0].set(1)
    signs = signs.at[0, 0, 1].set(-1)
    strip_value = 0.35 * signs[:, :, boundary].astype(jnp.float32)
    interior = jax.random.uniform(keys[1], (ALTITUDE_TIERS, NLAT, NLON), jnp.float32, -0.35, 0.35)
    return jnp.where(in_strip[None, None, :], strip_value, interior).astype(jnp.float32)


def draw_spreading_number(key, part):
    key = jax.random.fold_in(key, 23)
    keys = jax.random.split(key, 2)
    boundary, in_strip = strip_layout()
    low = jnp.log(jnp.float32(0.01))
    high = jnp.log(jnp.float32(0.07))
    interior = jnp.exp(jax.random.uniform(keys[0], (ALTITUDE_TIERS, NLAT, NLON), jnp.float32, low, high))
    interior = jnp.clip(interior, 0.01, 0.07)
    strip_value = jax.random.uniform(keys[1], (ALTITUDE_TIERS, NLAT, NLON), jnp.float32, 0.056, 0.07)
    values = jnp.where(in_strip[None, None, :], strip_value, interior)
    values = values.at[0, 0, 0].set(0.07)
    return values.astype(jnp.float32)


def draw_neighbours(key, part):
    key = jax.random.fold_in(key, 11)
    keys = jax.random.split(key, 3)
    shape = (NLAT, NLON, NNB)
    rows = jnp.arange(NLAT, dtype=jnp.int32)[:, None, None]
    block_row = rows // NORTH_SOUTH_SPAN
    block_total = NLAT // NORTH_SOUTH_SPAN
    lat_step = jax.random.randint(keys[0], shape, -1, 2, dtype=jnp.int32)
    outside = (block_row + lat_step < 0) | (block_row + lat_step >= block_total)
    lat_step = jnp.where(outside, 0, lat_step)
    lon_step = jax.random.randint(keys[1], shape, -1, 2, dtype=jnp.int32)
    position = jax.random.randint(keys[2], shape, 0, NOB, dtype=jnp.int32)
    index = ((lat_step + 1) * 3 + lon_step + 1) * NOB + position
    index = index.at[0, 0, NNB - 1].set(9 * NOB - 1)
    index = index.at[NLAT - 1, 0, 0].set(0)
    return index.astype(jnp.int32)


def place_ends(values, stream_key, low, top_value):
    longest = values.shape.index(max(values.shape))
    spots = []
    for shift in (0, 1):
        where = [jax.random.randint(jax.random.fold_in(stream_key, axis), (), 0, length) for axis, length in enumerate(values.shape)]
        where[longest] = (where[longest] + shift) % values.shape[longest]
        spots.append(tuple(where))
    return values.at[spots[0]].set(low).at[spots[1]].set(top_value)


def shard_levels(stream_key, extent, cuts, low, top_value):
    factor_of = 1.0
    for dim, parts in cuts:
        heights = jax.random.uniform(jax.random.fold_in(jax.random.fold_in(stream_key, 6), dim), (parts,), jnp.float32, low / len(cuts), top_value / len(cuts))
        factor_of = factor_of * jnp.repeat(jnp.exp(heights), extent[dim] // parts).reshape((-1,) + (1,) * (len(extent) - 1 - dim))
    return factor_of


def normal_values(key, extent, scale, most, cuts=(), held_as=jnp.bfloat16):
    array = jax.random.normal(key, extent, jnp.float32) * scale
    if len(cuts) > 0:
        array = shard_levels(key, extent, cuts, -0.22, 0.18) * array
    return jnp.clip(array, min=-most, max=most).astype(held_as)


def setup_inputs(seed: int = 0) -> dict:
    streams_of = jax.random.split(jax.random.key(seed), 9)
    return {
        "prior_sample_set": normal_values(streams_of[0], (SAMPLE_TOTAL, ALTITUDE_TIERS, NLAT, NLON), 3.0, 18.0, ((0, 16), (2, 2), (3, 16)), jnp.float32),
        "eastward_cfl_number": draw_eastward_cfl_number(jax.random.fold_in(streams_of[8], 71), 0),
        "northward_cfl_number": jnp.clip(jax.random.uniform(streams_of[2], (ALTITUDE_TIERS, NLAT, NLON), jnp.float32, -0.35, 0.35) * shard_levels(streams_of[2], (ALTITUDE_TIERS, NLAT, NLON), ((1, 2), (2, 16)), -0.4, 0.0), -0.35, 0.35),
        "spreading_number": draw_spreading_number(jax.random.fold_in(streams_of[8], 71), 0),
        "obs_value": normal_values(streams_of[4], (N_LAT, N_LON, NOB), 1.0, 6.0, ((0, 2), (1, 16)), jnp.float32),
        "obs_site": place_ends(jax.random.randint(streams_of[5], (N_LAT, N_LON, NOB), 0, ALTITUDE_TIERS * NORTH_SOUTH_SPAN * EAST_WEST_SPAN), jax.random.fold_in(streams_of[5], 1), 0, (ALTITUDE_TIERS * NORTH_SOUTH_SPAN * EAST_WEST_SPAN) - 1).astype(jnp.int32),
        "neighbours": draw_neighbours(jax.random.fold_in(streams_of[8], 71), 0),
        "loc_weight": jnp.clip(jnp.exp(math.log(1.0) - 1.89712 * jax.random.uniform(streams_of[7], (NLAT, NLON, NNB), jnp.float32) ** shard_levels(streams_of[7], (NLAT, NLON, NNB), ((0, 2), (1, 16)), -0.2, 0.2)), 0.15, 1.0),
    }


precise = lax.Precision.HIGHEST

def advance_in_time(bordered_values, speed_lon, speed_lat, diffuse):
    centre = bordered_values[:, :, 1:-1, 1:-1]
    west_cell = bordered_values[:, :, 1:-1, :-2]
    east_cell = bordered_values[:, :, 1:-1, 2:]
    south_cell = bordered_values[:, :, :-2, 1:-1]
    north_cell = bordered_values[:, :, 2:, 1:-1]
    flux_lon = jnp.maximum(speed_lon, 0.0) * (centre - west_cell) + jnp.minimum(speed_lon, 0.0) * (east_cell - centre)
    flux_lat = jnp.maximum(speed_lat, 0.0) * (centre - south_cell) + jnp.minimum(speed_lat, 0.0) * (north_cell - centre)
    return centre - flux_lon - flux_lat + diffuse * (west_cell + east_cell + south_cell + north_cell - 4.0 * centre)

def transform_weights(ens_pert, weight, innov_row):
    members = ens_pert.shape[0]
    scaled = ens_pert * weight[None]
    gram_matrix = jnp.einsum('kcn,mcn->ckm', scaled, ens_pert, precision=precise)
    identity = jnp.eye(members, dtype=jnp.float32)
    system = (members - 1.0) * identity + gram_matrix
    scale_bound = members - 1.0 + jnp.sqrt(lax.optimization_barrier(jnp.sum(gram_matrix * gram_matrix, axis=(1, 2))))
    iterate = system / scale_bound[:, None, None]
    inverse = jnp.broadcast_to(identity, system.shape)
    for repeat in range(NS_ITERS):
        correction = 1.5 * identity - 0.5 * jnp.einsum('cij,cjk->cik', inverse, iterate, precision=precise)
        iterate = jnp.einsum('cij,cjk->cik', iterate, correction, precision=precise)
        inverse = jnp.einsum('cij,cjk->cik', correction, inverse, precision=precise)
    drive = jnp.einsum('kcn,cn->ck', ens_pert, weight * innov_row, precision=precise)
    half_way = jnp.einsum('cjk,ck->cj', inverse, drive, precision=precise)
    mean_w = jnp.einsum('cjk,ck->cj', inverse, half_way, precision=precise) / scale_bound[:, None]
    spread = jnp.sqrt((members - 1.0) / scale_bound)[:, None, None] * inverse
    return spread + mean_w[:, :, None]

def apply_weights(vertical_trace, weights_all):
    centre = lax.optimization_barrier(jnp.sum(vertical_trace, axis=0)) / vertical_trace.shape[0]
    deviation = vertical_trace - centre[None]
    return centre[None] + jnp.einsum('jlc,cjk->klc', deviation, weights_all, precision=precise)

def reference(prior_sample_set, eastward_cfl_number, northward_cfl_number, spreading_number, obs_value, obs_site, neighbours, loc_weight):
    predicted_values = prior_sample_set
    for section in range(STEPS):
        bordered_values = jnp.pad(predicted_values, ((0, 0), (0, 0), (1, 1), (0, 0)))
        bordered_values = jnp.concatenate([bordered_values[..., -1:], bordered_values, bordered_values[..., :1]], axis=3)
        predicted_values = advance_in_time(bordered_values, eastward_cfl_number, northward_cfl_number, spreading_number)
    tile_sequence = predicted_values.reshape(SAMPLE_TOTAL, ALTITUDE_TIERS, N_LAT, NORTH_SOUTH_SPAN, N_LON, EAST_WEST_SPAN).transpose(0, 2, 4, 1, 3, 5)
    tile_sequence = tile_sequence.reshape(SAMPLE_TOTAL, N_LAT, N_LON, ALTITUDE_TIERS * NORTH_SOUTH_SPAN * EAST_WEST_SPAN)
    obs_ens = jnp.take_along_axis(tile_sequence, obs_site[None], axis=3)
    obs_mean = lax.optimization_barrier(jnp.sum(obs_ens, axis=0)) / SAMPLE_TOTAL
    obs_pert = obs_ens - obs_mean[None]
    innovation = obs_value - obs_mean

    def one_row(parallel_band):
        own_block = parallel_band // NORTH_SOUTH_SPAN
        near_ids = neighbours[parallel_band]
        block_code = near_ids // NOB
        position = near_ids % NOB
        lat_source = own_block + block_code // 3 - 1
        col_block = jnp.arange(NLON, dtype=jnp.int32) // EAST_WEST_SPAN
        lon_source = (col_block[:, None] + block_code % 3 - 1) % N_LON
        ens_pert = obs_pert[:, lat_source, lon_source, position]
        innov_row = innovation[lat_source, lon_source, position]
        weights_all = transform_weights(ens_pert, loc_weight[parallel_band], innov_row)
        vertical_trace = lax.dynamic_index_in_dim(predicted_values, parallel_band, axis=2, keepdims=False)
        return apply_weights(vertical_trace, weights_all)
    rows = lax.map(one_row, jnp.arange(NLAT, dtype=jnp.int32))
    return jnp.transpose(rows, (1, 2, 0, 3))
```

```python
import functools

import jax
import jax.numpy as jnp
from jax import lax
from jax.experimental import pallas as pl
from jax.experimental.pallas import tpu as pltpu
from jax.sharding import PartitionSpec as P

STEPS = 4
LANES = 128
OWNED = 32
GROUPS = LANES // OWNED
ROWS = 4
BATCH = 16
MEMBERS_HERE = 8
LEVELS = 8
NOB = 256
PLANE = LEVELS * ROWS
VALUE_ROW = 11 * PLANE
SITE_ROW = VALUE_ROW + 2
EDGE_ROW = SITE_ROW + 6
EDGE_ROWS = 16
PAYLOAD = EDGE_ROW + EDGE_ROWS
COLS = LEVELS * OWNED
SPREAD_ROWS = 136
FAR = -8192
F32 = jnp.float32
BF16 = jnp.bfloat16
VMEM_LIMIT = 40 * 1024 * 1024
PAYLOAD_LIMIT = 60 * 1024 * 1024


def vmem(count):
    return [pl.BlockSpec(memory_space=pltpu.VMEM)] * count


def params():
    return pltpu.CompilerParams(vmem_limit_bytes=VMEM_LIMIT)


def lane_index():
    return lax.broadcasted_iota(jnp.int32, (8, LANES), 1)


def lat_masks():
    here = lax.axis_index("lat")
    return [scalar_mask(here, 0), scalar_mask(here, 1)]


def lon_parity():
    return lax.rem(lax.axis_index("lon"), 2)


def scalar_mask(value, wanted):
    return jnp.full((8, LANES), value, jnp.int32) == wanted


def roll(x, shift):
    shift %= LANES
    return x if shift == 0 else pltpu.roll(x, shift, 1)


def member_rows(own_ref, other_ref, here, level, row):
    start = level * ROWS + row % ROWS
    own = own_ref[pl.ds(start, 8, stride=PLANE), :]
    other = other_ref[pl.ds(start, 8, stride=PLANE), :]
    return jnp.where(here[row // ROWS], own, other)


def coef_rows(own_ref, other_ref, here, which, row):
    start = (MEMBERS_HERE + which) * PLANE + row % ROWS
    own = own_ref[pl.ds(start, 8, stride=ROWS), :]
    other = other_ref[pl.ds(start, 8, stride=ROWS), :]
    return jnp.where(here[row // ROWS], own, other)


def payload_kernel(
    prior_ref,
    east_ref,
    north_ref,
    spread_ref,
    value_ref,
    site_ref,
    ids_ref,
    weight_ref,
    out_ref,
    first_ref,
    second_ref,
    ids_out,
    weight_out,
    value,
    site,
    sems,
):
    owned = pl.ds(pl.multiple_of(lax.axis_index("mem") * OWNED, OWNED), OWNED)
    moves = [
        (prior_ref, out_ref.at[pl.ds(0, MEMBERS_HERE * PLANE), :]),
        *[
            (ref, out_ref.at[pl.ds((MEMBERS_HERE + n) * PLANE, PLANE), :])
            for n, ref in enumerate((east_ref, north_ref, spread_ref))
        ],
        (value_ref, value),
        (site_ref, site),
        (ids_ref.at[owned, :], ids_out),
        (weight_ref.at[owned, :], weight_out),
    ]
    copies = [pltpu.make_async_copy(src, dst, sems.at[n]) for n, (src, dst) in enumerate(moves)]
    for copy in copies:
        copy.start()
    for copy in copies:
        copy.wait()
    values = value[...]
    sites = site[...].astype(F32)
    rest = jnp.zeros((PAYLOAD - SITE_ROW - 2, LANES), F32)
    pieces = [values[:, :LANES], values[:, LANES:], sites[:, :LANES], sites[:, LANES:], rest]
    out_ref[VALUE_ROW:, :] = jnp.concatenate(pieces, axis=0)
    lane = lane_index()
    even = scalar_mask(lon_parity(), 0)
    for tile in range(2):
        left = jnp.zeros((8, LANES), F32)
        right = jnp.zeros((8, LANES), F32)
        for slot in range(32 if tile == 0 else 12):
            if tile == 0:
                x = out_ref[pl.ds(slot, 8, stride=PLANE), :]
            else:
                x = out_ref[pl.ds((MEMBERS_HERE + slot // 4) * PLANE + slot % 4, 8, stride=ROWS), :]
            place = (lane // 4) == slot
            left = jnp.where(place, roll(x, 4 * slot), left)
            right = jnp.where(place, roll(x, 4 * slot + 4), right)
        first_ref[tile * 8 : tile * 8 + 8, :] = jnp.where(even, right, left)
        second_ref[tile * 8 : tile * 8 + 8, :] = jnp.where(even, left, right)


def forecast_kernel(
    own_ref, other_ref, first_ref, second_ref, corner_ref, send_ref, values_ref, coef, state
):
    lane = lane_index()
    here = lat_masks()
    even = scalar_mask(lon_parity(), 0)
    first_lane = lane == 0
    last_lane = lane == LANES - 1
    east_lanes = lane < 4
    west_lanes = lane >= LANES - 4
    east, west = {}, {}
    for block in range(2):
        for tile in range(2):
            part = slice(tile * 8, tile * 8 + 8)
            far = slice(EDGE_ROW + tile * 8, EDGE_ROW + tile * 8 + 8)
            a = jnp.where(here[block], first_ref[part, :], other_ref[far, :])
            b = jnp.where(here[block], second_ref[part, :], corner_ref[part, :])
            east[block, tile] = jnp.where(even, a, b)
            west[block, tile] = jnp.where(even, b, a)

    def halo(row, tile, group):
        slot = group * ROWS + row % ROWS
        key = (row // ROWS, tile)
        from_east = roll(east[key], -4 * slot)
        from_west = roll(west[key], LANES - 4 - 4 * slot)
        return jnp.where(east_lanes, from_east, jnp.where(west_lanes, from_west, 0.0))

    for row in range(8):
        for part in range(2):
            if part == 0:
                u, v, d = (coef_rows(own_ref, other_ref, here, q, row) for q in range(3))
            else:
                u, v, d = (halo(row, 1, q) for q in range(3))
            up, un = jnp.maximum(u, 0.0), jnp.minimum(u, 0.0)
            vp, vn = jnp.maximum(v, 0.0), jnp.minimum(v, 0.0)
            coef[row, 0, part] = 1.0 - (up - un) - (vp - vn) - 4.0 * d
            coef[row, 1, part] = up + d
            coef[row, 2, part] = d - un
            coef[row, 3, part] = vp + d
            coef[row, 4, part] = d - vn

    for level in range(LEVELS):
        q = []
        for row in range(8):
            q.append((member_rows(own_ref, other_ref, here, level, row), halo(row, 0, level)))
        for _ in range(STEPS):
            after = []
            for row in range(8):
                centre, border = q[row]
                rc, rb = roll(centre, 1), roll(border, 1)
                lc, lb = roll(centre, -1), roll(border, -1)
                wests = (jnp.where(first_lane, rb, rc), jnp.where(first_lane, rc, rb))
                easts = (jnp.where(last_lane, lb, lc), jnp.where(last_lane, lc, lb))
                pair = []
                for part in range(2):
                    c = [coef[row, n, part, level : level + 1, :] for n in range(5)]
                    total = c[0] * q[row][part] + c[1] * wests[part] + c[2] * easts[part]
                    if row > 0:
                        total = total + c[3] * q[row - 1][part]
                    if row < 7:
                        total = total + c[4] * q[row + 1][part]
                    pair.append(total)
                after.append(tuple(pair))
            q = after
        for row in range(8):
            state[level, row] = q[row][0]

    for block in range(2):
        site_own = jnp.concatenate(
            [own_ref[SITE_ROW : SITE_ROW + 1, :], own_ref[SITE_ROW + 1 : SITE_ROW + 2, :]], axis=1
        )
        site_other = jnp.concatenate(
            [other_ref[SITE_ROW : SITE_ROW + 1, :], other_ref[SITE_ROW + 1 : SITE_ROW + 2, :]], axis=1
        )
        mine = jnp.full((1, NOB), lax.axis_index("lat"), jnp.int32) == block
        site = jnp.where(mine, site_own, site_other).astype(jnp.int32)
        site_row = jnp.broadcast_to(site >> 7, (8, NOB))
        site_lane = jnp.broadcast_to(site & (LANES - 1), (LANES, NOB))
        pick = jnp.where(lax.broadcasted_iota(jnp.int32, (LANES, NOB), 0) == site_lane, 1.0, 0.0).astype(BF16)
        x = state[:, block * ROWS : (block + 1) * ROWS].reshape(PLANE * 8, LANES)
        x1 = x.astype(BF16)
        rest = x - x1.astype(F32)
        x2 = rest.astype(BF16)
        x3 = (rest - x2.astype(F32)).astype(BF16)
        picked = (
            jnp.dot(x3, pick, preferred_element_type=F32)
            + jnp.dot(x2, pick, preferred_element_type=F32)
            + jnp.dot(x1, pick, preferred_element_type=F32)
        )
        total = jnp.zeros((8, NOB), F32)
        for n in range(PLANE):
            total = jnp.where(site_row == n, picked[n * 8 : n * 8 + 8, :], total)
        for target in range(send_ref.shape[0]):
            send_ref[target, :, COLS + block * NOB : COLS + (block + 1) * NOB] = total

    own = jnp.concatenate([own_ref[VALUE_ROW + n : VALUE_ROW + n + 1, :] for n in range(2)], axis=1)
    other = jnp.concatenate([other_ref[VALUE_ROW + n : VALUE_ROW + n + 1, :] for n in range(2)], axis=1)
    south = jnp.full((1, NOB), lax.axis_index("lat"), jnp.int32) == 0
    values = jnp.concatenate([jnp.where(south, own, other), jnp.where(south, other, own)], axis=1)
    values_ref[...] = jnp.broadcast_to(values, (8, 2 * NOB))

    segment = lane // OWNED
    for row in range(ROWS):
        here_row = lax.axis_index("lat") * ROWS + row
        values = [state[level, here_row] for level in range(LEVELS)]
        for group in range(GROUPS):
            for half in range(2):
                total = jnp.zeros((8, LANES), F32)
                for n in range(4):
                    moved = roll(values[half * 4 + n], OWNED * (n - group))
                    total = jnp.where(segment == n, moved, total)
                send_ref[row * GROUPS + group, :, half * LANES : (half + 1) * LANES] = total


def halves(x):
    hi = x.astype(BF16)
    return hi, (x - hi.astype(F32)).astype(BF16)


def left_side(x):
    return jnp.concatenate(halves(x), axis=1)


def product(left, right):
    out = jnp.dot(left, right, preferred_element_type=F32)
    half = out.shape[1] // 2
    return out[:, :half] + out[:, half:]


def small_product(rows, halves_of_right):
    out = jnp.dot(jnp.concatenate(halves(rows), axis=0), halves_of_right, preferred_element_type=F32)
    half = out.shape[1] // 2
    return out[0:16, :half] + (out[0:16, half:] + out[16:32, :half])


def spread_kernel(recv_ref, values_ref, out_ref):
    members = recv_ref.shape[0]
    obs = recv_ref[:, COLS:]
    mean = jnp.sum(obs, axis=0, keepdims=True) / members
    out_ref[0:members, :] = obs - mean
    row = lax.broadcasted_iota(jnp.int32, (8, 2 * NOB), 0)
    out_ref[members:, :] = jnp.where(row == 0, values_ref[...] - mean, 0.0)


def fill_table(table, start, spread_ref):
    width = pl.ds(start, 2 * NOB)
    hi, lo = halves(spread_ref[0:128, :])
    table[0:128, width] = hi
    table[128:256, width] = lo
    innovation = spread_ref[128:129, :]
    first_term = innovation.astype(BF16).astype(F32)
    row = lax.broadcasted_iota(jnp.int32, (16, 2 * NOB), 0)
    extra = jnp.where(row == 0, first_term, jnp.where(row == 1, innovation - first_term, 0.0))
    table[256:272, width] = extra.astype(BF16)


def local_places(ids):
    code = ids >> 8
    lat_step = jnp.where(code >= 6, 2, jnp.where(code >= 3, 1, 0))
    lon_step = code - 3 * lat_step
    odd = jnp.full(ids.shape, lon_parity(), jnp.int32) == 1
    slot = jnp.where(odd, 2 - lon_step, lon_step)
    within = (lat_step - 1 + lax.axis_index("lat")) * NOB + (ids & (NOB - 1))
    near = jnp.where(slot == 0, FAR, within + jnp.where(slot == 2, 2 * NOB, 0))
    far = jnp.where(slot == 0, within, FAR)
    return near.astype(F32), far.astype(F32)


def own_kernel(payload_ref, ids_ref, weight_ref, own_ref, near_ref, far_ref, weight_out):
    own_ref[...] = payload_ref[0:EDGE_ROW, :]
    weight_out[...] = weight_ref[...]
    near_ref[...], far_ref[...] = local_places(ids_ref[...])


def gather_pair(table, places, first_column, blocks):
    place = lax.broadcasted_iota(jnp.int32, (NOB, LANES), 0).astype(F32).astype(BF16)
    one, zero = jnp.ones((), BF16), jnp.zeros((), BF16)
    hot = []
    for block in range(blocks):
        sides = []
        for k in range(2):
            row = places[pl.ds(first_column + k, 1), :] - float(block * NOB)
            sides.append(jnp.where(row.astype(BF16) == place, one, zero))
        hot.append(jnp.concatenate(sides, axis=1))
    both = jnp.dot(table[...], jnp.concatenate(hot, axis=0), preferred_element_type=F32)
    rows = both[0:128] + both[128:256]
    innov = both[256:257] + both[257:258]
    found = jnp.concatenate([rows, jnp.broadcast_to(innov, (8, 2 * LANES))], axis=0)
    return found[:, :LANES], found[:, LANES:]


def near_kernel(
    recv_ref, places, mine_ref, first_ref, part_ref, dev_ref, centre_ref, table
):
    members = recv_ref.shape[0]
    fill_table(table, 0, mine_ref)
    fill_table(table, 2 * NOB, first_ref)
    traces = jnp.transpose(recv_ref[:, :COLS])
    centre = jnp.sum(traces, axis=1, keepdims=True) / members
    dev_ref[...] = traces - centre
    centre_ref[...] = jnp.broadcast_to(centre, traces.shape)

    def turn(n, carry):
        for pair in range(BATCH // 2):
            c = n * BATCH + pair * 2
            left, right = gather_pair(table, places, c, 4)
            part_ref[c] = left
            part_ref[c + 1] = right
        return carry

    lax.fori_loop(0, OWNED // BATCH, turn, 0)


def columns_kernel(
    places,
    weight_ref,
    second_ref,
    part_ref,
    dev_ref,
    centre_ref,
    out_ref,
    table,
    res,
    eye,
    found,
    full,
    half_s,
    half_u,
    half_v,
    half_z,
    drives,
):
    members = 128
    scale = members - 1.0
    fill_table(table, 0, second_ref)
    i0 = lax.broadcasted_iota(jnp.int32, (members, members), 0)
    i1 = lax.broadcasted_iota(jnp.int32, (members, members), 1)
    eye[...] = jnp.where(i0 == i1, 1.0, 0.0).astype(F32)

    def put(ref, b, x):
        hi, lo = halves(x)
        ref[b, :, 0:members] = hi
        ref[b, :, members:] = lo

    def right_of(ref, b):
        top = ref[b]
        low = jnp.concatenate([ref[b, :, 0:members], jnp.zeros((members, members), BF16)], axis=1)
        return jnp.concatenate([top, low], axis=0)

    def turn(n, carry):
        base = n * BATCH
        slots = range(BATCH)
        invs = []
        for pair in range(BATCH // 2):
            for k, extra in enumerate(gather_pair(table, places, base + pair * 2, 2)):
                found[pair * 2 + k] = extra + part_ref[base + pair * 2 + k]
        for b in slots:
            pert = found[b, 0:members]
            innov = found[b, members : members + 1]
            w = weight_ref[pl.ds(base + b, 1), :]
            left = jnp.concatenate([pert * w, jnp.broadcast_to(w * innov, (16, LANES))], axis=0)
            e_hi, e_lo = halves(pert)
            right = jnp.concatenate(
                [
                    jnp.concatenate([e_hi, e_hi], axis=1),
                    jnp.concatenate([e_lo, jnp.zeros_like(e_lo)], axis=1),
                ],
                axis=0,
            )
            both = lax.dot_general(
                left_side(left), right, (((1,), (1,)), ((), ())), preferred_element_type=F32
            )
            both = both[:, :members] + both[:, members:]
            gram = both[:members]
            drives[b] = both[members : members + 8]
            norm = jnp.sum(jnp.sum(gram * gram, axis=0, keepdims=True), axis=1, keepdims=True)
            inv = 1.0 / (scale + jnp.sqrt(norm))
            invs.append(inv)
            s = (scale * eye[...] + gram) * inv
            full[b] = s
            put(half_s, b, s)
        for b in slots:
            square = product(half_s[b], right_of(half_s, b))
            s = full[b]
            put(half_u, b, square)
            put(half_v, b, 0.0625 * square - 0.5625 * s)
            full[b] = 2.25 * eye[...] - 2.4375 * s + 1.6875 * square
        for b in slots:
            put(half_z, b, full[b] + product(half_u[b], right_of(half_v, b)))
        rows = []
        for b in slots:
            x = jnp.concatenate([dev_ref[pl.ds(base + b, 8, stride=OWNED), :], drives[b]], axis=0)
            both = product(jnp.concatenate([half_s[b], left_side(x)], axis=0), right_of(half_z, b))
            put(half_u, b, both[0:members])
            rows.append(both[members:])
        for b in slots:
            put(half_s, b, product(half_u[b], right_of(half_z, b)))
        moved = [0.0625 * x for x in rows]
        for coefficient in (-0.5625, 1.6875, -2.4375, 2.25):
            moved = [coefficient * rows[b] + small_product(moved[b], half_s[b]) for b in slots]
        for b in slots:
            y = moved[b][0:8]
            shift = jnp.sum(y * moved[b][8:16], axis=1, keepdims=True) * invs[b]
            res[pl.ds(base + b, 8, stride=OWNED), :] = jnp.sqrt(scale * invs[b]) * y + shift
        return carry

    lax.fori_loop(0, OWNED // BATCH, turn, 0)
    out_ref[...] = jnp.transpose(res[...] + centre_ref[...])


def unpack_kernel(recv_ref, out_ref):
    segment = lane_index() // OWNED
    for row in range(ROWS):
        for half in range(2):
            parts = [
                recv_ref[row * GROUPS + g, :, half * LANES : (half + 1) * LANES] for g in range(GROUPS)
            ]
            for n in range(4):
                level = half * 4 + n
                total = jnp.zeros((8, LANES), F32)
                for g in range(GROUPS):
                    total = jnp.where(segment == g, roll(parts[g], OWNED * (g - n)), total)
                out_ref[pl.ds(level * ROWS + row, 8, stride=PLANE), :] = total


def call(kernel, shapes, operands, scratch=(), flops=None):
    single = not isinstance(shapes, list)
    cost = None
    if flops is not None:
        cost = pl.CostEstimate(flops=flops, bytes_accessed=1 << 22, transcendentals=0)
    return pl.pallas_call(
        kernel,
        out_shape=shapes,
        in_specs=vmem(len(operands)),
        out_specs=vmem(1)[0] if single else vmem(len(shapes)),
        scratch_shapes=list(scratch),
        compiler_params=params(),
        cost_estimate=cost,
    )(*operands)


def per_device(
    prior_sample_set,
    eastward_cfl_number,
    northward_cfl_number,
    spreading_number,
    obs_value,
    obs_site,
    neighbours,
    loc_weight,
):
    sds = functools.partial(jax.ShapeDtypeStruct, dtype=F32)
    mems = lax.axis_size("mem")
    lons = lax.axis_size("lon")
    on_chip = [(i, i ^ 1) for i in range(lons)]
    whole = 2 * lons
    off_chip, corners = [], []
    for i in range(whole):
        j = (i + 1 if i % 2 else i - 1) % whole
        off_chip.append((i % lons * 2 + i // lons, j % lons * 2 + j // lons))
        corners.append((i % lons * 2 + i // lons, j % lons * 2 + 1 - i // lons))
    off_lon = [(i, (i + 1 if i % 2 else i - 1) % lons) for i in range(lons)]

    edge = sds((EDGE_ROWS, LANES))
    payload, first, second, near_ids, weight = pl.pallas_call(
        payload_kernel,
        out_shape=[
            sds((PAYLOAD, LANES)),
            edge,
            edge,
            jax.ShapeDtypeStruct((OWNED, LANES), jnp.int32),
            sds((OWNED, LANES)),
        ],
        in_specs=[pl.BlockSpec(memory_space=pltpu.HBM)] * 8,
        out_specs=vmem(5),
        scratch_shapes=[
            pltpu.VMEM((1, NOB), F32),
            pltpu.VMEM((1, NOB), jnp.int32),
            pltpu.SemaphoreType.DMA((8,)),
        ],
        compiler_params=pltpu.CompilerParams(vmem_limit_bytes=PAYLOAD_LIMIT),
    )(
        prior_sample_set.reshape(MEMBERS_HERE * PLANE, LANES),
        eastward_cfl_number.reshape(PLANE, LANES),
        northward_cfl_number.reshape(PLANE, LANES),
        spreading_number.reshape(PLANE, LANES),
        obs_value.reshape(1, NOB),
        obs_site.reshape(1, NOB),
        neighbours.reshape(ROWS * LANES, LANES),
        loc_weight.reshape(ROWS * LANES, LANES),
    )
    first_in = lax.ppermute(first, "lon", on_chip)
    payload = lax.dynamic_update_slice(payload, first_in, (EDGE_ROW, 0))
    payload, second = lax.optimization_barrier((payload, second))
    other = lax.ppermute(payload, "lat", [(0, 1), (1, 0)])
    own, near, far, weight = call(
        own_kernel,
        [sds((EDGE_ROW, LANES))] + [sds((OWNED, LANES))] * 3,
        (payload, near_ids, weight),
        flops=1 << 20,
    )
    second_in = lax.ppermute(second, "lon", off_lon)
    corner_in = lax.ppermute(second, ("lon", "lat"), corners)
    send, values = call(
        forecast_kernel,
        [sds((mems, MEMBERS_HERE, COLS + 2 * NOB)), sds((8, 2 * NOB))],
        (own, other, first_in, second_in, corner_in),
        [pltpu.VMEM((8, 5, 2, 8, LANES), F32), pltpu.VMEM((LEVELS, 8, 8, LANES), F32)],
    )
    members = mems * MEMBERS_HERE
    got = lax.all_to_all(
        send.reshape(members, send.shape[2]), "mem", split_axis=0, concat_axis=0, tiled=True
    )
    spread = call(spread_kernel, sds((SPREAD_ROWS, 2 * NOB)), (got, values))
    spread_second = lax.ppermute(spread, ("lon", "lat"), off_chip)
    spread_first = lax.ppermute(spread, "lon", on_chip)
    part, dev, centre = call(
        near_kernel,
        [sds((OWNED, SPREAD_ROWS, LANES)), sds((COLS, members)), sds((COLS, members))],
        (got, near, spread, spread_first),
        [pltpu.VMEM((272, 4 * NOB), BF16)],
        flops=2 * OWNED * LANES * 272 * 4 * NOB,
    )
    updated = call(
        columns_kernel,
        sds((members, COLS)),
        (far, weight, spread_second, part, dev, centre),
        [
            pltpu.VMEM((272, 2 * NOB), BF16),
            pltpu.VMEM((COLS, members), F32),
            pltpu.VMEM((members, members), F32),
            pltpu.VMEM((BATCH, SPREAD_ROWS, LANES), F32),
            pltpu.VMEM((BATCH, members, members), F32),
            *[pltpu.VMEM((BATCH, members, 2 * members), BF16)] * 4,
            pltpu.VMEM((BATCH, 8, members), F32),
        ],
        flops=2 * OWNED * 7 * members * 4 * members * members,
    )
    back = lax.all_to_all(updated, "mem", split_axis=0, concat_axis=0, tiled=True)
    result = call(
        unpack_kernel,
        sds((MEMBERS_HERE * PLANE, LANES)),
        (back.reshape(mems, MEMBERS_HERE, COLS),),
    )
    return result.reshape(prior_sample_set.shape)


def solution(mesh):
    return jax.shard_map(
        per_device,
        mesh=mesh,
        in_specs=(
            P("mem", None, "lat", "lon"),
            P(None, "lat", "lon"),
            P(None, "lat", "lon"),
            P(None, "lat", "lon"),
            P("lat", "lon", None),
            P("lat", "lon", None),
            P("lat", "lon", None),
            P("lat", "lon", None),
        ),
        out_specs=P("mem", None, "lat", "lon"),
        check_vma=False,
    )
```

```python
import functools

import jax
import jax.numpy as jnp
from jax import lax
from jax.experimental import pallas as pl
from jax.experimental.pallas import tpu as pltpu
from jax.sharding import PartitionSpec as P

STEPS = 4
LANES = 128
OWNED = 32
GROUPS = LANES // OWNED
ROWS = 4
BATCH = 32
MEMBERS_HERE = 8
LEVELS = 8
NOB = 256
PLANE = LEVELS * ROWS
VALUE_ROW = 11 * PLANE
SITE_ROW = VALUE_ROW + 2
EDGE_ROW = SITE_ROW + 6
EDGE_ROWS = 16
PAYLOAD = EDGE_ROW + EDGE_ROWS
COLS = LEVELS * OWNED
SPREAD_ROWS = 136
FAR = -8192
F32 = jnp.float32
BF16 = jnp.bfloat16
VMEM_LIMIT = 40 * 1024 * 1024
PAYLOAD_LIMIT = 60 * 1024 * 1024


def vmem(count):
    return [pl.BlockSpec(memory_space=pltpu.VMEM)] * count


def params():
    return pltpu.CompilerParams(vmem_limit_bytes=VMEM_LIMIT)


def lane_index():
    return lax.broadcasted_iota(jnp.int32, (8, LANES), 1)


def lat_masks():
    here = lax.axis_index("lat")
    return [scalar_mask(here, 0), scalar_mask(here, 1)]


def lon_parity():
    return lax.rem(lax.axis_index("lon"), 2)


def scalar_mask(value, wanted):
    return jnp.full((8, LANES), value, jnp.int32) == wanted


def roll(x, shift):
    shift %= LANES
    return x if shift == 0 else pltpu.roll(x, shift, 1)


def member_rows(own_ref, other_ref, here, level, row):
    start = level * ROWS + row % ROWS
    own = own_ref[pl.ds(start, 8, stride=PLANE), :]
    other = other_ref[pl.ds(start, 8, stride=PLANE), :]
    return jnp.where(here[row // ROWS], own, other)


def coef_rows(own_ref, other_ref, here, which, row):
    start = (MEMBERS_HERE + which) * PLANE + row % ROWS
    own = own_ref[pl.ds(start, 8, stride=ROWS), :]
    other = other_ref[pl.ds(start, 8, stride=ROWS), :]
    return jnp.where(here[row // ROWS], own, other)


def payload_kernel(
    prior_ref,
    east_ref,
    north_ref,
    spread_ref,
    value_ref,
    site_ref,
    ids_ref,
    weight_ref,
    out_ref,
    first_ref,
    second_ref,
    ids_out,
    weight_out,
    value,
    site,
    sems,
):
    owned = pl.ds(pl.multiple_of(lax.axis_index("mem") * OWNED, OWNED), OWNED)
    moves = [
        (prior_ref, out_ref.at[pl.ds(0, MEMBERS_HERE * PLANE), :]),
        *[
            (ref, out_ref.at[pl.ds((MEMBERS_HERE + n) * PLANE, PLANE), :])
            for n, ref in enumerate((east_ref, north_ref, spread_ref))
        ],
        (value_ref, value),
        (site_ref, site),
        (ids_ref.at[owned, :], ids_out),
        (weight_ref.at[owned, :], weight_out),
    ]
    copies = [pltpu.make_async_copy(src, dst, sems.at[n]) for n, (src, dst) in enumerate(moves)]
    for copy in copies:
        copy.start()
    for copy in copies:
        copy.wait()
    values = value[...]
    sites = site[...].astype(F32)
    rest = jnp.zeros((PAYLOAD - SITE_ROW - 2, LANES), F32)
    pieces = [values[:, :LANES], values[:, LANES:], sites[:, :LANES], sites[:, LANES:], rest]
    out_ref[VALUE_ROW:, :] = jnp.concatenate(pieces, axis=0)
    lane = lane_index()
    even = scalar_mask(lon_parity(), 0)
    for tile in range(2):
        left = jnp.zeros((8, LANES), F32)
        right = jnp.zeros((8, LANES), F32)
        for slot in range(32 if tile == 0 else 12):
            if tile == 0:
                x = out_ref[pl.ds(slot, 8, stride=PLANE), :]
            else:
                x = out_ref[pl.ds((MEMBERS_HERE + slot // 4) * PLANE + slot % 4, 8, stride=ROWS), :]
            place = (lane // 4) == slot
            left = jnp.where(place, roll(x, 4 * slot), left)
            right = jnp.where(place, roll(x, 4 * slot + 4), right)
        first_ref[tile * 8 : tile * 8 + 8, :] = jnp.where(even, right, left)
        second_ref[tile * 8 : tile * 8 + 8, :] = jnp.where(even, left, right)


def advance_in_time(q, coef, level, first_lane, last_lane):
    after = []
    for row in range(8):
        centre, border = q[row]
        rc, rb = roll(centre, 1), roll(border, 1)
        lc, lb = roll(centre, -1), roll(border, -1)
        wests = (jnp.where(first_lane, rb, rc), jnp.where(first_lane, rc, rb))
        easts = (jnp.where(last_lane, lb, lc), jnp.where(last_lane, lc, lb))
        both = []
        for part in range(2):
            c = [coef[row, n, part, level : level + 1, :] for n in range(5)]
            total = c[0] * q[row][part] + c[1] * wests[part] + c[2] * easts[part]
            if row > 0:
                total = total + c[3] * q[row - 1][part]
            if row < 7:
                total = total + c[4] * q[row + 1][part]
            both.append(total)
        after.append(tuple(both))
    return after


def forecast_kernel(
    own_ref, other_ref, first_ref, second_ref, corner_ref, send_ref, values_ref, coef, state
):
    lane = lane_index()
    here = lat_masks()
    even = scalar_mask(lon_parity(), 0)
    first_lane = lane == 0
    last_lane = lane == LANES - 1
    east_lanes = lane < 4
    west_lanes = lane >= LANES - 4
    east, west = {}, {}
    for block in range(2):
        for tile in range(2):
            part = slice(tile * 8, tile * 8 + 8)
            far = slice(EDGE_ROW + tile * 8, EDGE_ROW + tile * 8 + 8)
            a = jnp.where(here[block], first_ref[part, :], other_ref[far, :])
            b = jnp.where(here[block], second_ref[part, :], corner_ref[part, :])
            east[block, tile] = jnp.where(even, a, b)
            west[block, tile] = jnp.where(even, b, a)

    def halo(row, tile, group):
        slot = group * ROWS + row % ROWS
        key = (row // ROWS, tile)
        from_east = roll(east[key], -4 * slot)
        from_west = roll(west[key], LANES - 4 - 4 * slot)
        return jnp.where(east_lanes, from_east, jnp.where(west_lanes, from_west, 0.0))

    for row in range(8):
        for part in range(2):
            if part == 0:
                u, v, d = (coef_rows(own_ref, other_ref, here, q, row) for q in range(3))
            else:
                u, v, d = (halo(row, 1, q) for q in range(3))
            up, un = jnp.maximum(u, 0.0), jnp.minimum(u, 0.0)
            vp, vn = jnp.maximum(v, 0.0), jnp.minimum(v, 0.0)
            coef[row, 0, part] = 1.0 - (up - un) - (vp - vn) - 4.0 * d
            coef[row, 1, part] = up + d
            coef[row, 2, part] = d - un
            coef[row, 3, part] = vp + d
            coef[row, 4, part] = d - vn

    for level in range(0, LEVELS, 2):
        pair = (level, level + 1)
        q = [
            [(member_rows(own_ref, other_ref, here, n, row), halo(row, 0, n)) for row in range(8)]
            for n in pair
        ]
        for _ in range(STEPS):
            q = [advance_in_time(q[n], coef, pair[n], first_lane, last_lane) for n in range(2)]
        for n in range(2):
            for row in range(8):
                state[pair[n], row] = q[n][row][0]

    for block in range(2):
        site_own = jnp.concatenate(
            [own_ref[SITE_ROW : SITE_ROW + 1, :], own_ref[SITE_ROW + 1 : SITE_ROW + 2, :]], axis=1
        )
        site_other = jnp.concatenate(
            [other_ref[SITE_ROW : SITE_ROW + 1, :], other_ref[SITE_ROW + 1 : SITE_ROW + 2, :]], axis=1
        )
        mine = jnp.full((1, NOB), lax.axis_index("lat"), jnp.int32) == block
        site = jnp.where(mine, site_own, site_other).astype(jnp.int32)
        site_row = jnp.broadcast_to(site >> 7, (8, NOB))
        site_lane = jnp.broadcast_to(site & (LANES - 1), (LANES, NOB))
        pick = jnp.where(lax.broadcasted_iota(jnp.int32, (LANES, NOB), 0) == site_lane, 1.0, 0.0).astype(BF16)
        x = state[:, block * ROWS : (block + 1) * ROWS].reshape(PLANE * 8, LANES)
        x1 = x.astype(BF16)
        rest = x - x1.astype(F32)
        x2 = rest.astype(BF16)
        x3 = (rest - x2.astype(F32)).astype(BF16)
        picked = (
            jnp.dot(x3, pick, preferred_element_type=F32)
            + jnp.dot(x2, pick, preferred_element_type=F32)
            + jnp.dot(x1, pick, preferred_element_type=F32)
        )
        total = jnp.zeros((8, NOB), F32)
        for n in range(PLANE):
            total = jnp.where(site_row == n, picked[n * 8 : n * 8 + 8, :], total)
        for target in range(send_ref.shape[0]):
            send_ref[target, :, COLS + block * NOB : COLS + (block + 1) * NOB] = total

    own = jnp.concatenate([own_ref[VALUE_ROW + n : VALUE_ROW + n + 1, :] for n in range(2)], axis=1)
    other = jnp.concatenate([other_ref[VALUE_ROW + n : VALUE_ROW + n + 1, :] for n in range(2)], axis=1)
    south = jnp.full((1, NOB), lax.axis_index("lat"), jnp.int32) == 0
    values = jnp.concatenate([jnp.where(south, own, other), jnp.where(south, other, own)], axis=1)
    values_ref[...] = jnp.broadcast_to(values, (8, 2 * NOB))

    segment = lane // OWNED
    for row in range(ROWS):
        here_row = lax.axis_index("lat") * ROWS + row
        values = [state[level, here_row] for level in range(LEVELS)]
        for group in range(GROUPS):
            for half in range(2):
                total = jnp.zeros((8, LANES), F32)
                for n in range(4):
                    moved = roll(values[half * 4 + n], OWNED * (n - group))
                    total = jnp.where(segment == n, moved, total)
                send_ref[row * GROUPS + group, :, half * LANES : (half + 1) * LANES] = total


def halves(x):
    hi = x.astype(BF16)
    return hi, (x - hi.astype(F32)).astype(BF16)


def left_side(x):
    return jnp.concatenate(halves(x), axis=1)


def product(left, right):
    out = jnp.dot(left, right, preferred_element_type=F32)
    half = out.shape[1] // 2
    return out[:, :half] + out[:, half:]


def small_product(rows, halves_of_right):
    out = jnp.dot(jnp.concatenate(halves(rows), axis=0), halves_of_right, preferred_element_type=F32)
    half = out.shape[1] // 2
    return out[0:16, :half] + (out[0:16, half:] + out[16:32, :half])


def spread_kernel(recv_ref, values_ref, out_ref):
    members = recv_ref.shape[0]
    obs = recv_ref[:, COLS:]
    mean = jnp.sum(obs, axis=0, keepdims=True) / members
    out_ref[0:members, :] = obs - mean
    row = lax.broadcasted_iota(jnp.int32, (8, 2 * NOB), 0)
    out_ref[members:, :] = jnp.where(row == 0, values_ref[...] - mean, 0.0)


def fill_table(table, start, spread_ref):
    width = pl.ds(start, 2 * NOB)
    hi, lo = halves(spread_ref[0:128, :])
    table[0:128, width] = hi
    table[128:256, width] = lo
    innovation = spread_ref[128:129, :]
    first_term = innovation.astype(BF16).astype(F32)
    row = lax.broadcasted_iota(jnp.int32, (16, 2 * NOB), 0)
    extra = jnp.where(row == 0, first_term, jnp.where(row == 1, innovation - first_term, 0.0))
    table[256:272, width] = extra.astype(BF16)


def local_places(ids):
    code = ids >> 8
    lat_step = jnp.where(code >= 6, 2, jnp.where(code >= 3, 1, 0))
    lon_step = code - 3 * lat_step
    odd = jnp.full(ids.shape, lon_parity(), jnp.int32) == 1
    slot = jnp.where(odd, 2 - lon_step, lon_step)
    within = (lat_step - 1 + lax.axis_index("lat")) * NOB + (ids & (NOB - 1))
    near = jnp.where(slot == 0, FAR, within + jnp.where(slot == 2, 2 * NOB, 0))
    far = jnp.where(slot == 0, within, FAR)
    return near.astype(F32), far.astype(F32)


def own_kernel(payload_ref, ids_ref, weight_ref, own_ref, near_ref, far_ref, weight_out):
    own_ref[...] = payload_ref[0:EDGE_ROW, :]
    weight_out[...] = weight_ref[...]
    near_ref[...], far_ref[...] = local_places(ids_ref[...])


def gather_pair(table, places, first_column, blocks):
    place = lax.broadcasted_iota(jnp.int32, (NOB, LANES), 0).astype(F32).astype(BF16)
    one, zero = jnp.ones((), BF16), jnp.zeros((), BF16)
    hot = []
    for block in range(blocks):
        sides = []
        for k in range(2):
            row = places[pl.ds(first_column + k, 1), :] - float(block * NOB)
            sides.append(jnp.where(row.astype(BF16) == place, one, zero))
        hot.append(jnp.concatenate(sides, axis=1))
    both = jnp.dot(table[...], jnp.concatenate(hot, axis=0), preferred_element_type=F32)
    rows = both[0:128] + both[128:256]
    innov = both[256:257] + both[257:258]
    found = jnp.concatenate([rows, jnp.broadcast_to(innov, (8, 2 * LANES))], axis=0)
    return found[:, :LANES], found[:, LANES:]


def near_kernel(
    recv_ref, places, mine_ref, first_ref, part_ref, dev_ref, centre_ref, table
):
    members = recv_ref.shape[0]
    fill_table(table, 0, mine_ref)
    fill_table(table, 2 * NOB, first_ref)
    traces = jnp.transpose(recv_ref[:, :COLS])
    centre = jnp.sum(traces, axis=1, keepdims=True) / members
    dev_ref[...] = traces - centre
    centre_ref[...] = jnp.broadcast_to(centre, traces.shape)

    def turn(n, carry):
        for pair in range(BATCH // 2):
            c = n * BATCH + pair * 2
            left, right = gather_pair(table, places, c, 4)
            part_ref[c] = left
            part_ref[c + 1] = right
        return carry

    lax.fori_loop(0, OWNED // BATCH, turn, 0)


def columns_kernel(
    places,
    weight_ref,
    second_ref,
    part_ref,
    dev_ref,
    centre_ref,
    out_ref,
    table,
    res,
    eye,
    found,
    full,
    half_s,
    half_u,
    half_v,
    half_z,
    drives,
):
    members = 128
    scale = members - 1.0
    fill_table(table, 0, second_ref)
    i0 = lax.broadcasted_iota(jnp.int32, (members, members), 0)
    i1 = lax.broadcasted_iota(jnp.int32, (members, members), 1)
    eye[...] = jnp.where(i0 == i1, 1.0, 0.0).astype(F32)

    def put(ref, b, x):
        hi, lo = halves(x)
        ref[b, :, 0:members] = hi
        ref[b, :, members:] = lo

    def right_of(ref, b):
        top = ref[b]
        low = jnp.concatenate([ref[b, :, 0:members], jnp.zeros((members, members), BF16)], axis=1)
        return jnp.concatenate([top, low], axis=0)

    def turn(n, carry):
        base = n * BATCH
        slots = range(BATCH)
        invs = []
        for pair in range(BATCH // 2):
            for k, extra in enumerate(gather_pair(table, places, base + pair * 2, 2)):
                found[pair * 2 + k] = extra + part_ref[base + pair * 2 + k]
        for b in slots:
            pert = found[b, 0:members]
            innov = found[b, members : members + 1]
            w = weight_ref[pl.ds(base + b, 1), :]
            left = jnp.concatenate([pert * w, jnp.broadcast_to(w * innov, (16, LANES))], axis=0)
            e_hi, e_lo = halves(pert)
            right = jnp.concatenate(
                [
                    jnp.concatenate([e_hi, e_hi], axis=1),
                    jnp.concatenate([e_lo, jnp.zeros_like(e_lo)], axis=1),
                ],
                axis=0,
            )
            both = lax.dot_general(
                left_side(left), right, (((1,), (1,)), ((), ())), preferred_element_type=F32
            )
            both = both[:, :members] + both[:, members:]
            gram = both[:members]
            drives[b] = both[members : members + 8]
            norm = jnp.sum(jnp.sum(gram * gram, axis=0, keepdims=True), axis=1, keepdims=True)
            inv = 1.0 / (scale + jnp.sqrt(norm))
            invs.append(inv)
            s = (scale * eye[...] + gram) * inv
            full[b] = s
            put(half_s, b, s)
        for b in slots:
            square = product(half_s[b], right_of(half_s, b))
            s = full[b]
            put(half_u, b, square)
            put(half_v, b, 0.0625 * square - 0.5625 * s)
            full[b] = 2.25 * eye[...] - 2.4375 * s + 1.6875 * square
        for b in slots:
            put(half_z, b, full[b] + product(half_u[b], right_of(half_v, b)))
        rows = []
        for b in slots:
            x = jnp.concatenate([dev_ref[pl.ds(base + b, 8, stride=OWNED), :], drives[b]], axis=0)
            both = product(jnp.concatenate([half_s[b], left_side(x)], axis=0), right_of(half_z, b))
            put(half_u, b, both[0:members])
            rows.append(both[members:])
        for b in slots:
            put(half_s, b, product(half_u[b], right_of(half_z, b)))
        moved = [0.0625 * x for x in rows]
        for coefficient in (-0.5625, 1.6875, -2.4375, 2.25):
            moved = [coefficient * rows[b] + small_product(moved[b], half_s[b]) for b in slots]
        for b in slots:
            y = moved[b][0:8]
            shift = jnp.sum(y * moved[b][8:16], axis=1, keepdims=True) * invs[b]
            res[pl.ds(base + b, 8, stride=OWNED), :] = jnp.sqrt(scale * invs[b]) * y + shift
        return carry

    lax.fori_loop(0, OWNED // BATCH, turn, 0)
    out_ref[...] = jnp.transpose(res[...] + centre_ref[...])


def unpack_kernel(recv_ref, out_ref):
    segment = lane_index() // OWNED
    for row in range(ROWS):
        for half in range(2):
            parts = [
                recv_ref[row * GROUPS + g, :, half * LANES : (half + 1) * LANES] for g in range(GROUPS)
            ]
            for n in range(4):
                level = half * 4 + n
                total = jnp.zeros((8, LANES), F32)
                for g in range(GROUPS):
                    total = jnp.where(segment == g, roll(parts[g], OWNED * (g - n)), total)
                out_ref[pl.ds(level * ROWS + row, 8, stride=PLANE), :] = total


def call(kernel, shapes, operands, scratch=(), flops=None):
    single = not isinstance(shapes, list)
    cost = None
    if flops is not None:
        cost = pl.CostEstimate(flops=flops, bytes_accessed=1 << 22, transcendentals=0)
    return pl.pallas_call(
        kernel,
        out_shape=shapes,
        in_specs=vmem(len(operands)),
        out_specs=vmem(1)[0] if single else vmem(len(shapes)),
        scratch_shapes=list(scratch),
        compiler_params=params(),
        cost_estimate=cost,
    )(*operands)


def per_device(
    prior_sample_set,
    eastward_cfl_number,
    northward_cfl_number,
    spreading_number,
    obs_value,
    obs_site,
    neighbours,
    loc_weight,
):
    sds = functools.partial(jax.ShapeDtypeStruct, dtype=F32)
    mems = lax.axis_size("mem")
    lons = lax.axis_size("lon")
    on_chip = [(i, i ^ 1) for i in range(lons)]
    whole = 2 * lons
    off_chip, corners = [], []
    for i in range(whole):
        j = (i + 1 if i % 2 else i - 1) % whole
        off_chip.append((i % lons * 2 + i // lons, j % lons * 2 + j // lons))
        corners.append((i % lons * 2 + i // lons, j % lons * 2 + 1 - i // lons))
    off_lon = [(i, (i + 1 if i % 2 else i - 1) % lons) for i in range(lons)]

    edge = sds((EDGE_ROWS, LANES))
    payload, first, second, near_ids, weight = pl.pallas_call(
        payload_kernel,
        out_shape=[
            sds((PAYLOAD, LANES)),
            edge,
            edge,
            jax.ShapeDtypeStruct((OWNED, LANES), jnp.int32),
            sds((OWNED, LANES)),
        ],
        in_specs=[pl.BlockSpec(memory_space=pltpu.HBM)] * 8,
        out_specs=vmem(5),
        scratch_shapes=[
            pltpu.VMEM((1, NOB), F32),
            pltpu.VMEM((1, NOB), jnp.int32),
            pltpu.SemaphoreType.DMA((8,)),
        ],
        compiler_params=pltpu.CompilerParams(vmem_limit_bytes=PAYLOAD_LIMIT),
    )(
        prior_sample_set.reshape(MEMBERS_HERE * PLANE, LANES),
        eastward_cfl_number.reshape(PLANE, LANES),
        northward_cfl_number.reshape(PLANE, LANES),
        spreading_number.reshape(PLANE, LANES),
        obs_value.reshape(1, NOB),
        obs_site.reshape(1, NOB),
        neighbours.reshape(ROWS * LANES, LANES),
        loc_weight.reshape(ROWS * LANES, LANES),
    )
    first_in = lax.ppermute(first, "lon", on_chip)
    payload = lax.dynamic_update_slice(payload, first_in, (EDGE_ROW, 0))
    payload, second = lax.optimization_barrier((payload, second))
    other = lax.ppermute(payload, "lat", [(0, 1), (1, 0)])
    own, near, far, weight = call(
        own_kernel,
        [sds((EDGE_ROW, LANES))] + [sds((OWNED, LANES))] * 3,
        (payload, near_ids, weight),
        flops=1 << 20,
    )
    second_in = lax.ppermute(second, "lon", off_lon)
    corner_in = lax.ppermute(second, ("lon", "lat"), corners)
    send, values = call(
        forecast_kernel,
        [sds((mems, MEMBERS_HERE, COLS + 2 * NOB)), sds((8, 2 * NOB))],
        (own, other, first_in, second_in, corner_in),
        [pltpu.VMEM((8, 5, 2, 8, LANES), F32), pltpu.VMEM((LEVELS, 8, 8, LANES), F32)],
    )
    members = mems * MEMBERS_HERE
    got = lax.all_to_all(
        send.reshape(members, send.shape[2]), "mem", split_axis=0, concat_axis=0, tiled=True
    )
    spread = call(spread_kernel, sds((SPREAD_ROWS, 2 * NOB)), (got, values))
    spread_second = lax.ppermute(spread, ("lon", "lat"), off_chip)
    spread_first = lax.ppermute(spread, "lon", on_chip)
    part, dev, centre = call(
        near_kernel,
        [sds((OWNED, SPREAD_ROWS, LANES)), sds((COLS, members)), sds((COLS, members))],
        (got, near, spread, spread_first),
        [pltpu.VMEM((272, 4 * NOB), BF16)],
        flops=2 * OWNED * LANES * 272 * 4 * NOB,
    )
    updated = call(
        columns_kernel,
        sds((members, COLS)),
        (far, weight, spread_second, part, dev, centre),
        [
            pltpu.VMEM((272, 2 * NOB), BF16),
            pltpu.VMEM((COLS, members), F32),
            pltpu.VMEM((members, members), F32),
            pltpu.VMEM((BATCH, SPREAD_ROWS, LANES), F32),
            pltpu.VMEM((BATCH, members, members), F32),
            *[pltpu.VMEM((BATCH, members, 2 * members), BF16)] * 4,
            pltpu.VMEM((BATCH, 8, members), F32),
        ],
        flops=2 * OWNED * 7 * members * 4 * members * members,
    )
    back = lax.all_to_all(updated, "mem", split_axis=0, concat_axis=0, tiled=True)
    result = call(
        unpack_kernel,
        sds((MEMBERS_HERE * PLANE, LANES)),
        (back.reshape(mems, MEMBERS_HERE, COLS),),
    )
    return result.reshape(prior_sample_set.shape)


def solution(mesh):
    return jax.shard_map(
        per_device,
        mesh=mesh,
        in_specs=(
            P("mem", None, "lat", "lon"),
            P(None, "lat", "lon"),
            P(None, "lat", "lon"),
            P(None, "lat", "lon"),
            P("lat", "lon", None),
            P("lat", "lon", None),
            P("lat", "lon", None),
            P("lat", "lon", None),
        ),
        out_specs=P("mem", None, "lat", "lon"),
        check_vma=False,
    )
```

```python
import functools

import jax
import jax.numpy as jnp
from jax import lax
from jax.experimental import pallas as pl
from jax.experimental.pallas import tpu as pltpu
from jax.sharding import PartitionSpec as P

STEPS = 4
LANES = 128
OWNED = 32
GROUPS = LANES // OWNED
ROWS = 4
BATCH = 32
MEMBERS_HERE = 8
LEVELS = 8
NOB = 256
PLANE = LEVELS * ROWS
VALUE_ROW = 11 * PLANE
SITE_ROW = VALUE_ROW + 2
EDGE_ROW = SITE_ROW + 6
EDGE_ROWS = 16
PAYLOAD = EDGE_ROW + EDGE_ROWS
COLS = LEVELS * OWNED
SPREAD_ROWS = 136
FAR = -8192
F32 = jnp.float32
BF16 = jnp.bfloat16
VMEM_LIMIT = 40 * 1024 * 1024
PAYLOAD_LIMIT = 60 * 1024 * 1024


def vmem(count):
    return [pl.BlockSpec(memory_space=pltpu.VMEM)] * count


def params():
    return pltpu.CompilerParams(vmem_limit_bytes=VMEM_LIMIT)


def lane_index():
    return lax.broadcasted_iota(jnp.int32, (8, LANES), 1)


def lat_masks():
    here = lax.axis_index("lat")
    return [scalar_mask(here, 0), scalar_mask(here, 1)]


def lon_parity():
    return lax.rem(lax.axis_index("lon"), 2)


def scalar_mask(value, wanted):
    return jnp.full((8, LANES), value, jnp.int32) == wanted


def roll(x, shift):
    shift %= LANES
    return x if shift == 0 else pltpu.roll(x, shift, 1)


def member_rows(own_ref, other_ref, here, level, row):
    start = level * ROWS + row % ROWS
    own = own_ref[pl.ds(start, 8, stride=PLANE), :]
    other = other_ref[pl.ds(start, 8, stride=PLANE), :]
    return jnp.where(here[row // ROWS], own, other)


def coef_rows(own_ref, other_ref, here, which, row):
    start = (MEMBERS_HERE + which) * PLANE + row % ROWS
    own = own_ref[pl.ds(start, 8, stride=ROWS), :]
    other = other_ref[pl.ds(start, 8, stride=ROWS), :]
    return jnp.where(here[row // ROWS], own, other)


def payload_kernel(
    prior_ref,
    east_ref,
    north_ref,
    spread_ref,
    value_ref,
    site_ref,
    ids_ref,
    weight_ref,
    out_ref,
    first_ref,
    second_ref,
    ids_out,
    weight_out,
    value,
    site,
    sems,
):
    owned = pl.ds(pl.multiple_of(lax.axis_index("mem") * OWNED, OWNED), OWNED)
    moves = [
        (prior_ref, out_ref.at[pl.ds(0, MEMBERS_HERE * PLANE), :]),
        *[
            (ref, out_ref.at[pl.ds((MEMBERS_HERE + n) * PLANE, PLANE), :])
            for n, ref in enumerate((east_ref, north_ref, spread_ref))
        ],
        (value_ref, value),
        (site_ref, site),
        (ids_ref.at[owned, :], ids_out),
        (weight_ref.at[owned, :], weight_out),
    ]
    copies = [pltpu.make_async_copy(src, dst, sems.at[n]) for n, (src, dst) in enumerate(moves)]
    for copy in copies:
        copy.start()
    for copy in copies:
        copy.wait()
    values = value[...]
    sites = site[...].astype(F32)
    rest = jnp.zeros((PAYLOAD - SITE_ROW - 2, LANES), F32)
    pieces = [values[:, :LANES], values[:, LANES:], sites[:, :LANES], sites[:, LANES:], rest]
    out_ref[VALUE_ROW:, :] = jnp.concatenate(pieces, axis=0)
    lane = lane_index()
    even = scalar_mask(lon_parity(), 0)
    for tile in range(2):
        left = jnp.zeros((8, LANES), F32)
        right = jnp.zeros((8, LANES), F32)
        for slot in range(32 if tile == 0 else 12):
            if tile == 0:
                x = out_ref[pl.ds(slot, 8, stride=PLANE), :]
            else:
                x = out_ref[pl.ds((MEMBERS_HERE + slot // 4) * PLANE + slot % 4, 8, stride=ROWS), :]
            place = (lane // 4) == slot
            left = jnp.where(place, roll(x, 4 * slot), left)
            right = jnp.where(place, roll(x, 4 * slot + 4), right)
        first_ref[tile * 8 : tile * 8 + 8, :] = jnp.where(even, right, left)
        second_ref[tile * 8 : tile * 8 + 8, :] = jnp.where(even, left, right)


def advance_in_time(q, coef, level, first_lane, last_lane):
    after = []
    for row in range(8):
        centre, border = q[row]
        rc, rb = roll(centre, 1), roll(border, 1)
        lc, lb = roll(centre, -1), roll(border, -1)
        wests = (jnp.where(first_lane, rb, rc), jnp.where(first_lane, rc, rb))
        easts = (jnp.where(last_lane, lb, lc), jnp.where(last_lane, lc, lb))
        both = []
        for part in range(2):
            c = [coef[row, n, part, level : level + 1, :] for n in range(5)]
            total = c[0] * q[row][part] + c[1] * wests[part] + c[2] * easts[part]
            if row > 0:
                total = total + c[3] * q[row - 1][part]
            if row < 7:
                total = total + c[4] * q[row + 1][part]
            both.append(total)
        after.append(tuple(both))
    return after


def forecast_kernel(
    own_ref, other_ref, corner_ref, second_ref, first_ref, send_ref, values_ref, coef, state
):
    lane = lane_index()
    here = lat_masks()
    even = scalar_mask(lon_parity(), 0)
    first_lane = lane == 0
    last_lane = lane == LANES - 1
    east_lanes = lane < 4
    west_lanes = lane >= LANES - 4
    east, west = {}, {}
    for block in range(2):
        for tile in range(2):
            part = slice(tile * 8, tile * 8 + 8)
            far = slice(EDGE_ROW + tile * 8, EDGE_ROW + tile * 8 + 8)
            a = jnp.where(here[block], first_ref[part, :], other_ref[far, :])
            b = jnp.where(here[block], second_ref[part, :], corner_ref[part, :])
            east[block, tile] = jnp.where(even, a, b)
            west[block, tile] = jnp.where(even, b, a)

    def halo(row, tile, group):
        slot = group * ROWS + row % ROWS
        key = (row // ROWS, tile)
        from_east = roll(east[key], -4 * slot)
        from_west = roll(west[key], LANES - 4 - 4 * slot)
        return jnp.where(east_lanes, from_east, jnp.where(west_lanes, from_west, 0.0))

    for row in range(8):
        for part in range(2):
            if part == 0:
                u, v, d = (coef_rows(own_ref, other_ref, here, q, row) for q in range(3))
            else:
                u, v, d = (halo(row, 1, q) for q in range(3))
            up, un = jnp.maximum(u, 0.0), jnp.minimum(u, 0.0)
            vp, vn = jnp.maximum(v, 0.0), jnp.minimum(v, 0.0)
            coef[row, 0, part] = 1.0 - (up - un) - (vp - vn) - 4.0 * d
            coef[row, 1, part] = up + d
            coef[row, 2, part] = d - un
            coef[row, 3, part] = vp + d
            coef[row, 4, part] = d - vn

    for level in range(0, LEVELS, 2):
        pair = (level, level + 1)
        q = [
            [(member_rows(own_ref, other_ref, here, n, row), halo(row, 0, n)) for row in range(8)]
            for n in pair
        ]
        for _ in range(STEPS):
            q = [advance_in_time(q[n], coef, pair[n], first_lane, last_lane) for n in range(2)]
        for n in range(2):
            for row in range(8):
                state[pair[n], row] = q[n][row][0]

    for block in range(2):
        site_own = jnp.concatenate(
            [own_ref[SITE_ROW : SITE_ROW + 1, :], own_ref[SITE_ROW + 1 : SITE_ROW + 2, :]], axis=1
        )
        site_other = jnp.concatenate(
            [other_ref[SITE_ROW : SITE_ROW + 1, :], other_ref[SITE_ROW + 1 : SITE_ROW + 2, :]], axis=1
        )
        mine = jnp.full((1, NOB), lax.axis_index("lat"), jnp.int32) == block
        site = jnp.where(mine, site_own, site_other).astype(jnp.int32)
        site_row = jnp.broadcast_to(site >> 7, (8, NOB))
        site_lane = jnp.broadcast_to(site & (LANES - 1), (LANES, NOB))
        pick = jnp.where(lax.broadcasted_iota(jnp.int32, (LANES, NOB), 0) == site_lane, 1.0, 0.0).astype(BF16)
        x = state[:, block * ROWS : (block + 1) * ROWS].reshape(PLANE * 8, LANES)
        x1 = x.astype(BF16)
        rest = x - x1.astype(F32)
        x2 = rest.astype(BF16)
        x3 = (rest - x2.astype(F32)).astype(BF16)
        picked = (
            jnp.dot(x3, pick, preferred_element_type=F32)
            + jnp.dot(x2, pick, preferred_element_type=F32)
            + jnp.dot(x1, pick, preferred_element_type=F32)
        )
        total = jnp.zeros((8, NOB), F32)
        for n in range(PLANE):
            total = jnp.where(site_row == n, picked[n * 8 : n * 8 + 8, :], total)
        for target in range(send_ref.shape[0]):
            send_ref[target, :, COLS + block * NOB : COLS + (block + 1) * NOB] = total

    own = jnp.concatenate([own_ref[VALUE_ROW + n : VALUE_ROW + n + 1, :] for n in range(2)], axis=1)
    other = jnp.concatenate([other_ref[VALUE_ROW + n : VALUE_ROW + n + 1, :] for n in range(2)], axis=1)
    south = jnp.full((1, NOB), lax.axis_index("lat"), jnp.int32) == 0
    values = jnp.concatenate([jnp.where(south, own, other), jnp.where(south, other, own)], axis=1)
    values_ref[...] = jnp.broadcast_to(values, (8, 2 * NOB))

    segment = lane // OWNED
    for row in range(ROWS):
        here_row = lax.axis_index("lat") * ROWS + row
        values = [state[level, here_row] for level in range(LEVELS)]
        for group in range(GROUPS):
            for half in range(2):
                total = jnp.zeros((8, LANES), F32)
                for n in range(4):
                    moved = roll(values[half * 4 + n], OWNED * (n - group))
                    total = jnp.where(segment == n, moved, total)
                send_ref[row * GROUPS + group, :, half * LANES : (half + 1) * LANES] = total


def halves(x):
    hi = x.astype(BF16)
    return hi, (x - hi.astype(F32)).astype(BF16)


def left_side(x):
    return jnp.concatenate(halves(x), axis=1)


def product(left, right):
    out = jnp.dot(left, right, preferred_element_type=F32)
    half = out.shape[1] // 2
    return out[:, :half] + out[:, half:]


def small_product(rows, halves_of_right):
    out = jnp.dot(jnp.concatenate(halves(rows), axis=0), halves_of_right, preferred_element_type=F32)
    half = out.shape[1] // 2
    return out[0:16, :half] + (out[0:16, half:] + out[16:32, :half])


def spread_kernel(recv_ref, values_ref, out_ref):
    members = recv_ref.shape[0]
    obs = recv_ref[:, COLS:]
    mean = jnp.sum(obs, axis=0, keepdims=True) / members
    out_ref[0:members, :] = obs - mean
    row = lax.broadcasted_iota(jnp.int32, (8, 2 * NOB), 0)
    out_ref[members:, :] = jnp.where(row == 0, values_ref[...] - mean, 0.0)


def fill_table(table, start, spread_ref):
    width = pl.ds(start, 2 * NOB)
    hi, lo = halves(spread_ref[0:128, :])
    table[0:128, width] = hi
    table[128:256, width] = lo
    innovation = spread_ref[128:129, :]
    first_term = innovation.astype(BF16).astype(F32)
    row = lax.broadcasted_iota(jnp.int32, (16, 2 * NOB), 0)
    extra = jnp.where(row == 0, first_term, jnp.where(row == 1, innovation - first_term, 0.0))
    table[256:272, width] = extra.astype(BF16)


def local_places(ids):
    code = ids >> 8
    lat_step = jnp.where(code >= 6, 2, jnp.where(code >= 3, 1, 0))
    lon_step = code - 3 * lat_step
    odd = jnp.full(ids.shape, lon_parity(), jnp.int32) == 1
    slot = jnp.where(odd, 2 - lon_step, lon_step)
    within = (lat_step - 1 + lax.axis_index("lat")) * NOB + (ids & (NOB - 1))
    near = jnp.where(slot == 0, FAR, within + jnp.where(slot == 2, 2 * NOB, 0))
    far = jnp.where(slot == 0, within, FAR)
    return near.astype(F32), far.astype(F32)


def own_kernel(payload_ref, ids_ref, weight_ref, own_ref, near_ref, far_ref, weight_out):
    own_ref[...] = payload_ref[0:EDGE_ROW, :]
    weight_out[...] = weight_ref[...]
    near_ref[...], far_ref[...] = local_places(ids_ref[...])


def gather_pair(table, places, first_column, blocks):
    place = lax.broadcasted_iota(jnp.int32, (NOB, LANES), 0).astype(F32).astype(BF16)
    one, zero = jnp.ones((), BF16), jnp.zeros((), BF16)
    hot = []
    for block in range(blocks):
        sides = []
        for k in range(2):
            row = places[pl.ds(first_column + k, 1), :] - float(block * NOB)
            sides.append(jnp.where(row.astype(BF16) == place, one, zero))
        hot.append(jnp.concatenate(sides, axis=1))
    both = jnp.dot(table[...], jnp.concatenate(hot, axis=0), preferred_element_type=F32)
    rows = both[0:128] + both[128:256]
    innov = both[256:257] + both[257:258]
    found = jnp.concatenate([rows, jnp.broadcast_to(innov, (8, 2 * LANES))], axis=0)
    return found[:, :LANES], found[:, LANES:]


def near_kernel(
    recv_ref, places, mine_ref, first_ref, part_ref, dev_ref, centre_ref, table
):
    members = recv_ref.shape[0]
    fill_table(table, 0, mine_ref)
    fill_table(table, 2 * NOB, first_ref)
    traces = jnp.transpose(recv_ref[:, :COLS])
    centre = jnp.sum(traces, axis=1, keepdims=True) / members
    dev_ref[...] = traces - centre
    centre_ref[...] = jnp.broadcast_to(centre, traces.shape)

    def turn(n, carry):
        for pair in range(BATCH // 2):
            c = n * BATCH + pair * 2
            left, right = gather_pair(table, places, c, 4)
            part_ref[c] = left
            part_ref[c + 1] = right
        return carry

    lax.fori_loop(0, OWNED // BATCH, turn, 0)


def columns_kernel(
    places,
    weight_ref,
    second_ref,
    part_ref,
    dev_ref,
    centre_ref,
    out_ref,
    table,
    res,
    eye,
    found,
    full,
    half_s,
    half_u,
    half_v,
    half_z,
    drives,
):
    members = 128
    scale = members - 1.0
    fill_table(table, 0, second_ref)
    i0 = lax.broadcasted_iota(jnp.int32, (members, members), 0)
    i1 = lax.broadcasted_iota(jnp.int32, (members, members), 1)
    eye[...] = jnp.where(i0 == i1, 1.0, 0.0).astype(F32)

    def put(ref, b, x):
        hi, lo = halves(x)
        ref[b, :, 0:members] = hi
        ref[b, :, members:] = lo

    def right_of(ref, b):
        top = ref[b]
        low = jnp.concatenate([ref[b, :, 0:members], jnp.zeros((members, members), BF16)], axis=1)
        return jnp.concatenate([top, low], axis=0)

    def turn(n, carry):
        base = n * BATCH
        slots = range(BATCH)
        invs = []
        for pair in range(BATCH // 2):
            for k, extra in enumerate(gather_pair(table, places, base + pair * 2, 2)):
                found[pair * 2 + k] = extra + part_ref[base + pair * 2 + k]
        for b in slots:
            pert = found[b, 0:members]
            innov = found[b, members : members + 1]
            w = weight_ref[pl.ds(base + b, 1), :]
            left = jnp.concatenate([pert * w, jnp.broadcast_to(w * innov, (16, LANES))], axis=0)
            e_hi, e_lo = halves(jnp.transpose(pert))
            right = jnp.concatenate(
                [
                    jnp.concatenate([e_hi, e_lo], axis=1),
                    jnp.concatenate([e_hi, jnp.zeros_like(e_hi)], axis=1),
                ],
                axis=0,
            )
            both = product(left_side(left), right)
            gram = both[:members]
            drives[b] = both[members : members + 8]
            norm = jnp.sum(jnp.sum(gram * gram, axis=0, keepdims=True), axis=1, keepdims=True)
            inv = 1.0 / (scale + jnp.sqrt(norm))
            invs.append(inv)
            s = (scale * eye[...] + gram) * inv
            full[b] = s
            put(half_s, b, s)
        for b in slots:
            square = product(half_s[b], right_of(half_s, b))
            s = full[b]
            put(half_u, b, square)
            put(half_v, b, 0.0625 * square - 0.5625 * s)
            full[b] = 2.25 * eye[...] - 2.4375 * s + 1.6875 * square
        for b in slots:
            put(half_z, b, full[b] + product(half_u[b], right_of(half_v, b)))
        rows = []
        for b in slots:
            x = jnp.concatenate([dev_ref[pl.ds(base + b, 8, stride=OWNED), :], drives[b]], axis=0)
            both = product(jnp.concatenate([half_s[b], left_side(x)], axis=0), right_of(half_z, b))
            put(half_u, b, both[0:members])
            rows.append(both[members:])
        for b in slots:
            put(half_s, b, product(half_u[b], right_of(half_z, b)))
        moved = [0.0625 * x for x in rows]
        for coefficient in (-0.5625, 1.6875, -2.4375, 2.25):
            moved = [coefficient * rows[b] + small_product(moved[b], half_s[b]) for b in slots]
        for b in slots:
            y = moved[b][0:8]
            shift = jnp.sum(y * moved[b][8:16], axis=1, keepdims=True) * invs[b]
            res[pl.ds(base + b, 8, stride=OWNED), :] = jnp.sqrt(scale * invs[b]) * y + shift
        return carry

    lax.fori_loop(0, OWNED // BATCH, turn, 0)
    out_ref[...] = jnp.transpose(res[...] + centre_ref[...])


def unpack_kernel(recv_ref, out_ref):
    segment = lane_index() // OWNED
    for row in range(ROWS):
        for half in range(2):
            parts = [
                recv_ref[row * GROUPS + g, :, half * LANES : (half + 1) * LANES] for g in range(GROUPS)
            ]
            for n in range(4):
                level = half * 4 + n
                total = jnp.zeros((8, LANES), F32)
                for g in range(GROUPS):
                    total = jnp.where(segment == g, roll(parts[g], OWNED * (g - n)), total)
                out_ref[pl.ds(level * ROWS + row, 8, stride=PLANE), :] = total


def call(kernel, shapes, operands, scratch=(), flops=None):
    single = not isinstance(shapes, list)
    cost = None
    if flops is not None:
        cost = pl.CostEstimate(flops=flops, bytes_accessed=1 << 22, transcendentals=0)
    return pl.pallas_call(
        kernel,
        out_shape=shapes,
        in_specs=vmem(len(operands)),
        out_specs=vmem(1)[0] if single else vmem(len(shapes)),
        scratch_shapes=list(scratch),
        compiler_params=params(),
        cost_estimate=cost,
    )(*operands)


def per_device(
    prior_sample_set,
    eastward_cfl_number,
    northward_cfl_number,
    spreading_number,
    obs_value,
    obs_site,
    neighbours,
    loc_weight,
):
    sds = functools.partial(jax.ShapeDtypeStruct, dtype=F32)
    mems = lax.axis_size("mem")
    lons = lax.axis_size("lon")
    on_chip = [(i, i ^ 1) for i in range(lons)]
    whole = 2 * lons
    off_chip, corners = [], []
    for i in range(whole):
        j = (i + 1 if i % 2 else i - 1) % whole
        off_chip.append((i % lons * 2 + i // lons, j % lons * 2 + j // lons))
        corners.append((i % lons * 2 + i // lons, j % lons * 2 + 1 - i // lons))
    off_lon = [(i, (i + 1 if i % 2 else i - 1) % lons) for i in range(lons)]

    edge = sds((EDGE_ROWS, LANES))
    payload, first, second, near_ids, weight = pl.pallas_call(
        payload_kernel,
        out_shape=[
            sds((PAYLOAD, LANES)),
            edge,
            edge,
            jax.ShapeDtypeStruct((OWNED, LANES), jnp.int32),
            sds((OWNED, LANES)),
        ],
        in_specs=[pl.BlockSpec(memory_space=pltpu.HBM)] * 8,
        out_specs=vmem(5),
        scratch_shapes=[
            pltpu.VMEM((1, NOB), F32),
            pltpu.VMEM((1, NOB), jnp.int32),
            pltpu.SemaphoreType.DMA((8,)),
        ],
        compiler_params=pltpu.CompilerParams(vmem_limit_bytes=PAYLOAD_LIMIT),
    )(
        prior_sample_set.reshape(MEMBERS_HERE * PLANE, LANES),
        eastward_cfl_number.reshape(PLANE, LANES),
        northward_cfl_number.reshape(PLANE, LANES),
        spreading_number.reshape(PLANE, LANES),
        obs_value.reshape(1, NOB),
        obs_site.reshape(1, NOB),
        neighbours.reshape(ROWS * LANES, LANES),
        loc_weight.reshape(ROWS * LANES, LANES),
    )
    first_in = lax.ppermute(first, "lon", on_chip)
    payload = lax.dynamic_update_slice(payload, first_in, (EDGE_ROW, 0))
    payload, second = lax.optimization_barrier((payload, second))
    other = lax.ppermute(payload, "lat", [(0, 1), (1, 0)])
    own, near, far, weight = call(
        own_kernel,
        [sds((EDGE_ROW, LANES))] + [sds((OWNED, LANES))] * 3,
        (payload, near_ids, weight),
        flops=1 << 20,
    )
    corner_in = lax.ppermute(second, ("lon", "lat"), corners)
    second_in = lax.ppermute(second, "lon", off_lon)
    send, values = call(
        forecast_kernel,
        [sds((mems, MEMBERS_HERE, COLS + 2 * NOB)), sds((8, 2 * NOB))],
        (own, other, corner_in, second_in, first_in),
        [pltpu.VMEM((8, 5, 2, 8, LANES), F32), pltpu.VMEM((LEVELS, 8, 8, LANES), F32)],
    )
    members = mems * MEMBERS_HERE
    got = lax.all_to_all(
        send.reshape(members, send.shape[2]), "mem", split_axis=0, concat_axis=0, tiled=True
    )
    spread = call(spread_kernel, sds((SPREAD_ROWS, 2 * NOB)), (got, values))
    spread_second = lax.ppermute(spread, ("lon", "lat"), off_chip)
    spread_first = lax.ppermute(spread, "lon", on_chip)
    part, dev, centre = call(
        near_kernel,
        [sds((OWNED, SPREAD_ROWS, LANES)), sds((COLS, members)), sds((COLS, members))],
        (got, near, spread, spread_first),
        [pltpu.VMEM((272, 4 * NOB), BF16)],
        flops=2 * OWNED * LANES * 272 * 4 * NOB,
    )
    updated = call(
        columns_kernel,
        sds((members, COLS)),
        (far, weight, spread_second, part, dev, centre),
        [
            pltpu.VMEM((272, 2 * NOB), BF16),
            pltpu.VMEM((COLS, members), F32),
            pltpu.VMEM((members, members), F32),
            pltpu.VMEM((BATCH, SPREAD_ROWS, LANES), F32),
            pltpu.VMEM((BATCH, members, members), F32),
            *[pltpu.VMEM((BATCH, members, 2 * members), BF16)] * 4,
            pltpu.VMEM((BATCH, 8, members), F32),
        ],
        flops=2 * OWNED * 7 * members * 4 * members * members,
    )
    back = lax.all_to_all(updated, "mem", split_axis=0, concat_axis=0, tiled=True)
    result = call(
        unpack_kernel,
        sds((MEMBERS_HERE * PLANE, LANES)),
        (back.reshape(mems, MEMBERS_HERE, COLS),),
    )
    return result.reshape(prior_sample_set.shape)


def solution(mesh):
    return jax.shard_map(
        per_device,
        mesh=mesh,
        in_specs=(
            P("mem", None, "lat", "lon"),
            P(None, "lat", "lon"),
            P(None, "lat", "lon"),
            P(None, "lat", "lon"),
            P("lat", "lon", None),
            P("lat", "lon", None),
            P("lat", "lon", None),
            P("lat", "lon", None),
        ),
        out_specs=P("mem", None, "lat", "lon"),
        check_vma=False,
    )
```

```python
import functools

import jax
import jax.numpy as jnp
from jax import lax
from jax.experimental import pallas as pl
from jax.experimental.pallas import tpu as pltpu
from jax.sharding import PartitionSpec as P

STEPS = 4
LANES = 128
OWNED = 32
GROUPS = LANES // OWNED
ROWS = 4
BATCH = 32
MEMBERS_HERE = 8
LEVELS = 8
NOB = 256
PLANE = LEVELS * ROWS
VALUE_ROW = 11 * PLANE
SITE_ROW = VALUE_ROW + 2
EDGE_ROW = SITE_ROW + 6
EDGE_ROWS = 16
PAYLOAD = EDGE_ROW + EDGE_ROWS
COLS = LEVELS * OWNED
SPREAD_ROWS = 136
FAR = -8192
F32 = jnp.float32
BF16 = jnp.bfloat16
VMEM_LIMIT = 40 * 1024 * 1024
PAYLOAD_LIMIT = 60 * 1024 * 1024


def vmem(count):
    return [pl.BlockSpec(memory_space=pltpu.VMEM)] * count


def params():
    return pltpu.CompilerParams(vmem_limit_bytes=VMEM_LIMIT)


def lane_index():
    return lax.broadcasted_iota(jnp.int32, (8, LANES), 1)


def lat_masks():
    here = lax.axis_index("lat")
    return [scalar_mask(here, 0), scalar_mask(here, 1)]


def lon_parity():
    return lax.rem(lax.axis_index("lon"), 2)


def scalar_mask(value, wanted):
    return jnp.full((8, LANES), value, jnp.int32) == wanted


def roll(x, shift):
    shift %= LANES
    return x if shift == 0 else pltpu.roll(x, shift, 1)


def member_rows(own_ref, other_ref, here, level, row):
    start = level * ROWS + row % ROWS
    own = own_ref[pl.ds(start, 8, stride=PLANE), :]
    other = other_ref[pl.ds(start, 8, stride=PLANE), :]
    return jnp.where(here[row // ROWS], own, other)


def coef_rows(own_ref, other_ref, here, which, row):
    start = (MEMBERS_HERE + which) * PLANE + row % ROWS
    own = own_ref[pl.ds(start, 8, stride=ROWS), :]
    other = other_ref[pl.ds(start, 8, stride=ROWS), :]
    return jnp.where(here[row // ROWS], own, other)


def payload_kernel(
    prior_ref,
    east_ref,
    north_ref,
    spread_ref,
    value_ref,
    site_ref,
    ids_ref,
    weight_ref,
    out_ref,
    first_ref,
    second_ref,
    ids_out,
    weight_out,
    value,
    site,
    sems,
):
    owned = pl.ds(pl.multiple_of(lax.axis_index("mem") * OWNED, OWNED), OWNED)
    moves = [
        (prior_ref, out_ref.at[pl.ds(0, MEMBERS_HERE * PLANE), :]),
        *[
            (ref, out_ref.at[pl.ds((MEMBERS_HERE + n) * PLANE, PLANE), :])
            for n, ref in enumerate((east_ref, north_ref, spread_ref))
        ],
        (value_ref, value),
        (site_ref, site),
        (ids_ref.at[owned, :], ids_out),
        (weight_ref.at[owned, :], weight_out),
    ]
    copies = [pltpu.make_async_copy(src, dst, sems.at[n]) for n, (src, dst) in enumerate(moves)]
    for copy in copies:
        copy.start()
    for copy in copies:
        copy.wait()
    values = value[...]
    sites = site[...].astype(F32)
    rest = jnp.zeros((PAYLOAD - SITE_ROW - 2, LANES), F32)
    pieces = [values[:, :LANES], values[:, LANES:], sites[:, :LANES], sites[:, LANES:], rest]
    out_ref[VALUE_ROW:, :] = jnp.concatenate(pieces, axis=0)
    lane = lane_index()
    even = scalar_mask(lon_parity(), 0)
    for tile in range(2):
        left = jnp.zeros((8, LANES), F32)
        right = jnp.zeros((8, LANES), F32)
        for slot in range(32 if tile == 0 else 12):
            if tile == 0:
                x = out_ref[pl.ds(slot, 8, stride=PLANE), :]
            else:
                x = out_ref[pl.ds((MEMBERS_HERE + slot // 4) * PLANE + slot % 4, 8, stride=ROWS), :]
            place = (lane // 4) == slot
            left = jnp.where(place, roll(x, 4 * slot), left)
            right = jnp.where(place, roll(x, 4 * slot + 4), right)
        first_ref[tile * 8 : tile * 8 + 8, :] = jnp.where(even, right, left)
        second_ref[tile * 8 : tile * 8 + 8, :] = jnp.where(even, left, right)


def advance_in_time(q, coef, level, first_lane, last_lane):
    after = []
    for row in range(8):
        centre, border = q[row]
        rc, rb = roll(centre, 1), roll(border, 1)
        lc, lb = roll(centre, -1), roll(border, -1)
        wests = (jnp.where(first_lane, rb, rc), jnp.where(first_lane, rc, rb))
        easts = (jnp.where(last_lane, lb, lc), jnp.where(last_lane, lc, lb))
        both = []
        for part in range(2):
            c = [coef[row, n, part, level : level + 1, :] for n in range(5)]
            total = c[0] * q[row][part] + c[1] * wests[part] + c[2] * easts[part]
            if row > 0:
                total = total + c[3] * q[row - 1][part]
            if row < 7:
                total = total + c[4] * q[row + 1][part]
            both.append(total)
        after.append(tuple(both))
    return after


def forecast_kernel(
    own_ref, other_ref, corner_ref, second_ref, first_ref, send_ref, values_ref, coef, state
):
    lane = lane_index()
    here = lat_masks()
    even = scalar_mask(lon_parity(), 0)
    first_lane = lane == 0
    last_lane = lane == LANES - 1
    east_lanes = lane < 4
    west_lanes = lane >= LANES - 4
    east, west = {}, {}
    for block in range(2):
        for tile in range(2):
            part = slice(tile * 8, tile * 8 + 8)
            far = slice(EDGE_ROW + tile * 8, EDGE_ROW + tile * 8 + 8)
            a = jnp.where(here[block], first_ref[part, :], other_ref[far, :])
            b = jnp.where(here[block], second_ref[part, :], corner_ref[part, :])
            east[block, tile] = jnp.where(even, a, b)
            west[block, tile] = jnp.where(even, b, a)

    def halo(row, tile, group):
        slot = group * ROWS + row % ROWS
        key = (row // ROWS, tile)
        from_east = roll(east[key], -4 * slot)
        from_west = roll(west[key], LANES - 4 - 4 * slot)
        return jnp.where(east_lanes, from_east, jnp.where(west_lanes, from_west, 0.0))

    for row in range(8):
        for part in range(2):
            if part == 0:
                u, v, d = (coef_rows(own_ref, other_ref, here, q, row) for q in range(3))
            else:
                u, v, d = (halo(row, 1, q) for q in range(3))
            up, un = jnp.maximum(u, 0.0), jnp.minimum(u, 0.0)
            vp, vn = jnp.maximum(v, 0.0), jnp.minimum(v, 0.0)
            coef[row, 0, part] = 1.0 - (up - un) - (vp - vn) - 4.0 * d
            coef[row, 1, part] = up + d
            coef[row, 2, part] = d - un
            coef[row, 3, part] = vp + d
            coef[row, 4, part] = d - vn

    for level in range(0, LEVELS, 2):
        pair = (level, level + 1)
        q = [
            [(member_rows(own_ref, other_ref, here, n, row), halo(row, 0, n)) for row in range(8)]
            for n in pair
        ]
        for _ in range(STEPS):
            q = [advance_in_time(q[n], coef, pair[n], first_lane, last_lane) for n in range(2)]
        for n in range(2):
            for row in range(8):
                state[pair[n], row] = q[n][row][0]

    for block in range(2):
        site_own = jnp.concatenate(
            [own_ref[SITE_ROW : SITE_ROW + 1, :], own_ref[SITE_ROW + 1 : SITE_ROW + 2, :]], axis=1
        )
        site_other = jnp.concatenate(
            [other_ref[SITE_ROW : SITE_ROW + 1, :], other_ref[SITE_ROW + 1 : SITE_ROW + 2, :]], axis=1
        )
        mine = jnp.full((1, NOB), lax.axis_index("lat"), jnp.int32) == block
        site = jnp.where(mine, site_own, site_other).astype(jnp.int32)
        site_row = jnp.broadcast_to(site >> 7, (8, NOB))
        site_lane = jnp.broadcast_to(site & (LANES - 1), (LANES, NOB))
        pick = jnp.where(lax.broadcasted_iota(jnp.int32, (LANES, NOB), 0) == site_lane, 1.0, 0.0).astype(BF16)
        x = state[:, block * ROWS : (block + 1) * ROWS].reshape(PLANE * 8, LANES)
        x1 = x.astype(BF16)
        rest = x - x1.astype(F32)
        x2 = rest.astype(BF16)
        x3 = (rest - x2.astype(F32)).astype(BF16)
        picked = (
            jnp.dot(x3, pick, preferred_element_type=F32)
            + jnp.dot(x2, pick, preferred_element_type=F32)
            + jnp.dot(x1, pick, preferred_element_type=F32)
        )
        total = jnp.zeros((8, NOB), F32)
        for n in range(PLANE):
            total = jnp.where(site_row == n, picked[n * 8 : n * 8 + 8, :], total)
        for target in range(send_ref.shape[0]):
            send_ref[target, :, COLS + block * NOB : COLS + (block + 1) * NOB] = total

    own = jnp.concatenate([own_ref[VALUE_ROW + n : VALUE_ROW + n + 1, :] for n in range(2)], axis=1)
    other = jnp.concatenate([other_ref[VALUE_ROW + n : VALUE_ROW + n + 1, :] for n in range(2)], axis=1)
    south = jnp.full((1, NOB), lax.axis_index("lat"), jnp.int32) == 0
    values = jnp.concatenate([jnp.where(south, own, other), jnp.where(south, other, own)], axis=1)
    values_ref[...] = jnp.broadcast_to(values, (8, 2 * NOB))

    segment = lane // OWNED
    for row in range(ROWS):
        here_row = lax.axis_index("lat") * ROWS + row
        values = [state[level, here_row] for level in range(LEVELS)]
        for group in range(GROUPS):
            for half in range(2):
                total = jnp.zeros((8, LANES), F32)
                for n in range(4):
                    moved = roll(values[half * 4 + n], OWNED * (n - group))
                    total = jnp.where(segment == n, moved, total)
                send_ref[row * GROUPS + group, :, half * LANES : (half + 1) * LANES] = total


def halves(x):
    hi = x.astype(BF16)
    return hi, (x - hi.astype(F32)).astype(BF16)


def left_side(x):
    return jnp.concatenate(halves(x), axis=1)


def product(left, right):
    out = jnp.dot(left, right, preferred_element_type=F32)
    half = out.shape[1] // 2
    return out[:, :half] + out[:, half:]


def small_product(rows, halves_of_right):
    out = jnp.dot(jnp.concatenate(halves(rows), axis=0), halves_of_right, preferred_element_type=F32)
    half = out.shape[1] // 2
    return out[0:16, :half] + (out[0:16, half:] + out[16:32, :half])


def spread_kernel(recv_ref, values_ref, out_ref, near_ref):
    members = recv_ref.shape[0]
    obs = recv_ref[:, COLS:]
    mean = jnp.sum(obs, axis=0, keepdims=True) / members
    pert = obs - mean
    innovation = values_ref[0:1, :] - mean
    out_ref[0:members, :] = pert
    near_ref[0:members, :] = pert
    near_ref[members:, :] = innovation
    row = lax.broadcasted_iota(jnp.int32, (8, 2 * NOB), 0)
    out_ref[members:, :] = jnp.where(row == 0, innovation, 0.0)


def fill_table(table, start, spread_ref):
    width = pl.ds(start, 2 * NOB)
    hi, lo = halves(spread_ref[0:128, :])
    table[0:128, width] = hi
    table[128:256, width] = lo
    innovation = spread_ref[128:129, :]
    first_term = innovation.astype(BF16).astype(F32)
    row = lax.broadcasted_iota(jnp.int32, (16, 2 * NOB), 0)
    extra = jnp.where(row == 0, first_term, jnp.where(row == 1, innovation - first_term, 0.0))
    table[256:272, width] = extra.astype(BF16)


def local_places(ids):
    code = ids >> 8
    lat_step = jnp.where(code >= 6, 2, jnp.where(code >= 3, 1, 0))
    lon_step = code - 3 * lat_step
    odd = jnp.full(ids.shape, lon_parity(), jnp.int32) == 1
    slot = jnp.where(odd, 2 - lon_step, lon_step)
    within = (lat_step - 1 + lax.axis_index("lat")) * NOB + (ids & (NOB - 1))
    near = jnp.where(slot == 0, FAR, within + jnp.where(slot == 2, 2 * NOB, 0))
    far = jnp.where(slot == 0, within, FAR)
    return near.astype(F32), far.astype(F32)


def own_kernel(payload_ref, ids_ref, weight_ref, own_ref, near_ref, far_ref, weight_out):
    own_ref[...] = payload_ref[0:EDGE_ROW, :]
    weight_out[...] = weight_ref[...]
    near_ref[...], far_ref[...] = local_places(ids_ref[...])


def gather_pair(table, places, first_column, blocks):
    place = lax.broadcasted_iota(jnp.int32, (NOB, LANES), 0).astype(F32).astype(BF16)
    one, zero = jnp.ones((), BF16), jnp.zeros((), BF16)
    hot = []
    for block in range(blocks):
        sides = []
        for k in range(2):
            row = places[pl.ds(first_column + k, 1), :] - float(block * NOB)
            sides.append(jnp.where(row.astype(BF16) == place, one, zero))
        hot.append(jnp.concatenate(sides, axis=1))
    both = jnp.dot(table[...], jnp.concatenate(hot, axis=0), preferred_element_type=F32)
    rows = both[0:128] + both[128:256]
    innov = both[256:257] + both[257:258]
    found = jnp.concatenate([rows, jnp.broadcast_to(innov, (8, 2 * LANES))], axis=0)
    return found[:, :LANES], found[:, LANES:]


def near_kernel(
    recv_ref, places, mine_ref, first_ref, part_ref, dev_ref, centre_ref, table
):
    members = recv_ref.shape[0]
    fill_table(table, 0, mine_ref)
    fill_table(table, 2 * NOB, first_ref)
    traces = jnp.transpose(recv_ref[:, :COLS])
    centre = jnp.sum(traces, axis=1, keepdims=True) / members
    dev_ref[...] = traces - centre
    centre_ref[...] = jnp.broadcast_to(centre, traces.shape)

    def turn(n, carry):
        for pair in range(BATCH // 2):
            c = n * BATCH + pair * 2
            left, right = gather_pair(table, places, c, 4)
            part_ref[c] = left
            part_ref[c + 1] = right
        return carry

    lax.fori_loop(0, OWNED // BATCH, turn, 0)


def columns_kernel(
    places,
    weight_ref,
    second_ref,
    part_ref,
    dev_ref,
    centre_ref,
    out_ref,
    table,
    res,
    eyes,
    found,
    full,
    half_s,
    half_u,
    half_z,
    drives,
):
    members = 128
    scale = members - 1.0
    fill_table(table, 0, second_ref)
    i0 = lax.broadcasted_iota(jnp.int32, (members, members), 0)
    i1 = lax.broadcasted_iota(jnp.int32, (members, members), 1)
    for n, value in enumerate((scale, 0.84375, 1.5380859375)):
        eyes[n] = jnp.where(i0 == i1, value, 0.0).astype(F32)

    def put(ref, b, x):
        hi, lo = halves(x)
        ref[b, :, 0:members] = hi
        ref[b, :, members:] = lo

    def right_of(ref, b):
        top = ref[b]
        low = jnp.concatenate([ref[b, :, 0:members], jnp.zeros((members, members), BF16)], axis=1)
        return jnp.concatenate([top, low], axis=0)

    def turn(n, carry):
        base = n * BATCH
        slots = range(BATCH)
        invs = []
        for pair in range(BATCH // 2):
            for k, extra in enumerate(gather_pair(table, places, base + pair * 2, 2)):
                found[pair * 2 + k] = extra + part_ref[base + pair * 2 + k]
        for b in slots:
            pert = found[b, 0:members]
            innov = found[b, members : members + 1]
            w = weight_ref[pl.ds(base + b, 1), :]
            left = jnp.concatenate([pert * w, jnp.broadcast_to(w * innov, (16, LANES))], axis=0)
            e_hi, e_lo = halves(jnp.transpose(pert))
            right = jnp.concatenate(
                [
                    jnp.concatenate([e_hi, e_lo], axis=1),
                    jnp.concatenate([e_hi, jnp.zeros_like(e_hi)], axis=1),
                ],
                axis=0,
            )
            both = product(left_side(left), right)
            gram = both[:members]
            drives[b] = both[members : members + 8]
            norm = jnp.sum(jnp.sum(gram * gram, axis=0, keepdims=True), axis=1, keepdims=True)
            inv = 1.0 / (scale + jnp.sqrt(norm))
            invs.append(inv)
            s = (eyes[0] + gram) * inv
            full[b] = s
            put(half_s, b, s)
        for b in slots:
            square = product(half_s[b], right_of(half_s, b))
            put(half_u, b, 0.25 * square - 1.125 * full[b] + eyes[1])
        for b in slots:
            square = product(half_u[b], right_of(half_u, b))
            put(half_z, b, square - 0.5390625 * full[b] + eyes[2])
        rows = []
        for b in slots:
            x = jnp.concatenate([dev_ref[pl.ds(base + b, 8, stride=OWNED), :], drives[b]], axis=0)
            both = product(jnp.concatenate([half_s[b], left_side(x)], axis=0), right_of(half_z, b))
            put(half_u, b, both[0:members])
            rows.append(both[members:])
        for b in slots:
            put(half_s, b, product(half_u[b], right_of(half_z, b)))
        moved = [0.0625 * x for x in rows]
        for coefficient in (-0.5625, 1.6875, -2.4375, 2.25):
            moved = [coefficient * rows[b] + small_product(moved[b], half_s[b]) for b in slots]
        for b in slots:
            y = moved[b][0:8]
            shift = jnp.sum(y * moved[b][8:16], axis=1, keepdims=True) * invs[b]
            res[pl.ds(base + b, 8, stride=OWNED), :] = jnp.sqrt(scale * invs[b]) * y + shift
        return carry

    lax.fori_loop(0, OWNED // BATCH, turn, 0)
    out_ref[...] = jnp.transpose(res[...] + centre_ref[...])


def unpack_kernel(recv_ref, out_ref):
    segment = lane_index() // OWNED
    for row in range(ROWS):
        for half in range(2):
            parts = [
                recv_ref[row * GROUPS + g, :, half * LANES : (half + 1) * LANES] for g in range(GROUPS)
            ]
            for n in range(4):
                level = half * 4 + n
                total = jnp.zeros((8, LANES), F32)
                for g in range(GROUPS):
                    total = jnp.where(segment == g, roll(parts[g], OWNED * (g - n)), total)
                out_ref[pl.ds(level * ROWS + row, 8, stride=PLANE), :] = total


def call(kernel, shapes, operands, scratch=(), flops=None):
    single = not isinstance(shapes, list)
    cost = None
    if flops is not None:
        cost = pl.CostEstimate(flops=flops, bytes_accessed=1 << 22, transcendentals=0)
    return pl.pallas_call(
        kernel,
        out_shape=shapes,
        in_specs=vmem(len(operands)),
        out_specs=vmem(1)[0] if single else vmem(len(shapes)),
        scratch_shapes=list(scratch),
        compiler_params=params(),
        cost_estimate=cost,
    )(*operands)


def per_device(
    prior_sample_set,
    eastward_cfl_number,
    northward_cfl_number,
    spreading_number,
    obs_value,
    obs_site,
    neighbours,
    loc_weight,
):
    sds = functools.partial(jax.ShapeDtypeStruct, dtype=F32)
    mems = lax.axis_size("mem")
    lons = lax.axis_size("lon")
    on_chip = [(i, i ^ 1) for i in range(lons)]
    whole = 2 * lons
    off_chip, corners = [], []
    for i in range(whole):
        j = (i + 1 if i % 2 else i - 1) % whole
        off_chip.append((i % lons * 2 + i // lons, j % lons * 2 + j // lons))
        corners.append((i % lons * 2 + i // lons, j % lons * 2 + 1 - i // lons))
    off_lon = [(i, (i + 1 if i % 2 else i - 1) % lons) for i in range(lons)]

    edge = sds((EDGE_ROWS, LANES))
    payload, first, second, near_ids, weight = pl.pallas_call(
        payload_kernel,
        out_shape=[
            sds((PAYLOAD, LANES)),
            edge,
            edge,
            jax.ShapeDtypeStruct((OWNED, LANES), jnp.int32),
            sds((OWNED, LANES)),
        ],
        in_specs=[pl.BlockSpec(memory_space=pltpu.HBM)] * 8,
        out_specs=vmem(5),
        scratch_shapes=[
            pltpu.VMEM((1, NOB), F32),
            pltpu.VMEM((1, NOB), jnp.int32),
            pltpu.SemaphoreType.DMA((8,)),
        ],
        compiler_params=pltpu.CompilerParams(vmem_limit_bytes=PAYLOAD_LIMIT),
    )(
        prior_sample_set.reshape(MEMBERS_HERE * PLANE, LANES),
        eastward_cfl_number.reshape(PLANE, LANES),
        northward_cfl_number.reshape(PLANE, LANES),
        spreading_number.reshape(PLANE, LANES),
        obs_value.reshape(1, NOB),
        obs_site.reshape(1, NOB),
        neighbours.reshape(ROWS * LANES, LANES),
        loc_weight.reshape(ROWS * LANES, LANES),
    )
    first_in = lax.ppermute(first, "lon", on_chip)
    payload = lax.dynamic_update_slice(payload, first_in, (EDGE_ROW, 0))
    payload, second = lax.optimization_barrier((payload, second))
    other = lax.ppermute(payload, "lat", [(0, 1), (1, 0)])
    own, near, far, weight = call(
        own_kernel,
        [sds((EDGE_ROW, LANES))] + [sds((OWNED, LANES))] * 3,
        (payload, near_ids, weight),
        flops=1 << 20,
    )
    corner_in = lax.ppermute(second, ("lon", "lat"), corners)
    second_in = lax.ppermute(second, "lon", off_lon)
    send, values = call(
        forecast_kernel,
        [sds((mems, MEMBERS_HERE, COLS + 2 * NOB)), sds((8, 2 * NOB))],
        (own, other, corner_in, second_in, first_in),
        [pltpu.VMEM((8, 5, 2, 8, LANES), F32), pltpu.VMEM((LEVELS, 8, 8, LANES), F32)],
    )
    members = mems * MEMBERS_HERE
    got = lax.all_to_all(
        send.reshape(members, send.shape[2]), "mem", split_axis=0, concat_axis=0, tiled=True
    )
    spread, spread_near = call(
        spread_kernel,
        [sds((SPREAD_ROWS, 2 * NOB)), sds((members + 1, 2 * NOB))],
        (got, values),
    )
    spread_second = lax.ppermute(spread, ("lon", "lat"), off_chip)
    spread_first = lax.ppermute(spread_near, "lon", on_chip)
    part, dev, centre = call(
        near_kernel,
        [sds((OWNED, SPREAD_ROWS, LANES)), sds((COLS, members)), sds((COLS, members))],
        (got, near, spread, spread_first),
        [pltpu.VMEM((272, 4 * NOB), BF16)],
    )
    updated = call(
        columns_kernel,
        sds((members, COLS)),
        (far, weight, spread_second, part, dev, centre),
        [
            pltpu.VMEM((272, 2 * NOB), BF16),
            pltpu.VMEM((COLS, members), F32),
            pltpu.VMEM((3, members, members), F32),
            pltpu.VMEM((BATCH, SPREAD_ROWS, LANES), F32),
            pltpu.VMEM((BATCH, members, members), F32),
            *[pltpu.VMEM((BATCH, members, 2 * members), BF16)] * 3,
            pltpu.VMEM((BATCH, 8, members), F32),
        ],
        flops=2 * OWNED * 7 * members * 4 * members * members,
    )
    back = lax.all_to_all(updated, "mem", split_axis=0, concat_axis=0, tiled=True)
    result = call(
        unpack_kernel,
        sds((MEMBERS_HERE * PLANE, LANES)),
        (back.reshape(mems, MEMBERS_HERE, COLS),),
    )
    return result.reshape(prior_sample_set.shape)


def solution(mesh):
    return jax.shard_map(
        per_device,
        mesh=mesh,
        in_specs=(
            P("mem", None, "lat", "lon"),
            P(None, "lat", "lon"),
            P(None, "lat", "lon"),
            P(None, "lat", "lon"),
            P("lat", "lon", None),
            P("lat", "lon", None),
            P("lat", "lon", None),
            P("lat", "lon", None),
        ),
        out_specs=P("mem", None, "lat", "lon"),
        check_vma=False,
    )
```

```python
import functools

import jax
import jax.numpy as jnp
from jax import lax
from jax.experimental import pallas as pl
from jax.experimental.pallas import tpu as pltpu
from jax.sharding import PartitionSpec as P

STEPS = 4
LANES = 128
OWNED = 32
GROUPS = LANES // OWNED
ROWS = 4
BATCH = 32
MEMBERS_HERE = 8
LEVELS = 8
NOB = 256
PLANE = LEVELS * ROWS
VALUE_ROW = 11 * PLANE
SITE_ROW = VALUE_ROW + 2
PAYLOAD = SITE_ROW + 6
EDGE_ROWS = 16
COLS = LEVELS * OWNED
SPREAD_ROWS = 136
FAR = -8192
F32 = jnp.float32
BF16 = jnp.bfloat16
VMEM_LIMIT = 40 * 1024 * 1024
PAYLOAD_LIMIT = 60 * 1024 * 1024


def vmem(count):
    return [pl.BlockSpec(memory_space=pltpu.VMEM)] * count


def params():
    return pltpu.CompilerParams(vmem_limit_bytes=VMEM_LIMIT)


def lane_index():
    return lax.broadcasted_iota(jnp.int32, (8, LANES), 1)


def lat_masks():
    here = lax.axis_index("lat")
    return [scalar_mask(here, 0), scalar_mask(here, 1)]


def lon_parity():
    return lax.rem(lax.axis_index("lon"), 2)


def scalar_mask(value, wanted):
    return jnp.full((8, LANES), value, jnp.int32) == wanted


def roll(x, shift):
    shift %= LANES
    return x if shift == 0 else pltpu.roll(x, shift, 1)


def member_rows(own_ref, other_ref, here, level, row):
    start = level * ROWS + row % ROWS
    own = own_ref[pl.ds(start, 8, stride=PLANE), :]
    other = other_ref[pl.ds(start, 8, stride=PLANE), :]
    return jnp.where(here[row // ROWS], own, other)


def coef_rows(own_ref, other_ref, here, which, row):
    start = (MEMBERS_HERE + which) * PLANE + row % ROWS
    own = own_ref[pl.ds(start, 8, stride=ROWS), :]
    other = other_ref[pl.ds(start, 8, stride=ROWS), :]
    return jnp.where(here[row // ROWS], own, other)


def payload_kernel(
    prior_ref,
    east_ref,
    north_ref,
    spread_ref,
    value_ref,
    site_ref,
    ids_ref,
    weight_ref,
    out_ref,
    first_ref,
    second_ref,
    ids_out,
    weight_out,
    value,
    site,
    sems,
):
    owned = pl.ds(pl.multiple_of(lax.axis_index("mem") * OWNED, OWNED), OWNED)
    moves = [
        (prior_ref, out_ref.at[pl.ds(0, MEMBERS_HERE * PLANE), :]),
        *[
            (ref, out_ref.at[pl.ds((MEMBERS_HERE + n) * PLANE, PLANE), :])
            for n, ref in enumerate((east_ref, north_ref, spread_ref))
        ],
        (value_ref, value),
        (site_ref, site),
        (ids_ref.at[owned, :], ids_out),
        (weight_ref.at[owned, :], weight_out),
    ]
    copies = [pltpu.make_async_copy(src, dst, sems.at[n]) for n, (src, dst) in enumerate(moves)]
    for copy in copies:
        copy.start()
    for copy in copies:
        copy.wait()
    values = value[...]
    sites = site[...].astype(F32)
    rest = jnp.zeros((PAYLOAD - SITE_ROW - 2, LANES), F32)
    pieces = [values[:, :LANES], values[:, LANES:], sites[:, :LANES], sites[:, LANES:], rest]
    out_ref[VALUE_ROW:, :] = jnp.concatenate(pieces, axis=0)
    lane = lane_index()
    even = scalar_mask(lon_parity(), 0)
    for tile in range(2):
        left = jnp.zeros((8, LANES), F32)
        right = jnp.zeros((8, LANES), F32)
        for slot in range(32 if tile == 0 else 12):
            if tile == 0:
                x = out_ref[pl.ds(slot, 8, stride=PLANE), :]
            else:
                x = out_ref[pl.ds((MEMBERS_HERE + slot // 4) * PLANE + slot % 4, 8, stride=ROWS), :]
            place = (lane // 4) == slot
            left = jnp.where(place, roll(x, 4 * slot), left)
            right = jnp.where(place, roll(x, 4 * slot + 4), right)
        first_ref[tile * 8 : tile * 8 + 8, :] = jnp.where(even, right, left)
        second_ref[tile * 8 : tile * 8 + 8, :] = jnp.where(even, left, right)


def advance_in_time(q, coef, level, first_lane, last_lane):
    after = []
    for row in range(8):
        centre, border = q[row]
        rc, rb = roll(centre, 1), roll(border, 1)
        lc, lb = roll(centre, -1), roll(border, -1)
        wests = (jnp.where(first_lane, rb, rc), jnp.where(first_lane, rc, rb))
        easts = (jnp.where(last_lane, lb, lc), jnp.where(last_lane, lc, lb))
        both = []
        for part in range(2):
            c = [coef[row, n, part, level : level + 1, :] for n in range(5)]
            total = c[0] * q[row][part] + c[1] * wests[part] + c[2] * easts[part]
            if row > 0:
                total = total + c[3] * q[row - 1][part]
            if row < 7:
                total = total + c[4] * q[row + 1][part]
            both.append(total)
        after.append(tuple(both))
    return after


def forecast_kernel(
    own_ref,
    other_ref,
    first_other_ref,
    second_other_ref,
    second_ref,
    first_ref,
    send_ref,
    values_ref,
    coef,
    state,
):
    lane = lane_index()
    here = lat_masks()
    even = scalar_mask(lon_parity(), 0)
    first_lane = lane == 0
    last_lane = lane == LANES - 1
    east_lanes = lane < 4
    west_lanes = lane >= LANES - 4
    east, west = {}, {}
    for block in range(2):
        for tile in range(2):
            part = slice(tile * 8, tile * 8 + 8)
            a = jnp.where(here[block], first_ref[part, :], first_other_ref[part, :])
            b = jnp.where(here[block], second_ref[part, :], second_other_ref[part, :])
            east[block, tile] = jnp.where(even, a, b)
            west[block, tile] = jnp.where(even, b, a)

    def halo(row, tile, group):
        slot = group * ROWS + row % ROWS
        key = (row // ROWS, tile)
        from_east = roll(east[key], -4 * slot)
        from_west = roll(west[key], LANES - 4 - 4 * slot)
        return jnp.where(east_lanes, from_east, jnp.where(west_lanes, from_west, 0.0))

    for row in range(8):
        for part in range(2):
            if part == 0:
                u, v, d = (coef_rows(own_ref, other_ref, here, q, row) for q in range(3))
            else:
                u, v, d = (halo(row, 1, q) for q in range(3))
            up, un = jnp.maximum(u, 0.0), jnp.minimum(u, 0.0)
            vp, vn = jnp.maximum(v, 0.0), jnp.minimum(v, 0.0)
            coef[row, 0, part] = 1.0 - (up - un) - (vp - vn) - 4.0 * d
            coef[row, 1, part] = up + d
            coef[row, 2, part] = d - un
            coef[row, 3, part] = vp + d
            coef[row, 4, part] = d - vn

    for level in range(0, LEVELS, 2):
        pair = (level, level + 1)
        q = [
            [(member_rows(own_ref, other_ref, here, n, row), halo(row, 0, n)) for row in range(8)]
            for n in pair
        ]
        for _ in range(STEPS):
            q = [advance_in_time(q[n], coef, pair[n], first_lane, last_lane) for n in range(2)]
        for n in range(2):
            for row in range(8):
                state[pair[n], row] = q[n][row][0]

    for block in range(2):
        site_own = jnp.concatenate(
            [own_ref[SITE_ROW : SITE_ROW + 1, :], own_ref[SITE_ROW + 1 : SITE_ROW + 2, :]], axis=1
        )
        site_other = jnp.concatenate(
            [other_ref[SITE_ROW : SITE_ROW + 1, :], other_ref[SITE_ROW + 1 : SITE_ROW + 2, :]], axis=1
        )
        mine = jnp.full((1, NOB), lax.axis_index("lat"), jnp.int32) == block
        site = jnp.where(mine, site_own, site_other).astype(jnp.int32)
        site_row = jnp.broadcast_to(site >> 7, (8, NOB))
        site_lane = jnp.broadcast_to(site & (LANES - 1), (LANES, NOB))
        pick = jnp.where(lax.broadcasted_iota(jnp.int32, (LANES, NOB), 0) == site_lane, 1.0, 0.0).astype(BF16)
        x = state[:, block * ROWS : (block + 1) * ROWS].reshape(PLANE * 8, LANES)
        x1 = x.astype(BF16)
        rest = x - x1.astype(F32)
        x2 = rest.astype(BF16)
        x3 = (rest - x2.astype(F32)).astype(BF16)
        picked = (
            jnp.dot(x3, pick, preferred_element_type=F32)
            + jnp.dot(x2, pick, preferred_element_type=F32)
            + jnp.dot(x1, pick, preferred_element_type=F32)
        )
        total = jnp.zeros((8, NOB), F32)
        for n in range(PLANE):
            total = jnp.where(site_row == n, picked[n * 8 : n * 8 + 8, :], total)
        for target in range(send_ref.shape[0]):
            send_ref[target, :, COLS + block * NOB : COLS + (block + 1) * NOB] = total

    own = jnp.concatenate([own_ref[VALUE_ROW + n : VALUE_ROW + n + 1, :] for n in range(2)], axis=1)
    other = jnp.concatenate([other_ref[VALUE_ROW + n : VALUE_ROW + n + 1, :] for n in range(2)], axis=1)
    south = jnp.full((1, NOB), lax.axis_index("lat"), jnp.int32) == 0
    values = jnp.concatenate([jnp.where(south, own, other), jnp.where(south, other, own)], axis=1)
    values_ref[...] = jnp.broadcast_to(values, (8, 2 * NOB))

    segment = lane // OWNED
    for row in range(ROWS):
        here_row = lax.axis_index("lat") * ROWS + row
        values = [state[level, here_row] for level in range(LEVELS)]
        for group in range(GROUPS):
            for half in range(2):
                total = jnp.zeros((8, LANES), F32)
                for n in range(4):
                    moved = roll(values[half * 4 + n], OWNED * (n - group))
                    total = jnp.where(segment == n, moved, total)
                send_ref[row * GROUPS + group, :, half * LANES : (half + 1) * LANES] = total


def halves(x):
    hi = x.astype(BF16)
    return hi, (x - hi.astype(F32)).astype(BF16)


def left_side(x):
    return jnp.concatenate(halves(x), axis=1)


def product(left, right):
    out = jnp.dot(left, right, preferred_element_type=F32)
    half = out.shape[1] // 2
    return out[:, :half] + out[:, half:]


def small_product(rows, halves_of_right):
    out = jnp.dot(jnp.concatenate(halves(rows), axis=0), halves_of_right, preferred_element_type=F32)
    half = out.shape[1] // 2
    return out[0:16, :half] + (out[0:16, half:] + out[16:32, :half])


def spread_kernel(recv_ref, values_ref, out_ref, near_ref):
    members = recv_ref.shape[0]
    obs = recv_ref[:, COLS:]
    mean = jnp.sum(obs, axis=0, keepdims=True) / members
    pert = obs - mean
    innovation = values_ref[0:1, :] - mean
    out_ref[0:members, :] = pert
    near_ref[0:members, :] = pert
    near_ref[members:, :] = innovation
    row = lax.broadcasted_iota(jnp.int32, (8, 2 * NOB), 0)
    out_ref[members:, :] = jnp.where(row == 0, innovation, 0.0)


def fill_table(table, start, spread_ref):
    width = pl.ds(start, 2 * NOB)
    hi, lo = halves(spread_ref[0:128, :])
    table[0:128, width] = hi
    table[128:256, width] = lo
    innovation = spread_ref[128:129, :]
    first_term = innovation.astype(BF16).astype(F32)
    row = lax.broadcasted_iota(jnp.int32, (16, 2 * NOB), 0)
    extra = jnp.where(row == 0, first_term, jnp.where(row == 1, innovation - first_term, 0.0))
    table[256:272, width] = extra.astype(BF16)


def local_places(ids):
    code = ids >> 8
    lat_step = jnp.where(code >= 6, 2, jnp.where(code >= 3, 1, 0))
    lon_step = code - 3 * lat_step
    odd = jnp.full(ids.shape, lon_parity(), jnp.int32) == 1
    slot = jnp.where(odd, 2 - lon_step, lon_step)
    within = (lat_step - 1 + lax.axis_index("lat")) * NOB + (ids & (NOB - 1))
    near = jnp.where(slot == 0, FAR, within + jnp.where(slot == 2, 2 * NOB, 0))
    far = jnp.where(slot == 0, within, FAR)
    return near.astype(F32), far.astype(F32)


def own_kernel(payload_ref, ids_ref, weight_ref, own_ref, near_ref, far_ref, weight_out):
    own_ref[...] = payload_ref[...]
    weight_out[...] = weight_ref[...]
    near_ref[...], far_ref[...] = local_places(ids_ref[...])


def gather_pair(table, places, first_column, blocks):
    place = lax.broadcasted_iota(jnp.int32, (NOB, LANES), 0).astype(F32).astype(BF16)
    one, zero = jnp.ones((), BF16), jnp.zeros((), BF16)
    hot = []
    for block in range(blocks):
        sides = []
        for k in range(2):
            row = places[pl.ds(first_column + k, 1), :] - float(block * NOB)
            sides.append(jnp.where(row.astype(BF16) == place, one, zero))
        hot.append(jnp.concatenate(sides, axis=1))
    both = jnp.dot(table[...], jnp.concatenate(hot, axis=0), preferred_element_type=F32)
    rows = both[0:128] + both[128:256]
    innov = both[256:257] + both[257:258]
    found = jnp.concatenate([rows, jnp.broadcast_to(innov, (8, 2 * LANES))], axis=0)
    return found[:, :LANES], found[:, LANES:]


def near_kernel(
    recv_ref, places, mine_ref, first_ref, part_ref, dev_ref, centre_ref, table
):
    members = recv_ref.shape[0]
    fill_table(table, 0, mine_ref)
    fill_table(table, 2 * NOB, first_ref)
    traces = jnp.transpose(recv_ref[:, :COLS])
    centre = jnp.sum(traces, axis=1, keepdims=True) / members
    dev_ref[...] = traces - centre
    centre_ref[...] = jnp.broadcast_to(centre, traces.shape)

    def turn(n, carry):
        for pair in range(BATCH // 2):
            c = n * BATCH + pair * 2
            left, right = gather_pair(table, places, c, 4)
            part_ref[c] = left
            part_ref[c + 1] = right
        return carry

    lax.fori_loop(0, OWNED // BATCH, turn, 0)


def columns_kernel(
    places,
    weight_ref,
    second_ref,
    part_ref,
    dev_ref,
    centre_ref,
    out_ref,
    table,
    res,
    eyes,
    found,
    full,
    half_s,
    half_u,
    half_z,
    drives,
):
    members = 128
    scale = members - 1.0
    fill_table(table, 0, second_ref)
    i0 = lax.broadcasted_iota(jnp.int32, (members, members), 0)
    i1 = lax.broadcasted_iota(jnp.int32, (members, members), 1)
    for n, value in enumerate((scale, 0.84375, 1.5380859375)):
        eyes[n] = jnp.where(i0 == i1, value, 0.0).astype(F32)

    def put(ref, b, x):
        hi, lo = halves(x)
        ref[b, :, 0:members] = hi
        ref[b, :, members:] = lo

    def right_of(ref, b):
        top = ref[b]
        low = jnp.concatenate([ref[b, :, 0:members], jnp.zeros((members, members), BF16)], axis=1)
        return jnp.concatenate([top, low], axis=0)

    def turn(n, carry):
        base = n * BATCH
        slots = range(BATCH)
        invs = []
        for pair in range(BATCH // 2):
            for k, extra in enumerate(gather_pair(table, places, base + pair * 2, 2)):
                found[pair * 2 + k] = extra + part_ref[base + pair * 2 + k]
        for b in slots:
            pert = found[b, 0:members]
            innov = found[b, members : members + 1]
            w = weight_ref[pl.ds(base + b, 1), :]
            left = jnp.concatenate([pert * w, jnp.broadcast_to(w * innov, (16, LANES))], axis=0)
            e_hi, e_lo = halves(jnp.transpose(pert))
            right = jnp.concatenate(
                [
                    jnp.concatenate([e_hi, e_lo], axis=1),
                    jnp.concatenate([e_hi, jnp.zeros_like(e_hi)], axis=1),
                ],
                axis=0,
            )
            both = product(left_side(left), right)
            gram = both[:members]
            drives[b] = both[members : members + 8]
            norm = jnp.sum(jnp.sum(gram * gram, axis=0, keepdims=True), axis=1, keepdims=True)
            inv = 1.0 / (scale + jnp.sqrt(norm))
            invs.append(inv)
            s = (eyes[0] + gram) * inv
            full[b] = s
            put(half_s, b, s)
        for b in slots:
            square = product(half_s[b], right_of(half_s, b))
            put(half_u, b, 0.25 * square - 1.125 * full[b] + eyes[1])
        for b in slots:
            square = product(half_u[b], right_of(half_u, b))
            put(half_z, b, square - 0.5390625 * full[b] + eyes[2])
        rows = []
        for b in slots:
            x = jnp.concatenate([dev_ref[pl.ds(base + b, 8, stride=OWNED), :], drives[b]], axis=0)
            both = product(jnp.concatenate([half_s[b], left_side(x)], axis=0), right_of(half_z, b))
            put(half_u, b, both[0:members])
            rows.append(both[members:])
        for b in slots:
            put(half_s, b, product(half_u[b], right_of(half_z, b)))
        moved = [0.0625 * x for x in rows]
        for coefficient in (-0.5625, 1.6875, -2.4375, 2.25):
            moved = [coefficient * rows[b] + small_product(moved[b], half_s[b]) for b in slots]
        for b in slots:
            y = moved[b][0:8]
            shift = jnp.sum(y * moved[b][8:16], axis=1, keepdims=True) * invs[b]
            res[pl.ds(base + b, 8, stride=OWNED), :] = jnp.sqrt(scale * invs[b]) * y + shift
        return carry

    lax.fori_loop(0, OWNED // BATCH, turn, 0)
    out_ref[...] = jnp.transpose(res[...] + centre_ref[...])


def unpack_kernel(recv_ref, out_ref):
    segment = lane_index() // OWNED
    for row in range(ROWS):
        for half in range(2):
            parts = [
                recv_ref[row * GROUPS + g, :, half * LANES : (half + 1) * LANES] for g in range(GROUPS)
            ]
            for n in range(4):
                level = half * 4 + n
                total = jnp.zeros((8, LANES), F32)
                for g in range(GROUPS):
                    total = jnp.where(segment == g, roll(parts[g], OWNED * (g - n)), total)
                out_ref[pl.ds(level * ROWS + row, 8, stride=PLANE), :] = total


def call(kernel, shapes, operands, scratch=(), flops=None):
    single = not isinstance(shapes, list)
    cost = None
    if flops is not None:
        cost = pl.CostEstimate(flops=flops, bytes_accessed=1 << 22, transcendentals=0)
    return pl.pallas_call(
        kernel,
        out_shape=shapes,
        in_specs=vmem(len(operands)),
        out_specs=vmem(1)[0] if single else vmem(len(shapes)),
        scratch_shapes=list(scratch),
        compiler_params=params(),
        cost_estimate=cost,
    )(*operands)


def per_device(
    prior_sample_set,
    eastward_cfl_number,
    northward_cfl_number,
    spreading_number,
    obs_value,
    obs_site,
    neighbours,
    loc_weight,
):
    sds = functools.partial(jax.ShapeDtypeStruct, dtype=F32)
    mems = lax.axis_size("mem")
    lons = lax.axis_size("lon")
    on_chip = [(i, i ^ 1) for i in range(lons)]
    whole = 2 * lons
    off_chip, corners, chip_corners = [], [], []
    for i in range(whole):
        j = (i + 1 if i % 2 else i - 1) % whole
        off_chip.append((i % lons * 2 + i // lons, j % lons * 2 + j // lons))
        corners.append((i % lons * 2 + i // lons, j % lons * 2 + 1 - i // lons))
        chip_corners.append((i % lons * 2 + i // lons, (i % lons ^ 1) * 2 + 1 - i // lons))
    off_lon = [(i, (i + 1 if i % 2 else i - 1) % lons) for i in range(lons)]

    edge = sds((EDGE_ROWS, LANES))
    payload, first, second, near_ids, weight = pl.pallas_call(
        payload_kernel,
        out_shape=[
            sds((PAYLOAD, LANES)),
            edge,
            edge,
            jax.ShapeDtypeStruct((OWNED, LANES), jnp.int32),
            sds((OWNED, LANES)),
        ],
        in_specs=[pl.BlockSpec(memory_space=pltpu.HBM)] * 8,
        out_specs=vmem(5),
        scratch_shapes=[
            pltpu.VMEM((1, NOB), F32),
            pltpu.VMEM((1, NOB), jnp.int32),
            pltpu.SemaphoreType.DMA((8,)),
        ],
        compiler_params=pltpu.CompilerParams(vmem_limit_bytes=PAYLOAD_LIMIT),
    )(
        prior_sample_set.reshape(MEMBERS_HERE * PLANE, LANES),
        eastward_cfl_number.reshape(PLANE, LANES),
        northward_cfl_number.reshape(PLANE, LANES),
        spreading_number.reshape(PLANE, LANES),
        obs_value.reshape(1, NOB),
        obs_site.reshape(1, NOB),
        neighbours.reshape(ROWS * LANES, LANES),
        loc_weight.reshape(ROWS * LANES, LANES),
    )
    other = lax.ppermute(payload, "lat", [(0, 1), (1, 0)])
    first_other = lax.ppermute(first, ("lon", "lat"), chip_corners)
    second_other = lax.ppermute(second, ("lon", "lat"), corners)
    second_in = lax.ppermute(second, "lon", off_lon)
    first_in = lax.ppermute(first, "lon", on_chip)
    own, near, far, weight = call(
        own_kernel,
        [sds((PAYLOAD, LANES))] + [sds((OWNED, LANES))] * 3,
        (payload, near_ids, weight),
        flops=1 << 20,
    )
    send, values = call(
        forecast_kernel,
        [sds((mems, MEMBERS_HERE, COLS + 2 * NOB)), sds((8, 2 * NOB))],
        (own, other, first_other, second_other, second_in, first_in),
        [pltpu.VMEM((8, 5, 2, 8, LANES), F32), pltpu.VMEM((LEVELS, 8, 8, LANES), F32)],
    )
    members = mems * MEMBERS_HERE
    got = lax.all_to_all(
        send.reshape(members, send.shape[2]), "mem", split_axis=0, concat_axis=0, tiled=True
    )
    spread, spread_near = call(
        spread_kernel,
        [sds((SPREAD_ROWS, 2 * NOB)), sds((members + 1, 2 * NOB))],
        (got, values),
    )
    spread_second = lax.ppermute(spread, ("lon", "lat"), off_chip)
    spread_first = lax.ppermute(spread_near, "lon", on_chip)
    part, dev, centre = call(
        near_kernel,
        [sds((OWNED, SPREAD_ROWS, LANES)), sds((COLS, members)), sds((COLS, members))],
        (got, near, spread, spread_first),
        [pltpu.VMEM((272, 4 * NOB), BF16)],
    )
    updated = call(
        columns_kernel,
        sds((members, COLS)),
        (far, weight, spread_second, part, dev, centre),
        [
            pltpu.VMEM((272, 2 * NOB), BF16),
            pltpu.VMEM((COLS, members), F32),
            pltpu.VMEM((3, members, members), F32),
            pltpu.VMEM((BATCH, SPREAD_ROWS, LANES), F32),
            pltpu.VMEM((BATCH, members, members), F32),
            *[pltpu.VMEM((BATCH, members, 2 * members), BF16)] * 3,
            pltpu.VMEM((BATCH, 8, members), F32),
        ],
        flops=2 * OWNED * 7 * members * 4 * members * members,
    )
    back = lax.all_to_all(updated, "mem", split_axis=0, concat_axis=0, tiled=True)
    result = call(
        unpack_kernel,
        sds((MEMBERS_HERE * PLANE, LANES)),
        (back.reshape(mems, MEMBERS_HERE, COLS),),
    )
    return result.reshape(prior_sample_set.shape)


def solution(mesh):
    return jax.shard_map(
        per_device,
        mesh=mesh,
        in_specs=(
            P("mem", None, "lat", "lon"),
            P(None, "lat", "lon"),
            P(None, "lat", "lon"),
            P(None, "lat", "lon"),
            P("lat", "lon", None),
            P("lat", "lon", None),
            P("lat", "lon", None),
            P("lat", "lon", None),
        ),
        out_specs=P("mem", None, "lat", "lon"),
        check_vma=False,
    )
```

```python
import functools

import jax
import jax.numpy as jnp
from jax import lax
from jax.experimental import pallas as pl
from jax.experimental.pallas import tpu as pltpu
from jax.sharding import PartitionSpec as P

STEPS = 4
LANES = 128
OWNED = 32
GROUPS = LANES // OWNED
ROWS = 4
BATCH = 32
MEMBERS_HERE = 8
LEVELS = 8
NOB = 256
PLANE = LEVELS * ROWS
VALUE_ROW = 11 * PLANE
SITE_ROW = VALUE_ROW + 2
PAYLOAD = SITE_ROW + 6
EDGE_ROWS = 16
COLS = LEVELS * OWNED
SPREAD_ROWS = 136
FAR = -8192
F32 = jnp.float32
BF16 = jnp.bfloat16
VMEM_LIMIT = 40 * 1024 * 1024
PAYLOAD_LIMIT = 60 * 1024 * 1024


def vmem(count):
    return [pl.BlockSpec(memory_space=pltpu.VMEM)] * count


def params():
    return pltpu.CompilerParams(vmem_limit_bytes=VMEM_LIMIT)


def lane_index():
    return lax.broadcasted_iota(jnp.int32, (8, LANES), 1)


def lat_masks():
    here = lax.axis_index("lat")
    return [scalar_mask(here, 0), scalar_mask(here, 1)]


def lon_parity():
    return lax.rem(lax.axis_index("lon"), 2)


def scalar_mask(value, wanted):
    return jnp.full((8, LANES), value, jnp.int32) == wanted


def roll(x, shift):
    shift %= LANES
    return x if shift == 0 else pltpu.roll(x, shift, 1)


def member_rows(own_ref, other_ref, here, level, row):
    start = level * ROWS + row % ROWS
    own = own_ref[pl.ds(start, 8, stride=PLANE), :]
    other = other_ref[pl.ds(start, 8, stride=PLANE), :]
    return jnp.where(here[row // ROWS], own, other)


def coef_rows(own_ref, other_ref, here, which, row):
    start = (MEMBERS_HERE + which) * PLANE + row % ROWS
    own = own_ref[pl.ds(start, 8, stride=ROWS), :]
    other = other_ref[pl.ds(start, 8, stride=ROWS), :]
    return jnp.where(here[row // ROWS], own, other)


def payload_kernel(
    prior_ref,
    east_ref,
    north_ref,
    spread_ref,
    value_ref,
    site_ref,
    ids_ref,
    weight_ref,
    out_ref,
    first_ref,
    second_ref,
    ids_out,
    weight_out,
    value,
    site,
    sems,
):
    owned = pl.ds(pl.multiple_of(lax.axis_index("mem") * OWNED, OWNED), OWNED)
    moves = [
        (prior_ref, out_ref.at[pl.ds(0, MEMBERS_HERE * PLANE), :]),
        *[
            (ref, out_ref.at[pl.ds((MEMBERS_HERE + n) * PLANE, PLANE), :])
            for n, ref in enumerate((east_ref, north_ref, spread_ref))
        ],
        (value_ref, value),
        (site_ref, site),
        (ids_ref.at[owned, :], ids_out),
        (weight_ref.at[owned, :], weight_out),
    ]
    copies = [pltpu.make_async_copy(src, dst, sems.at[n]) for n, (src, dst) in enumerate(moves)]
    for copy in copies:
        copy.start()
    for copy in copies:
        copy.wait()
    values = value[...]
    sites = site[...].astype(F32)
    rest = jnp.zeros((PAYLOAD - SITE_ROW - 2, LANES), F32)
    pieces = [values[:, :LANES], values[:, LANES:], sites[:, :LANES], sites[:, LANES:], rest]
    out_ref[VALUE_ROW:, :] = jnp.concatenate(pieces, axis=0)
    lane = lane_index()
    even = scalar_mask(lon_parity(), 0)
    for tile in range(2):
        left = jnp.zeros((8, LANES), F32)
        right = jnp.zeros((8, LANES), F32)
        for slot in range(32 if tile == 0 else 12):
            if tile == 0:
                x = out_ref[pl.ds(slot, 8, stride=PLANE), :]
            else:
                x = out_ref[pl.ds((MEMBERS_HERE + slot // 4) * PLANE + slot % 4, 8, stride=ROWS), :]
            place = (lane // 4) == slot
            left = jnp.where(place, roll(x, 4 * slot), left)
            right = jnp.where(place, roll(x, 4 * slot + 4), right)
        first_ref[tile * 8 : tile * 8 + 8, :] = jnp.where(even, right, left)
        second_ref[tile * 8 : tile * 8 + 8, :] = jnp.where(even, left, right)


def advance_in_time(q, coef, level, first_lane, last_lane):
    after = []
    for row in range(8):
        centre, border = q[row]
        rc, rb = roll(centre, 1), roll(border, 1)
        lc, lb = roll(centre, -1), roll(border, -1)
        wests = (jnp.where(first_lane, rb, rc), jnp.where(first_lane, rc, rb))
        easts = (jnp.where(last_lane, lb, lc), jnp.where(last_lane, lc, lb))
        both = []
        for part in range(2):
            c = [coef[row, n, part, level : level + 1, :] for n in range(5)]
            total = c[0] * q[row][part] + c[1] * wests[part] + c[2] * easts[part]
            if row > 0:
                total = total + c[3] * q[row - 1][part]
            if row < 7:
                total = total + c[4] * q[row + 1][part]
            both.append(total)
        after.append(tuple(both))
    return after


def forecast_kernel(
    own_ref,
    other_ref,
    first_other_ref,
    second_ref,
    second_other_ref,
    first_ref,
    send_ref,
    values_ref,
    coef,
    state,
):
    lane = lane_index()
    here = lat_masks()
    even = scalar_mask(lon_parity(), 0)
    first_lane = lane == 0
    last_lane = lane == LANES - 1
    east_lanes = lane < 4
    west_lanes = lane >= LANES - 4
    east, west = {}, {}
    for block in range(2):
        for tile in range(2):
            part = slice(tile * 8, tile * 8 + 8)
            a = jnp.where(here[block], first_ref[part, :], first_other_ref[part, :])
            b = jnp.where(here[block], second_ref[part, :], second_other_ref[part, :])
            east[block, tile] = jnp.where(even, a, b)
            west[block, tile] = jnp.where(even, b, a)

    def halo(row, tile, group):
        slot = group * ROWS + row % ROWS
        key = (row // ROWS, tile)
        from_east = roll(east[key], -4 * slot)
        from_west = roll(west[key], LANES - 4 - 4 * slot)
        return jnp.where(east_lanes, from_east, jnp.where(west_lanes, from_west, 0.0))

    for row in range(8):
        for part in range(2):
            if part == 0:
                u, v, d = (coef_rows(own_ref, other_ref, here, q, row) for q in range(3))
            else:
                u, v, d = (halo(row, 1, q) for q in range(3))
            up, un = jnp.maximum(u, 0.0), jnp.minimum(u, 0.0)
            vp, vn = jnp.maximum(v, 0.0), jnp.minimum(v, 0.0)
            coef[row, 0, part] = 1.0 - (up - un) - (vp - vn) - 4.0 * d
            coef[row, 1, part] = up + d
            coef[row, 2, part] = d - un
            coef[row, 3, part] = vp + d
            coef[row, 4, part] = d - vn

    for level in range(0, LEVELS, 2):
        pair = (level, level + 1)
        q = [
            [(member_rows(own_ref, other_ref, here, n, row), halo(row, 0, n)) for row in range(8)]
            for n in pair
        ]
        for _ in range(STEPS):
            q = [advance_in_time(q[n], coef, pair[n], first_lane, last_lane) for n in range(2)]
        for n in range(2):
            for row in range(8):
                state[pair[n], row] = q[n][row][0]

    for block in range(2):
        site_own = jnp.concatenate(
            [own_ref[SITE_ROW : SITE_ROW + 1, :], own_ref[SITE_ROW + 1 : SITE_ROW + 2, :]], axis=1
        )
        site_other = jnp.concatenate(
            [other_ref[SITE_ROW : SITE_ROW + 1, :], other_ref[SITE_ROW + 1 : SITE_ROW + 2, :]], axis=1
        )
        mine = jnp.full((1, NOB), lax.axis_index("lat"), jnp.int32) == block
        site = jnp.where(mine, site_own, site_other).astype(jnp.int32)
        site_row = jnp.broadcast_to(site >> 7, (8, NOB))
        site_lane = jnp.broadcast_to(site & (LANES - 1), (LANES, NOB))
        pick = jnp.where(lax.broadcasted_iota(jnp.int32, (LANES, NOB), 0) == site_lane, 1.0, 0.0).astype(BF16)
        x = state[:, block * ROWS : (block + 1) * ROWS].reshape(PLANE * 8, LANES)
        x1 = x.astype(BF16)
        rest = x - x1.astype(F32)
        x2 = rest.astype(BF16)
        x3 = (rest - x2.astype(F32)).astype(BF16)
        picked = (
            jnp.dot(x3, pick, preferred_element_type=F32)
            + jnp.dot(x2, pick, preferred_element_type=F32)
            + jnp.dot(x1, pick, preferred_element_type=F32)
        )
        total = jnp.zeros((8, NOB), F32)
        for n in range(PLANE):
            total = jnp.where(site_row == n, picked[n * 8 : n * 8 + 8, :], total)
        for target in range(send_ref.shape[0]):
            send_ref[target, :, COLS + block * NOB : COLS + (block + 1) * NOB] = total

    own = jnp.concatenate([own_ref[VALUE_ROW + n : VALUE_ROW + n + 1, :] for n in range(2)], axis=1)
    other = jnp.concatenate([other_ref[VALUE_ROW + n : VALUE_ROW + n + 1, :] for n in range(2)], axis=1)
    south = jnp.full((1, NOB), lax.axis_index("lat"), jnp.int32) == 0
    values = jnp.concatenate([jnp.where(south, own, other), jnp.where(south, other, own)], axis=1)
    values_ref[...] = jnp.broadcast_to(values, (8, 2 * NOB))

    segment = lane // OWNED
    for row in range(ROWS):
        here_row = lax.axis_index("lat") * ROWS + row
        values = [state[level, here_row] for level in range(LEVELS)]
        for group in range(GROUPS):
            for half in range(2):
                total = jnp.zeros((8, LANES), F32)
                for n in range(4):
                    moved = roll(values[half * 4 + n], OWNED * (n - group))
                    total = jnp.where(segment == n, moved, total)
                send_ref[row * GROUPS + group, :, half * LANES : (half + 1) * LANES] = total


def halves(x):
    hi = x.astype(BF16)
    return hi, (x - hi.astype(F32)).astype(BF16)


def left_side(x):
    return jnp.concatenate(halves(x), axis=1)


def product(left, right):
    out = jnp.dot(left, right, preferred_element_type=F32)
    half = out.shape[1] // 2
    return out[:, :half] + out[:, half:]


def small_product(rows, halves_of_right):
    out = jnp.dot(jnp.concatenate(halves(rows), axis=0), halves_of_right, preferred_element_type=F32)
    half = out.shape[1] // 2
    return out[0:16, :half] + (out[0:16, half:] + out[16:32, :half])


def spread_kernel(recv_ref, values_ref, out_ref, near_ref):
    members = recv_ref.shape[0]
    obs = recv_ref[:, COLS:]
    mean = jnp.sum(obs, axis=0, keepdims=True) / members
    pert = obs - mean
    innovation = values_ref[0:1, :] - mean
    out_ref[0:members, :] = pert
    near_ref[0:members, :] = pert
    near_ref[members:, :] = innovation
    row = lax.broadcasted_iota(jnp.int32, (8, 2 * NOB), 0)
    out_ref[members:, :] = jnp.where(row == 0, innovation, 0.0)


def fill_table(table, start, spread_ref):
    width = pl.ds(start, 2 * NOB)
    hi, lo = halves(spread_ref[0:128, :])
    table[0:128, width] = hi
    table[128:256, width] = lo
    innovation = spread_ref[128:129, :]
    first_term = innovation.astype(BF16).astype(F32)
    row = lax.broadcasted_iota(jnp.int32, (16, 2 * NOB), 0)
    extra = jnp.where(row == 0, first_term, jnp.where(row == 1, innovation - first_term, 0.0))
    table[256:272, width] = extra.astype(BF16)


def local_places(ids):
    code = ids >> 8
    lat_step = jnp.where(code >= 6, 2, jnp.where(code >= 3, 1, 0))
    lon_step = code - 3 * lat_step
    odd = jnp.full(ids.shape, lon_parity(), jnp.int32) == 1
    slot = jnp.where(odd, 2 - lon_step, lon_step)
    within = (lat_step - 1 + lax.axis_index("lat")) * NOB + (ids & (NOB - 1))
    near = jnp.where(slot == 0, FAR, within + jnp.where(slot == 2, 2 * NOB, 0))
    far = jnp.where(slot == 0, within, FAR)
    return near.astype(F32), far.astype(F32)


def own_kernel(payload_ref, own_ref):
    own_ref[...] = payload_ref[...]


def gather_pair(table, places, first_column, blocks):
    place = lax.broadcasted_iota(jnp.int32, (NOB, LANES), 0).astype(F32).astype(BF16)
    one, zero = jnp.ones((), BF16), jnp.zeros((), BF16)
    hot = []
    for block in range(blocks):
        sides = []
        for k in range(2):
            row = places[pl.ds(first_column + k, 1), :] - float(block * NOB)
            sides.append(jnp.where(row.astype(BF16) == place, one, zero))
        hot.append(jnp.concatenate(sides, axis=1))
    both = jnp.dot(table[...], jnp.concatenate(hot, axis=0), preferred_element_type=F32)
    rows = both[0:128] + both[128:256]
    innov = both[256:257] + both[257:258]
    found = jnp.concatenate([rows, jnp.broadcast_to(innov, (8, 2 * LANES))], axis=0)
    return found[:, :LANES], found[:, LANES:]


def near_kernel(
    recv_ref, ids_ref, mine_ref, first_ref, part_ref, dev_ref, centre_ref, table, places
):
    members = recv_ref.shape[0]
    fill_table(table, 0, mine_ref)
    fill_table(table, 2 * NOB, first_ref)
    places[...] = local_places(ids_ref[...])[0]
    traces = jnp.transpose(recv_ref[:, :COLS])
    centre = jnp.sum(traces, axis=1, keepdims=True) / members
    dev_ref[...] = traces - centre
    centre_ref[...] = jnp.broadcast_to(centre, traces.shape)

    def turn(n, carry):
        for pair in range(BATCH // 2):
            c = n * BATCH + pair * 2
            left, right = gather_pair(table, places, c, 4)
            part_ref[c] = left
            part_ref[c + 1] = right
        return carry

    lax.fori_loop(0, OWNED // BATCH, turn, 0)


def columns_kernel(
    ids_ref,
    weight_ref,
    second_ref,
    part_ref,
    dev_ref,
    centre_ref,
    out_ref,
    table,
    places,
    res,
    eyes,
    found,
    full,
    half_s,
    half_u,
    half_z,
    drives,
):
    members = 128
    scale = members - 1.0
    fill_table(table, 0, second_ref)
    places[...] = local_places(ids_ref[...])[1]
    i0 = lax.broadcasted_iota(jnp.int32, (members, members), 0)
    i1 = lax.broadcasted_iota(jnp.int32, (members, members), 1)
    for n, value in enumerate((scale, 0.84375, 1.5380859375)):
        eyes[n] = jnp.where(i0 == i1, value, 0.0).astype(F32)

    def put(ref, b, x):
        hi, lo = halves(x)
        ref[b, :, 0:members] = hi
        ref[b, :, members:] = lo

    def right_of(ref, b):
        top = ref[b]
        low = jnp.concatenate([ref[b, :, 0:members], jnp.zeros((members, members), BF16)], axis=1)
        return jnp.concatenate([top, low], axis=0)

    def turn(n, carry):
        base = n * BATCH
        slots = range(BATCH)
        invs = []
        for pair in range(BATCH // 2):
            for k, extra in enumerate(gather_pair(table, places, base + pair * 2, 2)):
                found[pair * 2 + k] = extra + part_ref[base + pair * 2 + k]
        for b in slots:
            pert = found[b, 0:members]
            innov = found[b, members : members + 1]
            w = weight_ref[pl.ds(base + b, 1), :]
            left = jnp.concatenate([pert * w, jnp.broadcast_to(w * innov, (16, LANES))], axis=0)
            e_hi, e_lo = halves(jnp.transpose(pert))
            right = jnp.concatenate(
                [
                    jnp.concatenate([e_hi, e_lo], axis=1),
                    jnp.concatenate([e_hi, jnp.zeros_like(e_hi)], axis=1),
                ],
                axis=0,
            )
            both = product(left_side(left), right)
            gram = both[:members]
            drives[b] = both[members : members + 8]
            norm = jnp.sum(jnp.sum(gram * gram, axis=0, keepdims=True), axis=1, keepdims=True)
            inv = 1.0 / (scale + jnp.sqrt(norm))
            invs.append(inv)
            s = (eyes[0] + gram) * inv
            full[b] = s
            put(half_s, b, s)
        for b in slots:
            square = product(half_s[b], right_of(half_s, b))
            put(half_u, b, 0.25 * square - 1.125 * full[b] + eyes[1])
        for b in slots:
            square = product(half_u[b], right_of(half_u, b))
            put(half_z, b, square - 0.5390625 * full[b] + eyes[2])
        rows = []
        for b in slots:
            x = jnp.concatenate([dev_ref[pl.ds(base + b, 8, stride=OWNED), :], drives[b]], axis=0)
            both = product(jnp.concatenate([half_s[b], left_side(x)], axis=0), right_of(half_z, b))
            put(half_u, b, both[0:members])
            rows.append(both[members:])
        for b in slots:
            put(half_s, b, product(half_u[b], right_of(half_z, b)))
        moved = [0.0625 * x for x in rows]
        for coefficient in (-0.5625, 1.6875, -2.4375, 2.25):
            moved = [coefficient * rows[b] + small_product(moved[b], half_s[b]) for b in slots]
        for b in slots:
            y = moved[b][0:8]
            shift = jnp.sum(y * moved[b][8:16], axis=1, keepdims=True) * invs[b]
            res[pl.ds(base + b, 8, stride=OWNED), :] = jnp.sqrt(scale * invs[b]) * y + shift
        return carry

    lax.fori_loop(0, OWNED // BATCH, turn, 0)
    out_ref[...] = jnp.transpose(res[...] + centre_ref[...])


def unpack_kernel(recv_ref, out_ref):
    segment = lane_index() // OWNED
    for row in range(ROWS):
        for half in range(2):
            parts = [
                recv_ref[row * GROUPS + g, :, half * LANES : (half + 1) * LANES] for g in range(GROUPS)
            ]
            for n in range(4):
                level = half * 4 + n
                total = jnp.zeros((8, LANES), F32)
                for g in range(GROUPS):
                    total = jnp.where(segment == g, roll(parts[g], OWNED * (g - n)), total)
                out_ref[pl.ds(level * ROWS + row, 8, stride=PLANE), :] = total


def call(kernel, shapes, operands, scratch=(), flops=None):
    single = not isinstance(shapes, list)
    cost = None
    if flops is not None:
        cost = pl.CostEstimate(flops=flops, bytes_accessed=1 << 22, transcendentals=0)
    return pl.pallas_call(
        kernel,
        out_shape=shapes,
        in_specs=vmem(len(operands)),
        out_specs=vmem(1)[0] if single else vmem(len(shapes)),
        scratch_shapes=list(scratch),
        compiler_params=params(),
        cost_estimate=cost,
    )(*operands)


def per_device(
    prior_sample_set,
    eastward_cfl_number,
    northward_cfl_number,
    spreading_number,
    obs_value,
    obs_site,
    neighbours,
    loc_weight,
):
    sds = functools.partial(jax.ShapeDtypeStruct, dtype=F32)
    mems = lax.axis_size("mem")
    lons = lax.axis_size("lon")
    on_chip = [(i, i ^ 1) for i in range(lons)]
    whole = 2 * lons
    off_chip, corners, chip_corners = [], [], []
    for i in range(whole):
        j = (i + 1 if i % 2 else i - 1) % whole
        off_chip.append((i % lons * 2 + i // lons, j % lons * 2 + j // lons))
        corners.append((i % lons * 2 + i // lons, j % lons * 2 + 1 - i // lons))
        chip_corners.append((i % lons * 2 + i // lons, (i % lons ^ 1) * 2 + 1 - i // lons))
    off_lon = [(i, (i + 1 if i % 2 else i - 1) % lons) for i in range(lons)]

    edge = sds((EDGE_ROWS, LANES))
    payload, first, second, near_ids, weight = pl.pallas_call(
        payload_kernel,
        out_shape=[
            sds((PAYLOAD, LANES)),
            edge,
            edge,
            jax.ShapeDtypeStruct((OWNED, LANES), jnp.int32),
            sds((OWNED, LANES)),
        ],
        in_specs=[pl.BlockSpec(memory_space=pltpu.HBM)] * 8,
        out_specs=vmem(5),
        scratch_shapes=[
            pltpu.VMEM((1, NOB), F32),
            pltpu.VMEM((1, NOB), jnp.int32),
            pltpu.SemaphoreType.DMA((8,)),
        ],
        compiler_params=pltpu.CompilerParams(vmem_limit_bytes=PAYLOAD_LIMIT),
    )(
        prior_sample_set.reshape(MEMBERS_HERE * PLANE, LANES),
        eastward_cfl_number.reshape(PLANE, LANES),
        northward_cfl_number.reshape(PLANE, LANES),
        spreading_number.reshape(PLANE, LANES),
        obs_value.reshape(1, NOB),
        obs_site.reshape(1, NOB),
        neighbours.reshape(ROWS * LANES, LANES),
        loc_weight.reshape(ROWS * LANES, LANES),
    )
    other = lax.ppermute(payload, "lat", [(0, 1), (1, 0)])
    first_other = lax.ppermute(first, ("lon", "lat"), chip_corners)
    second_in = lax.ppermute(second, "lon", off_lon)
    second_other = lax.ppermute(second, ("lon", "lat"), corners)
    first_in = lax.ppermute(first, "lon", on_chip)
    own = call(own_kernel, sds((PAYLOAD, LANES)), (payload,), flops=1 << 20)
    send, values = call(
        forecast_kernel,
        [sds((mems, MEMBERS_HERE, COLS + 2 * NOB)), sds((8, 2 * NOB))],
        (own, other, first_other, second_in, second_other, first_in),
        [pltpu.VMEM((8, 5, 2, 8, LANES), F32), pltpu.VMEM((LEVELS, 8, 8, LANES), F32)],
    )
    members = mems * MEMBERS_HERE
    got = lax.all_to_all(
        send.reshape(members, send.shape[2]), "mem", split_axis=0, concat_axis=0, tiled=True
    )
    spread, spread_near = call(
        spread_kernel,
        [sds((SPREAD_ROWS, 2 * NOB)), sds((members + 1, 2 * NOB))],
        (got, values),
    )
    spread_second = lax.ppermute(spread, ("lon", "lat"), off_chip)
    spread_first = lax.ppermute(spread_near, "lon", on_chip)
    part, dev, centre = call(
        near_kernel,
        [sds((OWNED, SPREAD_ROWS, LANES)), sds((COLS, members)), sds((COLS, members))],
        (got, near_ids, spread, spread_first),
        [pltpu.VMEM((272, 4 * NOB), BF16), pltpu.VMEM((OWNED, LANES), F32)],
    )
    updated = call(
        columns_kernel,
        sds((members, COLS)),
        (near_ids, weight, spread_second, part, dev, centre),
        [
            pltpu.VMEM((272, 2 * NOB), BF16),
            pltpu.VMEM((OWNED, LANES), F32),
            pltpu.VMEM((COLS, members), F32),
            pltpu.VMEM((3, members, members), F32),
            pltpu.VMEM((BATCH, SPREAD_ROWS, LANES), F32),
            pltpu.VMEM((BATCH, members, members), F32),
            *[pltpu.VMEM((BATCH, members, 2 * members), BF16)] * 3,
            pltpu.VMEM((BATCH, 8, members), F32),
        ],
        flops=2 * OWNED * 7 * members * 4 * members * members,
    )
    back = lax.all_to_all(updated, "mem", split_axis=0, concat_axis=0, tiled=True)
    result = call(
        unpack_kernel,
        sds((MEMBERS_HERE * PLANE, LANES)),
        (back.reshape(mems, MEMBERS_HERE, COLS),),
    )
    return result.reshape(prior_sample_set.shape)


def solution(mesh):
    return jax.shard_map(
        per_device,
        mesh=mesh,
        in_specs=(
            P("mem", None, "lat", "lon"),
            P(None, "lat", "lon"),
            P(None, "lat", "lon"),
            P(None, "lat", "lon"),
            P("lat", "lon", None),
            P("lat", "lon", None),
            P("lat", "lon", None),
            P("lat", "lon", None),
        ),
        out_specs=P("mem", None, "lat", "lon"),
        check_vma=False,
    )
```

```python
import functools

import jax
import jax.numpy as jnp
from jax import lax
from jax.experimental import pallas as pl
from jax.experimental.pallas import tpu as pltpu
from jax.sharding import PartitionSpec as P

STEPS = 4
LANES = 128
OWNED = 32
GROUPS = LANES // OWNED
ROWS = 4
BATCH = 32
MEMBERS_HERE = 8
LEVELS = 8
NOB = 256
PLANE = LEVELS * ROWS
VALUE_ROW = 11 * PLANE
SITE_ROW = VALUE_ROW + 2
PAYLOAD = SITE_ROW + 6
EDGE_ROWS = 16
COLS = LEVELS * OWNED
SPREAD_ROWS = 136
FAR = -8192
F32 = jnp.float32
BF16 = jnp.bfloat16
VMEM_LIMIT = 40 * 1024 * 1024
PAYLOAD_LIMIT = 60 * 1024 * 1024


def vmem(count):
    return [pl.BlockSpec(memory_space=pltpu.VMEM)] * count


def params():
    return pltpu.CompilerParams(vmem_limit_bytes=VMEM_LIMIT)


def lane_index():
    return lax.broadcasted_iota(jnp.int32, (8, LANES), 1)


def lat_masks():
    here = lax.axis_index("lat")
    return [scalar_mask(here, 0), scalar_mask(here, 1)]


def lon_parity():
    return lax.rem(lax.axis_index("lon"), 2)


def scalar_mask(value, wanted):
    return jnp.full((8, LANES), value, jnp.int32) == wanted


def roll(x, shift):
    shift %= LANES
    return x if shift == 0 else pltpu.roll(x, shift, 1)


def member_rows(own_ref, other_ref, here, level, row):
    start = level * ROWS + row % ROWS
    own = own_ref[pl.ds(start, 8, stride=PLANE), :]
    other = other_ref[pl.ds(start, 8, stride=PLANE), :]
    return jnp.where(here[row // ROWS], own, other)


def coef_rows(own_ref, other_ref, here, which, row):
    start = (MEMBERS_HERE + which) * PLANE + row % ROWS
    own = own_ref[pl.ds(start, 8, stride=ROWS), :]
    other = other_ref[pl.ds(start, 8, stride=ROWS), :]
    return jnp.where(here[row // ROWS], own, other)


def payload_kernel(
    prior_ref,
    east_ref,
    north_ref,
    spread_ref,
    value_ref,
    site_ref,
    ids_ref,
    weight_ref,
    out_ref,
    first_ref,
    second_ref,
    extra_ref,
    value,
    site,
    ids,
    sems,
):
    owned = pl.ds(pl.multiple_of(lax.axis_index("mem") * OWNED, OWNED), OWNED)
    moves = [
        (prior_ref, out_ref.at[pl.ds(0, MEMBERS_HERE * PLANE), :]),
        *[
            (ref, out_ref.at[pl.ds((MEMBERS_HERE + n) * PLANE, PLANE), :])
            for n, ref in enumerate((east_ref, north_ref, spread_ref))
        ],
        (value_ref, value),
        (site_ref, site),
        (ids_ref.at[owned, :], ids),
        (weight_ref.at[owned, :], extra_ref.at[pl.ds(OWNED, OWNED), :]),
    ]
    copies = [pltpu.make_async_copy(src, dst, sems.at[n]) for n, (src, dst) in enumerate(moves)]
    for copy in copies:
        copy.start()
    for copy in copies:
        copy.wait()
    extra_ref[0:OWNED, :] = ids[...].astype(F32)
    values = value[...]
    sites = site[...].astype(F32)
    rest = jnp.zeros((PAYLOAD - SITE_ROW - 2, LANES), F32)
    pieces = [values[:, :LANES], values[:, LANES:], sites[:, :LANES], sites[:, LANES:], rest]
    out_ref[VALUE_ROW:, :] = jnp.concatenate(pieces, axis=0)
    lane = lane_index()
    even = scalar_mask(lon_parity(), 0)
    for tile in range(2):
        left = jnp.zeros((8, LANES), F32)
        right = jnp.zeros((8, LANES), F32)
        for slot in range(32 if tile == 0 else 12):
            if tile == 0:
                x = out_ref[pl.ds(slot, 8, stride=PLANE), :]
            else:
                x = out_ref[pl.ds((MEMBERS_HERE + slot // 4) * PLANE + slot % 4, 8, stride=ROWS), :]
            place = (lane // 4) == slot
            left = jnp.where(place, roll(x, 4 * slot), left)
            right = jnp.where(place, roll(x, 4 * slot + 4), right)
        first_ref[tile * 8 : tile * 8 + 8, :] = jnp.where(even, right, left)
        second_ref[tile * 8 : tile * 8 + 8, :] = jnp.where(even, left, right)


def advance_in_time(q, coef, level, first_lane, last_lane):
    after = []
    for row in range(8):
        centre, border = q[row]
        rc, rb = roll(centre, 1), roll(border, 1)
        lc, lb = roll(centre, -1), roll(border, -1)
        wests = (jnp.where(first_lane, rb, rc), jnp.where(first_lane, rc, rb))
        easts = (jnp.where(last_lane, lb, lc), jnp.where(last_lane, lc, lb))
        both = []
        for part in range(2):
            c = [coef[row, n, part, level : level + 1, :] for n in range(5)]
            total = c[0] * q[row][part] + c[1] * wests[part] + c[2] * easts[part]
            if row > 0:
                total = total + c[3] * q[row - 1][part]
            if row < 7:
                total = total + c[4] * q[row + 1][part]
            both.append(total)
        after.append(tuple(both))
    return after


def forecast_kernel(
    own_ref,
    other_ref,
    first_other_ref,
    second_other_ref,
    second_ref,
    first_ref,
    send_ref,
    values_ref,
    coef,
    state,
):
    lane = lane_index()
    here = lat_masks()
    even = scalar_mask(lon_parity(), 0)
    first_lane = lane == 0
    last_lane = lane == LANES - 1
    east_lanes = lane < 4
    west_lanes = lane >= LANES - 4
    east, west = {}, {}
    for block in range(2):
        for tile in range(2):
            part = slice(tile * 8, tile * 8 + 8)
            a = jnp.where(here[block], first_ref[part, :], first_other_ref[part, :])
            b = jnp.where(here[block], second_ref[part, :], second_other_ref[part, :])
            east[block, tile] = jnp.where(even, a, b)
            west[block, tile] = jnp.where(even, b, a)

    def halo(row, tile, group):
        slot = group * ROWS + row % ROWS
        key = (row // ROWS, tile)
        from_east = roll(east[key], -4 * slot)
        from_west = roll(west[key], LANES - 4 - 4 * slot)
        return jnp.where(east_lanes, from_east, jnp.where(west_lanes, from_west, 0.0))

    for row in range(8):
        for part in range(2):
            if part == 0:
                u, v, d = (coef_rows(own_ref, other_ref, here, q, row) for q in range(3))
            else:
                u, v, d = (halo(row, 1, q) for q in range(3))
            up, un = jnp.maximum(u, 0.0), jnp.minimum(u, 0.0)
            vp, vn = jnp.maximum(v, 0.0), jnp.minimum(v, 0.0)
            coef[row, 0, part] = 1.0 - (up - un) - (vp - vn) - 4.0 * d
            coef[row, 1, part] = up + d
            coef[row, 2, part] = d - un
            coef[row, 3, part] = vp + d
            coef[row, 4, part] = d - vn

    for level in range(0, LEVELS, 2):
        pair = (level, level + 1)
        q = [
            [(member_rows(own_ref, other_ref, here, n, row), halo(row, 0, n)) for row in range(8)]
            for n in pair
        ]
        for _ in range(STEPS):
            q = [advance_in_time(q[n], coef, pair[n], first_lane, last_lane) for n in range(2)]
        for n in range(2):
            for row in range(8):
                state[pair[n], row] = q[n][row][0]

    for block in range(2):
        site_own = jnp.concatenate(
            [own_ref[SITE_ROW : SITE_ROW + 1, :], own_ref[SITE_ROW + 1 : SITE_ROW + 2, :]], axis=1
        )
        site_other = jnp.concatenate(
            [other_ref[SITE_ROW : SITE_ROW + 1, :], other_ref[SITE_ROW + 1 : SITE_ROW + 2, :]], axis=1
        )
        mine = jnp.full((1, NOB), lax.axis_index("lat"), jnp.int32) == block
        site = jnp.where(mine, site_own, site_other).astype(jnp.int32)
        site_row = jnp.broadcast_to(site >> 7, (8, NOB))
        site_lane = jnp.broadcast_to(site & (LANES - 1), (LANES, NOB))
        pick = jnp.where(lax.broadcasted_iota(jnp.int32, (LANES, NOB), 0) == site_lane, 1.0, 0.0).astype(BF16)
        x = state[:, block * ROWS : (block + 1) * ROWS].reshape(PLANE * 8, LANES)
        x1 = x.astype(BF16)
        rest = x - x1.astype(F32)
        x2 = rest.astype(BF16)
        x3 = (rest - x2.astype(F32)).astype(BF16)
        picked = (
            jnp.dot(x3, pick, preferred_element_type=F32)
            + jnp.dot(x2, pick, preferred_element_type=F32)
            + jnp.dot(x1, pick, preferred_element_type=F32)
        )
        total = jnp.zeros((8, NOB), F32)
        for n in range(PLANE):
            total = jnp.where(site_row == n, picked[n * 8 : n * 8 + 8, :], total)
        for target in range(send_ref.shape[0]):
            send_ref[target, :, COLS + block * NOB : COLS + (block + 1) * NOB] = total

    own = jnp.concatenate([own_ref[VALUE_ROW + n : VALUE_ROW + n + 1, :] for n in range(2)], axis=1)
    other = jnp.concatenate([other_ref[VALUE_ROW + n : VALUE_ROW + n + 1, :] for n in range(2)], axis=1)
    south = jnp.full((1, NOB), lax.axis_index("lat"), jnp.int32) == 0
    values = jnp.concatenate([jnp.where(south, own, other), jnp.where(south, other, own)], axis=1)
    values_ref[...] = jnp.broadcast_to(values, (8, 2 * NOB))

    segment = lane // OWNED
    for row in range(ROWS):
        here_row = lax.axis_index("lat") * ROWS + row
        values = [state[level, here_row] for level in range(LEVELS)]
        for group in range(GROUPS):
            for half in range(2):
                total = jnp.zeros((8, LANES), F32)
                for n in range(4):
                    moved = roll(values[half * 4 + n], OWNED * (n - group))
                    total = jnp.where(segment == n, moved, total)
                send_ref[row * GROUPS + group, :, half * LANES : (half + 1) * LANES] = total


def halves(x):
    hi = x.astype(BF16)
    return hi, (x - hi.astype(F32)).astype(BF16)


def left_side(x):
    return jnp.concatenate(halves(x), axis=1)


def product(left, right):
    out = jnp.dot(left, right, preferred_element_type=F32)
    half = out.shape[1] // 2
    return out[:, :half] + out[:, half:]


def small_product(rows, halves_of_right):
    out = jnp.dot(jnp.concatenate(halves(rows), axis=0), halves_of_right, preferred_element_type=F32)
    half = out.shape[1] // 2
    return out[0:16, :half] + (out[0:16, half:] + out[16:32, :half])


def spread_kernel(recv_ref, values_ref, out_ref, near_ref):
    members = recv_ref.shape[0]
    obs = recv_ref[:, COLS:]
    mean = jnp.sum(obs, axis=0, keepdims=True) / members
    pert = obs - mean
    innovation = values_ref[0:1, :] - mean
    out_ref[0:members, :] = pert
    near_ref[0:members, :] = pert
    near_ref[members:, :] = innovation
    row = lax.broadcasted_iota(jnp.int32, (8, 2 * NOB), 0)
    out_ref[members:, :] = jnp.where(row == 0, innovation, 0.0)


def fill_table(table, start, spread_ref):
    width = pl.ds(start, 2 * NOB)
    hi, lo = halves(spread_ref[0:128, :])
    table[0:128, width] = hi
    table[128:256, width] = lo
    innovation = spread_ref[128:129, :]
    first_term = innovation.astype(BF16).astype(F32)
    row = lax.broadcasted_iota(jnp.int32, (16, 2 * NOB), 0)
    extra = jnp.where(row == 0, first_term, jnp.where(row == 1, innovation - first_term, 0.0))
    table[256:272, width] = extra.astype(BF16)


def local_places(ids):
    code = ids >> 8
    lat_step = jnp.where(code >= 6, 2, jnp.where(code >= 3, 1, 0))
    lon_step = code - 3 * lat_step
    odd = jnp.full(ids.shape, lon_parity(), jnp.int32) == 1
    slot = jnp.where(odd, 2 - lon_step, lon_step)
    within = (lat_step - 1 + lax.axis_index("lat")) * NOB + (ids & (NOB - 1))
    near = jnp.where(slot == 0, FAR, within + jnp.where(slot == 2, 2 * NOB, 0))
    far = jnp.where(slot == 0, within, FAR)
    return near.astype(F32), far.astype(F32)


def own_kernel(payload_ref, extra_ref, own_ref, near_ref, far_ref, weight_out):
    own_ref[...] = payload_ref[...]
    weight_out[...] = extra_ref[OWNED:, :]
    near_ref[...], far_ref[...] = local_places(extra_ref[0:OWNED, :].astype(jnp.int32))


def gather_pair(table, places, first_column, blocks):
    place = lax.broadcasted_iota(jnp.int32, (NOB, LANES), 0).astype(F32).astype(BF16)
    one, zero = jnp.ones((), BF16), jnp.zeros((), BF16)
    hot = []
    for block in range(blocks):
        sides = []
        for k in range(2):
            row = places[pl.ds(first_column + k, 1), :] - float(block * NOB)
            sides.append(jnp.where(row.astype(BF16) == place, one, zero))
        hot.append(jnp.concatenate(sides, axis=1))
    both = jnp.dot(table[...], jnp.concatenate(hot, axis=0), preferred_element_type=F32)
    rows = both[0:128] + both[128:256]
    innov = both[256:257] + both[257:258]
    found = jnp.concatenate([rows, jnp.broadcast_to(innov, (8, 2 * LANES))], axis=0)
    return found[:, :LANES], found[:, LANES:]


def near_kernel(
    recv_ref, places, mine_ref, first_ref, part_ref, dev_ref, centre_ref, table
):
    members = recv_ref.shape[0]
    fill_table(table, 0, mine_ref)
    fill_table(table, 2 * NOB, first_ref)
    traces = jnp.transpose(recv_ref[:, :COLS])
    centre = jnp.sum(traces, axis=1, keepdims=True) / members
    dev_ref[...] = traces - centre
    centre_ref[...] = jnp.broadcast_to(centre, traces.shape)

    def turn(n, carry):
        for pair in range(BATCH // 2):
            c = n * BATCH + pair * 2
            left, right = gather_pair(table, places, c, 4)
            part_ref[c] = left
            part_ref[c + 1] = right
        return carry

    lax.fori_loop(0, OWNED // BATCH, turn, 0)


def columns_kernel(
    places,
    weight_ref,
    second_ref,
    part_ref,
    dev_ref,
    centre_ref,
    out_ref,
    table,
    res,
    eyes,
    found,
    full,
    half_s,
    half_u,
    half_z,
    drives,
):
    members = 128
    scale = members - 1.0
    fill_table(table, 0, second_ref)
    i0 = lax.broadcasted_iota(jnp.int32, (members, members), 0)
    i1 = lax.broadcasted_iota(jnp.int32, (members, members), 1)
    for n, value in enumerate((scale, 0.84375, 1.5380859375)):
        eyes[n] = jnp.where(i0 == i1, value, 0.0).astype(F32)

    def put(ref, b, x):
        hi, lo = halves(x)
        ref[b, :, 0:members] = hi
        ref[b, :, members:] = lo

    def right_of(ref, b):
        top = ref[b]
        low = jnp.concatenate([ref[b, :, 0:members], jnp.zeros((members, members), BF16)], axis=1)
        return jnp.concatenate([top, low], axis=0)

    def turn(n, carry):
        base = n * BATCH
        slots = range(BATCH)
        invs = []
        for pair in range(BATCH // 2):
            for k, extra in enumerate(gather_pair(table, places, base + pair * 2, 2)):
                found[pair * 2 + k] = extra + part_ref[base + pair * 2 + k]
        for b in slots:
            pert = found[b, 0:members]
            innov = found[b, members : members + 1]
            w = weight_ref[pl.ds(base + b, 1), :]
            left = jnp.concatenate([pert * w, jnp.broadcast_to(w * innov, (16, LANES))], axis=0)
            e_hi, e_lo = halves(jnp.transpose(pert))
            right = jnp.concatenate(
                [
                    jnp.concatenate([e_hi, e_lo], axis=1),
                    jnp.concatenate([e_hi, jnp.zeros_like(e_hi)], axis=1),
                ],
                axis=0,
            )
            both = product(left_side(left), right)
            gram = both[:members]
            drives[b] = both[members : members + 8]
            norm = jnp.sum(jnp.sum(gram * gram, axis=0, keepdims=True), axis=1, keepdims=True)
            inv = 1.0 / (scale + jnp.sqrt(norm))
            invs.append(inv)
            s = (eyes[0] + gram) * inv
            full[b] = s
            put(half_s, b, s)
        for b in slots:
            square = product(half_s[b], right_of(half_s, b))
            put(half_u, b, 0.25 * square - 1.125 * full[b] + eyes[1])
        for b in slots:
            square = product(half_u[b], right_of(half_u, b))
            put(half_z, b, square - 0.5390625 * full[b] + eyes[2])
        rows = []
        for b in slots:
            x = jnp.concatenate([dev_ref[pl.ds(base + b, 8, stride=OWNED), :], drives[b]], axis=0)
            both = product(jnp.concatenate([half_s[b], left_side(x)], axis=0), right_of(half_z, b))
            put(half_u, b, both[0:members])
            rows.append(both[members:])
        for b in slots:
            put(half_s, b, product(half_u[b], right_of(half_z, b)))
        moved = [0.0625 * x for x in rows]
        for coefficient in (-0.5625, 1.6875, -2.4375, 2.25):
            moved = [coefficient * rows[b] + small_product(moved[b], half_s[b]) for b in slots]
        for b in slots:
            y = moved[b][0:8]
            shift = jnp.sum(y * moved[b][8:16], axis=1, keepdims=True) * invs[b]
            res[pl.ds(base + b, 8, stride=OWNED), :] = jnp.sqrt(scale * invs[b]) * y + shift
        return carry

    lax.fori_loop(0, OWNED // BATCH, turn, 0)
    out_ref[...] = jnp.transpose(res[...] + centre_ref[...])


def unpack_kernel(recv_ref, out_ref):
    segment = lane_index() // OWNED
    for row in range(ROWS):
        for half in range(2):
            parts = [
                recv_ref[row * GROUPS + g, :, half * LANES : (half + 1) * LANES] for g in range(GROUPS)
            ]
            for n in range(4):
                level = half * 4 + n
                total = jnp.zeros((8, LANES), F32)
                for g in range(GROUPS):
                    total = jnp.where(segment == g, roll(parts[g], OWNED * (g - n)), total)
                out_ref[pl.ds(level * ROWS + row, 8, stride=PLANE), :] = total


def call(kernel, shapes, operands, scratch=(), flops=None):
    single = not isinstance(shapes, list)
    cost = None
    if flops is not None:
        cost = pl.CostEstimate(flops=flops, bytes_accessed=1 << 22, transcendentals=0)
    return pl.pallas_call(
        kernel,
        out_shape=shapes,
        in_specs=vmem(len(operands)),
        out_specs=vmem(1)[0] if single else vmem(len(shapes)),
        scratch_shapes=list(scratch),
        compiler_params=params(),
        cost_estimate=cost,
    )(*operands)


def per_device(
    prior_sample_set,
    eastward_cfl_number,
    northward_cfl_number,
    spreading_number,
    obs_value,
    obs_site,
    neighbours,
    loc_weight,
):
    sds = functools.partial(jax.ShapeDtypeStruct, dtype=F32)
    mems = lax.axis_size("mem")
    lons = lax.axis_size("lon")
    on_chip = [(i, i ^ 1) for i in range(lons)]
    whole = 2 * lons
    off_chip, corners, chip_corners = [], [], []
    for i in range(whole):
        j = (i + 1 if i % 2 else i - 1) % whole
        off_chip.append((i % lons * 2 + i // lons, j % lons * 2 + j // lons))
        corners.append((i % lons * 2 + i // lons, j % lons * 2 + 1 - i // lons))
        chip_corners.append((i % lons * 2 + i // lons, (i % lons ^ 1) * 2 + 1 - i // lons))
    off_lon = [(i, (i + 1 if i % 2 else i - 1) % lons) for i in range(lons)]

    edge = sds((EDGE_ROWS, LANES))
    payload, first, second, extra = pl.pallas_call(
        payload_kernel,
        out_shape=[
            sds((PAYLOAD, LANES)),
            edge,
            edge,
            sds((2 * OWNED, LANES)),
        ],
        in_specs=[pl.BlockSpec(memory_space=pltpu.HBM)] * 8,
        out_specs=vmem(4),
        scratch_shapes=[
            pltpu.VMEM((1, NOB), F32),
            pltpu.VMEM((1, NOB), jnp.int32),
            pltpu.VMEM((OWNED, LANES), jnp.int32),
            pltpu.SemaphoreType.DMA((8,)),
        ],
        compiler_params=pltpu.CompilerParams(vmem_limit_bytes=PAYLOAD_LIMIT),
    )(
        prior_sample_set.reshape(MEMBERS_HERE * PLANE, LANES),
        eastward_cfl_number.reshape(PLANE, LANES),
        northward_cfl_number.reshape(PLANE, LANES),
        spreading_number.reshape(PLANE, LANES),
        obs_value.reshape(1, NOB),
        obs_site.reshape(1, NOB),
        neighbours.reshape(ROWS * LANES, LANES),
        loc_weight.reshape(ROWS * LANES, LANES),
    )
    other = lax.ppermute(payload, "lat", [(0, 1), (1, 0)])
    first_other = lax.ppermute(first, ("lon", "lat"), chip_corners)
    second_other = lax.ppermute(second, ("lon", "lat"), corners)
    second_in = lax.ppermute(second, "lon", off_lon)
    first_in = lax.ppermute(first, "lon", on_chip)
    own, near, far, weight = call(
        own_kernel,
        [sds((PAYLOAD, LANES))] + [sds((OWNED, LANES))] * 3,
        (payload, extra),
        flops=1 << 20,
    )
    send, values = call(
        forecast_kernel,
        [sds((mems, MEMBERS_HERE, COLS + 2 * NOB)), sds((8, 2 * NOB))],
        (own, other, first_other, second_other, second_in, first_in),
        [pltpu.VMEM((8, 5, 2, 8, LANES), F32), pltpu.VMEM((LEVELS, 8, 8, LANES), F32)],
    )
    members = mems * MEMBERS_HERE
    got = lax.all_to_all(
        send.reshape(members, send.shape[2]), "mem", split_axis=0, concat_axis=0, tiled=True
    )
    spread, spread_near = call(
        spread_kernel,
        [sds((SPREAD_ROWS, 2 * NOB)), sds((members + 1, 2 * NOB))],
        (got, values),
    )
    spread_second = lax.ppermute(spread, ("lon", "lat"), off_chip)
    spread_first = lax.ppermute(spread_near, "lon", on_chip)
    part, dev, centre = call(
        near_kernel,
        [sds((OWNED, SPREAD_ROWS, LANES)), sds((COLS, members)), sds((COLS, members))],
        (got, near, spread, spread_first),
        [pltpu.VMEM((272, 4 * NOB), BF16)],
    )
    updated = call(
        columns_kernel,
        sds((members, COLS)),
        (far, weight, spread_second, part, dev, centre),
        [
            pltpu.VMEM((272, 2 * NOB), BF16),
            pltpu.VMEM((COLS, members), F32),
            pltpu.VMEM((3, members, members), F32),
            pltpu.VMEM((BATCH, SPREAD_ROWS, LANES), F32),
            pltpu.VMEM((BATCH, members, members), F32),
            *[pltpu.VMEM((BATCH, members, 2 * members), BF16)] * 3,
            pltpu.VMEM((BATCH, 8, members), F32),
        ],
        flops=2 * OWNED * 7 * members * 4 * members * members,
    )
    back = lax.all_to_all(updated, "mem", split_axis=0, concat_axis=0, tiled=True)
    result = call(
        unpack_kernel,
        sds((MEMBERS_HERE * PLANE, LANES)),
        (back.reshape(mems, MEMBERS_HERE, COLS),),
    )
    return result.reshape(prior_sample_set.shape)


def solution(mesh):
    return jax.shard_map(
        per_device,
        mesh=mesh,
        in_specs=(
            P("mem", None, "lat", "lon"),
            P(None, "lat", "lon"),
            P(None, "lat", "lon"),
            P(None, "lat", "lon"),
            P("lat", "lon", None),
            P("lat", "lon", None),
            P("lat", "lon", None),
            P("lat", "lon", None),
        ),
        out_specs=P("mem", None, "lat", "lon"),
        check_vma=False,
    )
```

```python
import functools

import jax
import jax.numpy as jnp
from jax import lax
from jax.experimental import pallas as pl
from jax.experimental.pallas import tpu as pltpu
from jax.sharding import PartitionSpec as P

STEPS = 4
LANES = 128
OWNED = 32
GROUPS = LANES // OWNED
ROWS = 4
BATCH = 32
MEMBERS_HERE = 8
LEVELS = 8
NOB = 256
PLANE = LEVELS * ROWS
VALUE_ROW = 11 * PLANE
SITE_ROW = VALUE_ROW + 2
PAYLOAD = SITE_ROW + 6
EDGE_ROWS = 16
COLS = LEVELS * OWNED
SPREAD_ROWS = 136
FAR = -8192
F32 = jnp.float32
BF16 = jnp.bfloat16
VMEM_LIMIT = 40 * 1024 * 1024
PAYLOAD_LIMIT = 60 * 1024 * 1024


def vmem(count):
    return [pl.BlockSpec(memory_space=pltpu.VMEM)] * count


def params():
    return pltpu.CompilerParams(vmem_limit_bytes=VMEM_LIMIT)


def lane_index():
    return lax.broadcasted_iota(jnp.int32, (8, LANES), 1)


def lat_masks():
    here = lax.axis_index("lat")
    return [scalar_mask(here, 0), scalar_mask(here, 1)]


def lon_parity():
    return lax.rem(lax.axis_index("lon"), 2)


def scalar_mask(value, wanted):
    return jnp.full((8, LANES), value, jnp.int32) == wanted


def roll(x, shift):
    shift %= LANES
    return x if shift == 0 else pltpu.roll(x, shift, 1)


def member_rows(own_ref, other_ref, here, level, row):
    start = level * ROWS + row % ROWS
    own = own_ref[pl.ds(start, 8, stride=PLANE), :]
    other = other_ref[pl.ds(start, 8, stride=PLANE), :]
    return jnp.where(here[row // ROWS], own, other)


def coef_rows(own_ref, other_ref, here, which, row):
    start = (MEMBERS_HERE + which) * PLANE + row % ROWS
    own = own_ref[pl.ds(start, 8, stride=ROWS), :]
    other = other_ref[pl.ds(start, 8, stride=ROWS), :]
    return jnp.where(here[row // ROWS], own, other)


def payload_kernel(
    prior_ref,
    east_ref,
    north_ref,
    spread_ref,
    value_ref,
    site_ref,
    ids_ref,
    weight_ref,
    out_ref,
    first_ref,
    second_ref,
    extra_ref,
    value,
    site,
    ids,
    sems,
):
    owned = pl.ds(pl.multiple_of(lax.axis_index("mem") * OWNED, OWNED), OWNED)
    moves = [
        (prior_ref, out_ref.at[pl.ds(0, MEMBERS_HERE * PLANE), :]),
        *[
            (ref, out_ref.at[pl.ds((MEMBERS_HERE + n) * PLANE, PLANE), :])
            for n, ref in enumerate((east_ref, north_ref, spread_ref))
        ],
        (value_ref, value),
        (site_ref, site),
        (ids_ref.at[owned, :], ids),
        (weight_ref.at[owned, :], extra_ref.at[pl.ds(OWNED, OWNED), :]),
    ]
    copies = [pltpu.make_async_copy(src, dst, sems.at[n]) for n, (src, dst) in enumerate(moves)]
    for copy in copies:
        copy.start()
    for copy in copies[:4]:
        copy.wait()
    lane = lane_index()
    even = scalar_mask(lon_parity(), 0)
    for tile in range(2):
        left = jnp.zeros((8, LANES), F32)
        right = jnp.zeros((8, LANES), F32)
        for slot in range(32 if tile == 0 else 12):
            if tile == 0:
                x = out_ref[pl.ds(slot, 8, stride=PLANE), :]
            else:
                x = out_ref[pl.ds((MEMBERS_HERE + slot // 4) * PLANE + slot % 4, 8, stride=ROWS), :]
            place = (lane // 4) == slot
            left = jnp.where(place, roll(x, 4 * slot), left)
            right = jnp.where(place, roll(x, 4 * slot + 4), right)
        first_ref[tile * 8 : tile * 8 + 8, :] = jnp.where(even, right, left)
        second_ref[tile * 8 : tile * 8 + 8, :] = jnp.where(even, left, right)
    for copy in copies[4:]:
        copy.wait()
    extra_ref[0:OWNED, :] = ids[...].astype(F32)
    values = value[...]
    sites = site[...].astype(F32)
    rest = jnp.zeros((PAYLOAD - SITE_ROW - 2, LANES), F32)
    pieces = [values[:, :LANES], values[:, LANES:], sites[:, :LANES], sites[:, LANES:], rest]
    out_ref[VALUE_ROW:, :] = jnp.concatenate(pieces, axis=0)


def advance_in_time(q, coef, level, first_lane, last_lane):
    after = []
    for row in range(8):
        centre, border = q[row]
        rc, rb = roll(centre, 1), roll(border, 1)
        lc, lb = roll(centre, -1), roll(border, -1)
        wests = (jnp.where(first_lane, rb, rc), jnp.where(first_lane, rc, rb))
        easts = (jnp.where(last_lane, lb, lc), jnp.where(last_lane, lc, lb))
        both = []
        for part in range(2):
            c = [coef[row, n, part, level : level + 1, :] for n in range(5)]
            total = c[0] * q[row][part] + c[1] * wests[part] + c[2] * easts[part]
            if row > 0:
                total = total + c[3] * q[row - 1][part]
            if row < 7:
                total = total + c[4] * q[row + 1][part]
            both.append(total)
        after.append(tuple(both))
    return after


def forecast_kernel(
    own_ref,
    other_ref,
    first_other_ref,
    second_other_ref,
    second_ref,
    first_ref,
    send_ref,
    values_ref,
    coef,
    state,
):
    lane = lane_index()
    here = lat_masks()
    even = scalar_mask(lon_parity(), 0)
    first_lane = lane == 0
    last_lane = lane == LANES - 1
    east_lanes = lane < 4
    west_lanes = lane >= LANES - 4
    east, west = {}, {}
    for block in range(2):
        for tile in range(2):
            part = slice(tile * 8, tile * 8 + 8)
            a = jnp.where(here[block], first_ref[part, :], first_other_ref[part, :])
            b = jnp.where(here[block], second_ref[part, :], second_other_ref[part, :])
            east[block, tile] = jnp.where(even, a, b)
            west[block, tile] = jnp.where(even, b, a)

    def halo(row, tile, group):
        slot = group * ROWS + row % ROWS
        key = (row // ROWS, tile)
        from_east = roll(east[key], -4 * slot)
        from_west = roll(west[key], LANES - 4 - 4 * slot)
        return jnp.where(east_lanes, from_east, jnp.where(west_lanes, from_west, 0.0))

    for row in range(8):
        for part in range(2):
            if part == 0:
                u, v, d = (coef_rows(own_ref, other_ref, here, q, row) for q in range(3))
            else:
                u, v, d = (halo(row, 1, q) for q in range(3))
            up, un = jnp.maximum(u, 0.0), jnp.minimum(u, 0.0)
            vp, vn = jnp.maximum(v, 0.0), jnp.minimum(v, 0.0)
            coef[row, 0, part] = 1.0 - (up - un) - (vp - vn) - 4.0 * d
            coef[row, 1, part] = up + d
            coef[row, 2, part] = d - un
            coef[row, 3, part] = vp + d
            coef[row, 4, part] = d - vn

    for level in range(0, LEVELS, 2):
        pair = (level, level + 1)
        q = [
            [(member_rows(own_ref, other_ref, here, n, row), halo(row, 0, n)) for row in range(8)]
            for n in pair
        ]
        for _ in range(STEPS):
            q = [advance_in_time(q[n], coef, pair[n], first_lane, last_lane) for n in range(2)]
        for n in range(2):
            for row in range(8):
                state[pair[n], row] = q[n][row][0]

    for block in range(2):
        site_own = jnp.concatenate(
            [own_ref[SITE_ROW : SITE_ROW + 1, :], own_ref[SITE_ROW + 1 : SITE_ROW + 2, :]], axis=1
        )
        site_other = jnp.concatenate(
            [other_ref[SITE_ROW : SITE_ROW + 1, :], other_ref[SITE_ROW + 1 : SITE_ROW + 2, :]], axis=1
        )
        mine = jnp.full((1, NOB), lax.axis_index("lat"), jnp.int32) == block
        site = jnp.where(mine, site_own, site_other).astype(jnp.int32)
        site_row = jnp.broadcast_to(site >> 7, (8, NOB))
        site_lane = jnp.broadcast_to(site & (LANES - 1), (LANES, NOB))
        pick = jnp.where(lax.broadcasted_iota(jnp.int32, (LANES, NOB), 0) == site_lane, 1.0, 0.0).astype(BF16)
        x = state[:, block * ROWS : (block + 1) * ROWS].reshape(PLANE * 8, LANES)
        x1 = x.astype(BF16)
        rest = x - x1.astype(F32)
        x2 = rest.astype(BF16)
        x3 = (rest - x2.astype(F32)).astype(BF16)
        picked = (
            jnp.dot(x3, pick, preferred_element_type=F32)
            + jnp.dot(x2, pick, preferred_element_type=F32)
            + jnp.dot(x1, pick, preferred_element_type=F32)
        )
        total = jnp.zeros((8, NOB), F32)
        for n in range(PLANE):
            total = jnp.where(site_row == n, picked[n * 8 : n * 8 + 8, :], total)
        for target in range(send_ref.shape[0]):
            send_ref[target, :, COLS + block * NOB : COLS + (block + 1) * NOB] = total

    own = jnp.concatenate([own_ref[VALUE_ROW + n : VALUE_ROW + n + 1, :] for n in range(2)], axis=1)
    other = jnp.concatenate([other_ref[VALUE_ROW + n : VALUE_ROW + n + 1, :] for n in range(2)], axis=1)
    south = jnp.full((1, NOB), lax.axis_index("lat"), jnp.int32) == 0
    values = jnp.concatenate([jnp.where(south, own, other), jnp.where(south, other, own)], axis=1)
    values_ref[...] = jnp.broadcast_to(values, (8, 2 * NOB))

    segment = lane // OWNED
    for row in range(ROWS):
        here_row = lax.axis_index("lat") * ROWS + row
        values = [state[level, here_row] for level in range(LEVELS)]
        for group in range(GROUPS):
            for half in range(2):
                total = jnp.zeros((8, LANES), F32)
                for n in range(4):
                    moved = roll(values[half * 4 + n], OWNED * (n - group))
                    total = jnp.where(segment == n, moved, total)
                send_ref[row * GROUPS + group, :, half * LANES : (half + 1) * LANES] = total


def halves(x):
    hi = x.astype(BF16)
    return hi, (x - hi.astype(F32)).astype(BF16)


def left_side(x):
    return jnp.concatenate(halves(x), axis=1)


def product(left, right):
    out = jnp.dot(left, right, preferred_element_type=F32)
    half = out.shape[1] // 2
    return out[:, :half] + out[:, half:]


def small_product(rows, halves_of_right):
    out = jnp.dot(jnp.concatenate(halves(rows), axis=0), halves_of_right, preferred_element_type=F32)
    half = out.shape[1] // 2
    return out[0:16, :half] + (out[0:16, half:] + out[16:32, :half])


def spread_kernel(recv_ref, values_ref, out_ref, near_ref):
    members = recv_ref.shape[0]
    obs = recv_ref[:, COLS:]
    mean = jnp.sum(obs, axis=0, keepdims=True) / members
    pert = obs - mean
    innovation = values_ref[0:1, :] - mean
    out_ref[0:members, :] = pert
    near_ref[0:members, :] = pert
    near_ref[members:, :] = innovation
    row = lax.broadcasted_iota(jnp.int32, (8, 2 * NOB), 0)
    out_ref[members:, :] = jnp.where(row == 0, innovation, 0.0)


def fill_table(table, start, spread_ref):
    width = pl.ds(start, 2 * NOB)
    hi, lo = halves(spread_ref[0:128, :])
    table[0:128, width] = hi
    table[128:256, width] = lo
    innovation = spread_ref[128:129, :]
    first_term = innovation.astype(BF16).astype(F32)
    row = lax.broadcasted_iota(jnp.int32, (16, 2 * NOB), 0)
    extra = jnp.where(row == 0, first_term, jnp.where(row == 1, innovation - first_term, 0.0))
    table[256:272, width] = extra.astype(BF16)


def local_places(ids):
    code = ids >> 8
    lat_step = jnp.where(code >= 6, 2, jnp.where(code >= 3, 1, 0))
    lon_step = code - 3 * lat_step
    odd = jnp.full(ids.shape, lon_parity(), jnp.int32) == 1
    slot = jnp.where(odd, 2 - lon_step, lon_step)
    within = (lat_step - 1 + lax.axis_index("lat")) * NOB + (ids & (NOB - 1))
    near = jnp.where(slot == 0, FAR, within + jnp.where(slot == 2, 2 * NOB, 0))
    far = jnp.where(slot == 0, within, FAR)
    return near.astype(F32), far.astype(F32)


def own_kernel(payload_ref, extra_ref, own_ref, near_ref, far_ref, weight_out):
    own_ref[...] = payload_ref[...]
    weight_out[...] = extra_ref[OWNED:, :]
    near_ref[...], far_ref[...] = local_places(extra_ref[0:OWNED, :].astype(jnp.int32))


def gather_pair(table, places, first_column, blocks):
    place = lax.broadcasted_iota(jnp.int32, (NOB, LANES), 0).astype(F32).astype(BF16)
    one, zero = jnp.ones((), BF16), jnp.zeros((), BF16)
    hot = []
    for block in range(blocks):
        sides = []
        for k in range(2):
            row = places[pl.ds(first_column + k, 1), :] - float(block * NOB)
            sides.append(jnp.where(row.astype(BF16) == place, one, zero))
        hot.append(jnp.concatenate(sides, axis=1))
    both = jnp.dot(table[...], jnp.concatenate(hot, axis=0), preferred_element_type=F32)
    rows = both[0:128] + both[128:256]
    innov = both[256:257] + both[257:258]
    found = jnp.concatenate([rows, jnp.broadcast_to(innov, (8, 2 * LANES))], axis=0)
    return found[:, :LANES], found[:, LANES:]


def near_kernel(
    recv_ref, places, mine_ref, first_ref, part_ref, dev_ref, centre_ref, table
):
    members = recv_ref.shape[0]
    fill_table(table, 0, mine_ref)
    fill_table(table, 2 * NOB, first_ref)
    traces = jnp.transpose(recv_ref[:, :COLS])
    centre = jnp.sum(traces, axis=1, keepdims=True) / members
    dev_ref[...] = traces - centre
    centre_ref[...] = jnp.broadcast_to(centre, traces.shape)

    def turn(n, carry):
        for pair in range(BATCH // 2):
            c = n * BATCH + pair * 2
            left, right = gather_pair(table, places, c, 4)
            part_ref[c] = left
            part_ref[c + 1] = right
        return carry

    lax.fori_loop(0, OWNED // BATCH, turn, 0)


def columns_kernel(
    places,
    weight_ref,
    second_ref,
    part_ref,
    dev_ref,
    centre_ref,
    out_ref,
    table,
    res,
    eyes,
    found,
    full,
    half_s,
    half_u,
    half_z,
    drives,
):
    members = 128
    scale = members - 1.0
    fill_table(table, 0, second_ref)
    i0 = lax.broadcasted_iota(jnp.int32, (members, members), 0)
    i1 = lax.broadcasted_iota(jnp.int32, (members, members), 1)
    for n, value in enumerate((scale, 0.84375, 1.5380859375)):
        eyes[n] = jnp.where(i0 == i1, value, 0.0).astype(F32)

    def put(ref, b, x):
        hi, lo = halves(x)
        ref[b, :, 0:members] = hi
        ref[b, :, members:] = lo

    def right_of(ref, b):
        top = ref[b]
        low = jnp.concatenate([ref[b, :, 0:members], jnp.zeros((members, members), BF16)], axis=1)
        return jnp.concatenate([top, low], axis=0)

    def turn(n, carry):
        base = n * BATCH
        slots = range(BATCH)
        invs = []
        for pair in range(BATCH // 2):
            for k, extra in enumerate(gather_pair(table, places, base + pair * 2, 2)):
                found[pair * 2 + k] = extra + part_ref[base + pair * 2 + k]
        for b in slots:
            pert = found[b, 0:members]
            innov = found[b, members : members + 1]
            w = weight_ref[pl.ds(base + b, 1), :]
            left = jnp.concatenate([pert * w, jnp.broadcast_to(w * innov, (16, LANES))], axis=0)
            e_hi, e_lo = halves(jnp.transpose(pert))
            right = jnp.concatenate(
                [
                    jnp.concatenate([e_hi, e_lo], axis=1),
                    jnp.concatenate([e_hi, jnp.zeros_like(e_hi)], axis=1),
                ],
                axis=0,
            )
            both = product(left_side(left), right)
            gram = both[:members]
            drives[b] = both[members : members + 8]
            norm = jnp.sum(jnp.sum(gram * gram, axis=0, keepdims=True), axis=1, keepdims=True)
            inv = 1.0 / (scale + jnp.sqrt(norm))
            invs.append(inv)
            s = (eyes[0] + gram) * inv
            full[b] = s
            put(half_s, b, s)
        for b in slots:
            square = product(half_s[b], right_of(half_s, b))
            put(half_u, b, 0.25 * square - 1.125 * full[b] + eyes[1])
        for b in slots:
            square = product(half_u[b], right_of(half_u, b))
            put(half_z, b, square - 0.5390625 * full[b] + eyes[2])
        rows = []
        for b in slots:
            x = jnp.concatenate([dev_ref[pl.ds(base + b, 8, stride=OWNED), :], drives[b]], axis=0)
            both = product(jnp.concatenate([half_s[b], left_side(x)], axis=0), right_of(half_z, b))
            put(half_u, b, both[0:members])
            rows.append(both[members:])
        for b in slots:
            put(half_s, b, product(half_u[b], right_of(half_z, b)))
        moved = [0.0625 * x for x in rows]
        for coefficient in (-0.5625, 1.6875, -2.4375, 2.25):
            moved = [coefficient * rows[b] + small_product(moved[b], half_s[b]) for b in slots]
        for b in slots:
            y = moved[b][0:8]
            shift = jnp.sum(y * moved[b][8:16], axis=1, keepdims=True) * invs[b]
            res[pl.ds(base + b, 8, stride=OWNED), :] = jnp.sqrt(scale * invs[b]) * y + shift
        return carry

    lax.fori_loop(0, OWNED // BATCH, turn, 0)
    out_ref[...] = jnp.transpose(res[...] + centre_ref[...])


def unpack_kernel(recv_ref, out_ref):
    segment = lane_index() // OWNED
    for row in range(ROWS):
        for half in range(2):
            parts = [
                recv_ref[row * GROUPS + g, :, half * LANES : (half + 1) * LANES] for g in range(GROUPS)
            ]
            for n in range(4):
                level = half * 4 + n
                total = jnp.zeros((8, LANES), F32)
                for g in range(GROUPS):
                    total = jnp.where(segment == g, roll(parts[g], OWNED * (g - n)), total)
                out_ref[pl.ds(level * ROWS + row, 8, stride=PLANE), :] = total


def call(kernel, shapes, operands, scratch=(), flops=None):
    single = not isinstance(shapes, list)
    cost = None
    if flops is not None:
        cost = pl.CostEstimate(flops=flops, bytes_accessed=1 << 22, transcendentals=0)
    return pl.pallas_call(
        kernel,
        out_shape=shapes,
        in_specs=vmem(len(operands)),
        out_specs=vmem(1)[0] if single else vmem(len(shapes)),
        scratch_shapes=list(scratch),
        compiler_params=params(),
        cost_estimate=cost,
    )(*operands)


def per_device(
    prior_sample_set,
    eastward_cfl_number,
    northward_cfl_number,
    spreading_number,
    obs_value,
    obs_site,
    neighbours,
    loc_weight,
):
    sds = functools.partial(jax.ShapeDtypeStruct, dtype=F32)
    mems = lax.axis_size("mem")
    lons = lax.axis_size("lon")
    on_chip = [(i, i ^ 1) for i in range(lons)]
    whole = 2 * lons
    off_chip, corners, chip_corners = [], [], []
    for i in range(whole):
        j = (i + 1 if i % 2 else i - 1) % whole
        off_chip.append((i % lons * 2 + i // lons, j % lons * 2 + j // lons))
        corners.append((i % lons * 2 + i // lons, j % lons * 2 + 1 - i // lons))
        chip_corners.append((i % lons * 2 + i // lons, (i % lons ^ 1) * 2 + 1 - i // lons))
    off_lon = [(i, (i + 1 if i % 2 else i - 1) % lons) for i in range(lons)]

    edge = sds((EDGE_ROWS, LANES))
    payload, first, second, extra = pl.pallas_call(
        payload_kernel,
        out_shape=[
            sds((PAYLOAD, LANES)),
            edge,
            edge,
            sds((2 * OWNED, LANES)),
        ],
        in_specs=[pl.BlockSpec(memory_space=pltpu.HBM)] * 8,
        out_specs=vmem(4),
        scratch_shapes=[
            pltpu.VMEM((1, NOB), F32),
            pltpu.VMEM((1, NOB), jnp.int32),
            pltpu.VMEM((OWNED, LANES), jnp.int32),
            pltpu.SemaphoreType.DMA((8,)),
        ],
        compiler_params=pltpu.CompilerParams(vmem_limit_bytes=PAYLOAD_LIMIT),
    )(
        prior_sample_set.reshape(MEMBERS_HERE * PLANE, LANES),
        eastward_cfl_number.reshape(PLANE, LANES),
        northward_cfl_number.reshape(PLANE, LANES),
        spreading_number.reshape(PLANE, LANES),
        obs_value.reshape(1, NOB),
        obs_site.reshape(1, NOB),
        neighbours.reshape(ROWS * LANES, LANES),
        loc_weight.reshape(ROWS * LANES, LANES),
    )
    other = lax.ppermute(payload, "lat", [(0, 1), (1, 0)])
    first_other = lax.ppermute(first, ("lon", "lat"), chip_corners)
    second_other = lax.ppermute(second, ("lon", "lat"), corners)
    second_in = lax.ppermute(second, "lon", off_lon)
    first_in = lax.ppermute(first, "lon", on_chip)
    own, near, far, weight = call(
        own_kernel,
        [sds((PAYLOAD, LANES))] + [sds((OWNED, LANES))] * 3,
        (payload, extra),
        flops=1 << 20,
    )
    send, values = call(
        forecast_kernel,
        [sds((mems, MEMBERS_HERE, COLS + 2 * NOB)), sds((8, 2 * NOB))],
        (own, other, first_other, second_other, second_in, first_in),
        [pltpu.VMEM((8, 5, 2, 8, LANES), F32), pltpu.VMEM((LEVELS, 8, 8, LANES), F32)],
    )
    members = mems * MEMBERS_HERE
    got = lax.all_to_all(
        send.reshape(members, send.shape[2]), "mem", split_axis=0, concat_axis=0, tiled=True
    )
    spread, spread_near = call(
        spread_kernel,
        [sds((SPREAD_ROWS, 2 * NOB)), sds((members + 1, 2 * NOB))],
        (got, values),
    )
    spread_second = lax.ppermute(spread, ("lon", "lat"), off_chip)
    spread_first = lax.ppermute(spread_near, "lon", on_chip)
    part, dev, centre = call(
        near_kernel,
        [sds((OWNED, SPREAD_ROWS, LANES)), sds((COLS, members)), sds((COLS, members))],
        (got, near, spread, spread_first),
        [pltpu.VMEM((272, 4 * NOB), BF16)],
    )
    updated = call(
        columns_kernel,
        sds((members, COLS)),
        (far, weight, spread_second, part, dev, centre),
        [
            pltpu.VMEM((272, 2 * NOB), BF16),
            pltpu.VMEM((COLS, members), F32),
            pltpu.VMEM((3, members, members), F32),
            pltpu.VMEM((BATCH, SPREAD_ROWS, LANES), F32),
            pltpu.VMEM((BATCH, members, members), F32),
            *[pltpu.VMEM((BATCH, members, 2 * members), BF16)] * 3,
            pltpu.VMEM((BATCH, 8, members), F32),
        ],
        flops=2 * OWNED * 7 * members * 4 * members * members,
    )
    back = lax.all_to_all(updated, "mem", split_axis=0, concat_axis=0, tiled=True)
    result = call(
        unpack_kernel,
        sds((MEMBERS_HERE * PLANE, LANES)),
        (back.reshape(mems, MEMBERS_HERE, COLS),),
    )
    return result.reshape(prior_sample_set.shape)


def solution(mesh):
    return jax.shard_map(
        per_device,
        mesh=mesh,
        in_specs=(
            P("mem", None, "lat", "lon"),
            P(None, "lat", "lon"),
            P(None, "lat", "lon"),
            P(None, "lat", "lon"),
            P("lat", "lon", None),
            P("lat", "lon", None),
            P("lat", "lon", None),
            P("lat", "lon", None),
        ),
        out_specs=P("mem", None, "lat", "lon"),
        check_vma=False,
    )
```
